256 devices in a mesh: diag: 256 (over x, y, z, core).
Axes of the slice: x: 4, y: 4, z: 8, core: 2. Of those that a mesh axis runs over, the one named last changes fastest.
Arguments:
- features: bfloat16 [8192, 256], P('diag'), may hold values from -6 to 6
- row_proj: bfloat16 [256, 32], replicated, may hold values from -0.375 to 0.375
- col_proj: bfloat16 [256, 32], replicated, may hold values from -0.375 to 0.375
- first_filter: bfloat16 [3, 3, 32, 32], replicated, may hold values from -0.375 to 0.375
- second_filter: bfloat16 [3, 3, 32, 32], replicated, may hold values from -0.375 to 0.375
- readout: bfloat16 [32], replicated, may hold values from -1 to 1
- target: float32 [8192, 256], P('diag'), may hold values from -6 to 6
Outputs:
- grad_features: float32 [8192, 256], P('diag')
- grad_row_proj: float32 [256, 32], replicated
- grad_col_proj: float32 [256, 32], replicated
- grad_conv_one: float32 [3, 3, 32, 32], replicated
- grad_conv_two: float32 [3, 3, 32, 32], replicated
- grad_readout: float32 [32], replicated
The draws below stay inside these ranges and needn't reach their ends.
All inputs are finite; a program needn't handle non-finite values.
Results may differ from the reference program's by a relative error of at most 0.0006.
Values may be sent and summed in bfloat16 or wider, within the bound.
A program may use at most 128 MiB of HBM per device.

```python
import jax
import jax.numpy as jnp
from jax import lax

FEAT = 256
PAIR = 32
BAND = 256
FIRST_SPACING = 2
SECOND_SPACING = 4
BINS = 8192


def level_of(own_key, dims, shards, low, largest):
    factor_of, own = 1.0, jax.random.fold_in(own_key, 6)
    for position, blocks in shards:
        steps = jnp.exp(jax.random.uniform(jax.random.fold_in(own, position), (blocks,), jnp.float32, low / len(shards), largest / len(shards)))
        factor_of = factor_of * jnp.repeat(steps, dims[position] // blocks).reshape([-1 if axis == position else 1 for axis in range(len(dims))])
    return factor_of


def normal_values(key, shape, scale, limit, shards=(), kind=jnp.bfloat16):
    entries = jax.random.normal(key, shape, jnp.float32) * scale
    if len(shards) > 0:
        entries = level_of(key, shape, shards, -0.22, 0.18) * entries
    return jnp.clip(entries, min=-limit, max=limit).astype(kind)


def setup_inputs(seed: int = 0) -> dict:
    seeds = jax.random.split(jax.random.key(seed), 8)
    features = normal_values(seeds[0], (BINS, FEAT), 1.0, 6.0, ((0, 256),))
    row_proj = normal_values(seeds[1], (FEAT, PAIR), FEAT ** -0.5, 0.375)
    col_proj = normal_values(seeds[2], (FEAT, PAIR), FEAT ** -0.5, 0.375)
    first_filter = normal_values(seeds[3], (3, 3, PAIR, PAIR), (9 * PAIR) ** -0.5, 0.375)
    second_filter = normal_values(seeds[4], (3, 3, PAIR, PAIR), (9 * PAIR) ** -0.5, 0.375)
    readout = normal_values(seeds[5], (PAIR,), PAIR ** -0.5, 1.0)
    target = normal_values(seeds[6], (BINS, BAND), 1.0, 6.0, ((0, 256),), jnp.float32)
    return {"features": features, "row_proj": row_proj, "col_proj": col_proj, "first_filter": first_filter, "second_filter": second_filter, "readout": readout, "target": target}


highest = lax.Precision.HIGHEST

def activate(values):
    return jax.nn.gelu(values, approximate=True)

def stored(values):
    rounded = lax.optimization_barrier(values.astype(jnp.bfloat16)).astype(values.dtype)
    return values + lax.stop_gradient(rounded - values)

def spaced_filter(field_in, kernel, spread):
    count_of_rows = field_in.shape[1]
    band_width = field_in.shape[2]
    padded = jnp.pad(field_in, ((0, 0), (spread, spread), (2 * spread, 2 * spread)))
    running = None
    for tap_row in (-1, 0, 1):
        for tap_col in (-1, 0, 1):
            row_start = spread * (tap_row + 1)
            col_start = 2 * spread + spread * (tap_col - tap_row)
            portion = padded[:, row_start:row_start + count_of_rows, col_start:col_start + band_width]
            product = jnp.einsum('co,cik->oik', kernel[tap_row + 1, tap_col + 1], portion, precision=highest)
            running = product if running is None else running + product
    return running

def block_loss(parameters, window_in, target_block, start_row):
    row_weight, col_weight, first_taps, second_taps, read_weight = parameters
    border_width = FIRST_SPACING + SECOND_SPACING
    ext_rows = window_in.shape[0] - BAND
    own_count = ext_rows - 2 * border_width
    row_feat = jnp.dot(window_in[:ext_rows], row_weight, precision=highest)
    col_feat = jnp.dot(window_in, col_weight, precision=highest)
    offsets = jnp.arange(BAND, dtype=jnp.int32)
    positions = start_row - border_width + jnp.arange(ext_rows, dtype=jnp.int32)
    interior_mask = ((positions[:, None] >= 0) & (positions[:, None] + offsets[None, :] < BINS)).astype(row_feat.dtype)
    paired = col_feat[jnp.arange(ext_rows, dtype=jnp.int32)[:, None] + offsets[None, :]]
    input_plane = interior_mask[None] * (row_feat.T[:, :, None] + jnp.transpose(paired, (2, 0, 1)))
    input_activation = stored(activate(input_plane))
    hidden_plane = input_plane + interior_mask[None] * spaced_filter(input_activation, first_taps, FIRST_SPACING)
    hidden_activation = stored(activate(hidden_plane))
    output_plane = hidden_plane + interior_mask[None] * spaced_filter(hidden_activation, second_taps, SECOND_SPACING)
    own_rows = output_plane[:, border_width:border_width + own_count]
    predicted = jnp.einsum('c,cik->ik', read_weight, own_rows, precision=highest)
    kept_mask = interior_mask[border_width:border_width + own_count]
    return 0.5 / BAND * jnp.sum(kept_mask * (predicted - target_block) ** 2)

def reference(features, row_proj, col_proj, first_filter, second_filter, readout, target):
    border_width = FIRST_SPACING + SECOND_SPACING
    block_rows = min(512, BINS)
    blocks_total = BINS // block_rows
    parameters = tuple((weight.astype(jnp.float32) for weight in (row_proj, col_proj, first_filter, second_filter, readout)))
    padded = jnp.pad(features.astype(jnp.float32), ((border_width, border_width + BAND), (0, 0)))

    def one_block(state_now, block_index):
        grad_feat, param_grads = state_now
        start_row = (block_index * block_rows).astype(jnp.int32)
        window_in = lax.dynamic_slice_in_dim(padded, start_row, block_rows + 2 * border_width + BAND, 0)
        target_block = lax.dynamic_slice_in_dim(target, start_row, block_rows, 0)
        loss_value, pullback = jax.vjp(lambda given, rows_in: block_loss(given, rows_in, target_block, start_row), parameters, window_in)
        grad_params, grad_window = pullback(jnp.ones_like(loss_value))
        current = lax.dynamic_slice_in_dim(grad_feat, start_row, block_rows + 2 * border_width + BAND, 0)
        grad_feat = lax.dynamic_update_slice_in_dim(grad_feat, current + grad_window, start_row, 0)
        param_grads = jax.tree.map(jnp.add, param_grads, grad_params)
        return ((grad_feat, param_grads), None)
    initial = (jnp.zeros(padded.shape, jnp.float32), tuple((jnp.zeros_like(weight) for weight in parameters)))
    (grad_feat, param_grads), _ = lax.scan(one_block, initial, jnp.arange(blocks_total, dtype=jnp.int32))
    grad_features = grad_feat[border_width:border_width + BINS]
    return (grad_features, param_grads[0], param_grads[1], param_grads[2], param_grads[3], param_grads[4])
```

```python
import functools
import math

import jax
import jax.numpy as jnp
from jax import lax
from jax.experimental import pallas as pl
from jax.experimental.pallas import tpu as pltpu
from jax.sharding import PartitionSpec as P

MESH = pl.DeviceIdType.MESH
F32, BF16 = jnp.float32, jnp.bfloat16

ROWS = 32
BAND = 256
PAIR = 32
HALO = 12
GROUPS = (ROWS + 2 * HALO) // 4
FIRST_OWN, LAST_OWN = 3, 10
PAD = 16
LENGTH = 352
WIDE, SPAN, CHUNK = 272, 264, 88
AHEAD = 9
REACH = 8
C0 = math.sqrt(2.0 / math.pi)
C1 = C0 * 0.044715
SIDE = 16
PART = 16
SEM = pltpu.SemaphoreType.DMA


def iota(shape, dim):
    return lax.broadcasted_iota(jnp.int32, shape, dim)


def lane_block(rows):
    return lax.shift_right_logical(iota((rows, 128), 1), 5)


def gelu_and_slope(x):
    square = x * x
    t = jnp.tanh(x * (C0 + C1 * square))
    h = 0.5 * x
    act = h + h * t
    slope = (0.5 + 0.5 * t) + h * (1.0 - t * t) * (C0 + 3.0 * C1 * square)
    return act.astype(BF16).astype(F32), slope


def split(x):
    high = x.astype(BF16)
    return high, (x - high.astype(F32)).astype(BF16)


def fold(x):
    total = x[0:8]
    for i in range(1, x.shape[0] // 8):
        total = total + x[8 * i : 8 * i + 8]
    return total


def dot(a, b):
    return jnp.dot(a, b, preferred_element_type=F32)


def dot_t(a, b):
    return lax.dot_general(a, b, (((0,), (0,)), ((), ())), preferred_element_type=F32)


def dot_nt(a, b):
    return lax.dot_general(a, b, (((1,), (1,)), ((), ())), preferred_element_type=F32)


def repeater(lanes):
    return (jnp.bitwise_and(iota((PAIR, lanes), 1), 31) == iota((PAIR, lanes), 0)).astype(F32).astype(BF16)


def spread(block):
    turned = [block] + [pltpu.roll(block, 32 * s, 1) for s in (1, 2, 3)]
    where_block = lane_block(8)
    outs = []
    for b in range(4):
        value = turned[(3 - b) % 4]
        for other in range(3):
            value = jnp.where(where_block == other, turned[(other - b) % 4], value)
        outs.append(value)
    return outs


def gather_kernel(n, feat, row_proj, col_proj, target, colw, roww, targ, proj, sbuf, rbuf, tlow, thigh, s1, r1, s2, r2):
    me = lax.axis_index("diag")

    def dev(step):
        return lax.rem(me + step + n, n)

    barrier = pltpu.get_barrier_semaphore()
    for step in (-1,) + tuple(range(1, AHEAD + 1)):
        pl.semaphore_signal(barrier, inc=1, device_id=(dev(step),), device_id_type=MESH)
    rep = repeater(128)
    proj[0] = dot(feat[...], dot(row_proj[...], rep).astype(BF16))
    cc = dot(feat[...], dot(col_proj[...], rep).astype(BF16))
    where_block = lane_block(8)
    row_c = jnp.zeros((8, 128), F32)
    col_c = jnp.zeros((8, 128), F32)
    for b in range(4):
        row_c = jnp.where(where_block == b, proj[0, pl.ds(b, 8, stride=4), :], row_c)
        col_c = jnp.where(where_block == b, cc[8 * b : 8 * b + 8], col_c)
    sbuf[0:8] = col_c
    sbuf[8:16] = row_c
    pl.semaphore_wait(barrier, AHEAD + 1)
    copies = []
    for slot, step in ((0, 1), (2, -1)):
        copies.append(
            pltpu.make_async_remote_copy(sbuf, rbuf.at[slot], s1.at[slot], r1.at[slot], device_id=(dev(step),), device_id_type=MESH)
        )
    for m in range(3, AHEAD + 2):
        copies.append(
            pltpu.make_async_remote_copy(
                sbuf.at[pl.ds(0, 8)], rbuf.at[m, pl.ds(0, 8)], s1.at[m], r1.at[m], device_id=(dev(1 - m),), device_id_type=MESH
            )
        )
    copies.append(
        pltpu.make_async_remote_copy(target.at[pl.ds(24, 8)], tlow, s2.at[0], r2.at[0], device_id=(dev(1),), device_id_type=MESH)
    )
    copies.append(
        pltpu.make_async_remote_copy(target.at[pl.ds(0, 8)], thigh, s2.at[1], r2.at[1], device_id=(dev(-1),), device_id_type=MESH)
    )
    for copy in copies:
        copy.start()
    colw[8:16] = col_c
    roww[8:16] = row_c
    targ[8:40] = target[...]
    for copy in copies:
        copy.wait()
    for m in range(AHEAD + 2):
        if m != 1:
            colw[8 * m : 8 * m + 8] = rbuf[m, 0:8]
    roww[0:8] = rbuf[0, 8:16]
    roww[16:24] = rbuf[2, 8:16]
    targ[0:8] = tlow[...]
    targ[40:48] = thigh[...]


def band_kernel(
    total, colw, roww, targ, k1, k2, ro, out, colp, rowg,
    w1, wa, w2, rol, colr, mk, ts, act0, f0, d0, act1, f1, d1, mis, g1, lhs, lhs2, res, qbuf, xbuf, gbuf, fg, tacc, colacc, tiles,
):
    me = lax.axis_index("diag")
    start = me * ROWS

    rep8 = repeater(256)
    tiles[...] = dot(k1[...], rep8)
    where_out = lax.shift_right_logical(iota((PAIR, 256), 1), 5)
    for q in range(3):
        for ri in range(-4, 12):
            value = jnp.zeros((PAIR, 256), F32)
            for p in range(3):
                tap = 3 * p + q
                value = jnp.where(where_out == ri - 2 * (p - 1), tiles[32 * tap : 32 * tap + 32], value)
            row = (q * 16 + ri + 4) * 32
            w1[row : row + 32] = value.astype(BF16)
    for tap in range(9):
        tiles[32 * tap : 32 * tap + 32] = dot_t(k1[32 * tap : 32 * tap + 32], rep8)
    for q in range(3):
        for ri in range(-4, 12):
            value = jnp.zeros((PAIR, 256), F32)
            for p in range(3):
                tap = 3 * p + q
                value = jnp.where(where_out == ri + 2 * (p - 1), tiles[32 * tap : 32 * tap + 32], value)
            row = (q * 16 + ri + 4) * 32
            wa[row : row + 32] = value.astype(BF16)
    ro8 = jnp.broadcast_to(ro[...].astype(F32), (8, PAIR)).astype(BF16)
    rol[...] = dot(ro8, repeater(128))
    for tap in range(9):
        taps = k2[32 * tap : 32 * tap + 32]
        w2[8 * tap : 8 * tap + 8] = dot_nt(ro8, jnp.concatenate([taps] * 4, axis=0))

    for m in range(AHEAD + 2):
        for b, value in enumerate(spread(colw[8 * m : 8 * m + 8])):
            row = 32 * (m - 1) + 8 * b + HALO + PAD
            if row >= 0 and row + 8 <= LENGTH:
                colr[row : row + 8] = value
    column = iota((LENGTH, 128), 0) - PAD
    mk[...] = jnp.where(column + (start - HALO) < total, column - lane_block(LENGTH), 1 << 20)
    wide = jnp.concatenate([targ[...], jnp.zeros((48, 128), F32)], axis=1)
    wide = jnp.concatenate([wide, jnp.zeros((80, 384), F32)], axis=0)
    sheared = pltpu.roll(wide, 0, 1, stride=1, stride_axis=0)
    ts[...] = jnp.zeros((LENGTH, 128), F32)
    ts[4 + PAD : 4 + PAD + 312] = sheared.T[0:312]

    act0[0] = jnp.zeros((LENGTH, 128), F32)
    act0[GROUPS + 1] = jnp.zeros((LENGTH, 128), F32)
    colacc[...] = jnp.zeros((LENGTH, 128), F32)
    tacc[...] = jnp.zeros((80, 128), F32)
    fg[...] = jnp.zeros((256, 1152), F32)

    def first_column(u):
        return pl.multiple_of(8 * lax.shift_right_logical(u, 1), 8)

    def mask_at(u, row, count):
        k = mk[pl.ds(row, count), :] - 4 * u
        limit = jnp.where(start + 4 * u - HALO >= 0, BAND, 0)
        return jnp.logical_and(k >= 0, k < limit)

    def clear_sides(buffer, index, base):
        buffer[index, pl.ds(base, 16), :] = jnp.zeros((16, 128), F32)
        buffer[index, pl.ds(base + PAD + SPAN, 24), :] = jnp.zeros((24, 128), F32)

    def make_field(u, carry):
        base = first_column(u)
        clear_sides(act0, u + 1, base)
        row_here = roww[pl.ds(u + 5, 1), :]
        for ch in range(3):
            row = base + PAD + CHUNK * ch
            x = jnp.where(mask_at(u, row, CHUNK), row_here + colr[pl.ds(row, CHUNK), :], 0.0)
            f0[u, pl.ds(row, CHUNK), :] = x
            act, slope = gelu_and_slope(x)
            act0[u + 1, pl.ds(row, CHUNK), :] = act
            d0[u, pl.ds(row, CHUNK), :] = slope
        return carry

    lax.fori_loop(0, GROUPS, make_field, 0)

    def first_conv(v, carry):
        base = pl.multiple_of(8 * v, 8)
        for q in range(3):
            for d in range(4):
                piece = act0[2 * v + d, pl.ds(base + PAD + 2 * (q - 1), WIDE), :]
                lhs[:, 128 * (4 * q + d) : 128 * (4 * q + d + 1)] = piece.astype(BF16)
        res[0:WIDE] = dot(lhs[...], w1[...])
        for h in range(2):
            u = 2 * v + h
            clear_sides(act1, u, base)
            for ch in range(3):
                row = base + PAD + CHUNK * ch
                conv = res[CHUNK * ch : CHUNK * ch + CHUNK, 128 * h : 128 * h + 128]
                x = jnp.where(mask_at(u, row, CHUNK), f0[u, pl.ds(row, CHUNK), :] + conv, 0.0)
                f1[u, pl.ds(row, CHUNK), :] = x
                act, slope = gelu_and_slope(x)
                act1[u, pl.ds(row, CHUNK), :] = act
                d1[u, pl.ds(row, CHUNK), :] = slope
        return carry

    lax.fori_loop(0, GROUPS // 2, first_conv, 0)

    bins = lax.shift_right_logical(iota((128, 128), 0), 5)
    ones = (bins == lane_block(128)).astype(F32).astype(BF16)

    def make_misfit(u, carry):
        base = first_column(u)
        clear_sides(mis, u, base)
        for ch in range(3):
            row = base + PAD + CHUNK * ch
            value = rol[0:1] * f1[u, pl.ds(row, CHUNK), :]
            for p in range(3):
                for q in range(3):
                    tap = 3 * p + q
                    value = value + w2[8 * tap : 8 * tap + 1] * act1[u + p - 1, pl.ds(row + 4 * (q - 1), CHUNK), :]
            res[CHUNK * ch : CHUNK * ch + CHUNK, 0:128] = value
        high, low = split(res[0:WIDE, 0:128])
        qbuf[:, 0:128] = high
        qbuf[:, 128:256] = low
        high, low = split(ts[pl.ds(base + PAD, WIDE), :])
        qbuf[:, 256:384] = high
        qbuf[:, 384:512] = low
        pick = jnp.where(iota((128, 128), 0) == 4 * u - 4 + lane_block(128), -1.0, 0.0).astype(BF16)
        res[0:WIDE, 128:256] = dot(qbuf[...], jnp.concatenate([ones, ones, pick, pick], axis=0))
        for ch in range(3):
            row = base + PAD + CHUNK * ch
            value = res[CHUNK * ch : CHUNK * ch + CHUNK, 128:256] * (1.0 / BAND)
            mis[u, pl.ds(row, CHUNK), :] = jnp.where(mask_at(u, row, CHUNK), value, 0.0)
        return carry

    lax.fori_loop(1, GROUPS - 1, make_misfit, 0)

    def make_cotangent(u, carry):
        base = first_column(u)
        clear_sides(g1, u, base)
        sums = [None] * 10
        for ch in range(3):
            row = base + PAD + CHUNK * ch
            act = act1[u, pl.ds(row, CHUNK), :]
            back = None
            for p in range(3):
                for q in range(3):
                    tap = 3 * p + q
                    m = mis[u - (p - 1), pl.ds(row - 4 * (q - 1), CHUNK), :]
                    term = w2[8 * tap : 8 * tap + 1] * m
                    back = term if back is None else back + term
                    part = fold(act * m)
                    sums[tap] = part if sums[tap] is None else sums[tap] + part
            m = mis[u, pl.ds(row, CHUNK), :]
            part = fold(m * f1[u, pl.ds(row, CHUNK), :])
            sums[9] = part if sums[9] is None else sums[9] + part
            value = rol[0:1] * m + d1[u, pl.ds(row, CHUNK), :] * back
            g1[u, pl.ds(row, CHUNK), :] = jnp.where(mask_at(u, row, CHUNK), value, 0.0)
        for tap in range(10):
            source = u - (tap // 3 - 1) if tap < 9 else u
            own = jnp.logical_and(source >= FIRST_OWN, source <= LAST_OWN)
            tacc[8 * tap : 8 * tap + 8] += jnp.where(own, sums[tap], 0.0)
        return carry

    lax.fori_loop(2, GROUPS - 2, make_cotangent, 0)

    def first_adjoint(w, carry):
        base = pl.multiple_of(8 * w + 8, 8)
        for q in range(3):
            for d in range(4):
                piece = g1[2 * w + 2 + d, pl.ds(base + PAD - 2 * (q - 1), WIDE), :]
                high, low = split(piece)
                lanes = slice(128 * (4 * q + d), 128 * (4 * q + d + 1))
                lhs2[0:WIDE, lanes] = high
                lhs2[WIDE : 2 * WIDE, lanes] = low
        res[...] = dot(lhs2[...], wa[...])
        for h in range(2):
            u = 2 * w + 3 + h
            total_row = None
            for at, count in ((0, 88), (88, 88), (176, 96)):
                row = base + PAD + at
                lanes = slice(128 * h, 128 * h + 128)
                back = res[at : at + count, lanes] + res[WIDE + at : WIDE + at + count, lanes]
                value = g1[u, pl.ds(row, count), :] + d0[u, pl.ds(row, count), :] * back
                value = jnp.where(mask_at(u, row, count), value, 0.0)
                colacc[pl.ds(row, count), :] += value
                part = fold(value)
                total_row = part if total_row is None else total_row + part
            rowg[pl.ds(u - 3, 1), :] = jnp.sum(total_row, axis=0, keepdims=True)
        return carry

    lax.fori_loop(0, 4, first_adjoint, 0)

    def filter_gradient(u, carry):
        base = first_column(u)
        high, low = split(g1[u, pl.ds(base + PAD, WIDE), :])
        gbuf[:, 0:128] = high
        gbuf[:, 128:256] = low
        for q in range(3):
            for d in range(3):
                piece = act0[u + d, pl.ds(base + PAD + 2 * (q - 1), WIDE), :]
                xbuf[:, 128 * (3 * q + d) : 128 * (3 * q + d + 1)] = piece.astype(BF16)
        fg[...] += dot_t(gbuf[...], xbuf[...])
        return carry

    lax.fori_loop(FIRST_OWN, LAST_OWN + 1, filter_gradient, 0)

    where_block = lane_block(32)
    for group in range(3):
        packed = jnp.zeros((32, 128), F32)
        for place in range(4):
            tap = 4 * group + place
            if tap > 8:
                continue
            p, q = tap // 3 - 1, tap % 3
            value = jnp.zeros((32, 128), F32)
            for b in range(4):
                source = b + 2 * p
                lanes = 128 * (3 * q + source // 4 + 1)
                both = fg[32 * b : 32 * b + 32, lanes : lanes + 128] + fg[128 + 32 * b : 160 + 32 * b, lanes : lanes + 128]
                value = value + jnp.where(where_block == source % 4, both, 0.0)
            value = value + pltpu.roll(value, 64, 1)
            value = value + pltpu.roll(value, 32, 1)
            packed = jnp.where(where_block == place, value, packed)
        out[32 * group : 32 * group + 32] = packed
    out[96:112] = jnp.zeros((16, 128), F32)
    for tap in range(10):
        out[96 + tap : 97 + tap] = jnp.sum(tacc[8 * tap : 8 * tap + 8], axis=0, keepdims=True)

    where_block = lane_block(8)
    for m in range(REACH + 1):
        packed = jnp.zeros((8, 128), F32)
        for b in range(4):
            row = 32 * m + 8 * b + HALO + PAD
            value = colacc[row : row + 8]
            value = value + pltpu.roll(value, 64, 1)
            value = value + pltpu.roll(value, 32, 1)
            packed = jnp.where(where_block == b, value, packed)
        colp[8 * m : 8 * m + 8] = packed


def reduce_kernel(n, feat, part, colp, rowg, red, vout, cbuf, vbuf, arbuf, rsbuf, bbuf, mine, gbuf, s1, r1, s2, r2, s3, r3, s4, r4):
    me = lax.axis_index("diag")
    side = n // SIDE
    pos = lax.rem(me, SIDE)
    first = me - pos
    plane = lax.div(me, SIDE)

    def dev(step):
        return lax.rem(me + step + n, n)

    def in_line(q):
        return first + q

    def across(q):
        return q * SIDE + pos

    barrier = pltpu.get_barrier_semaphore()
    for step in range(1, REACH + 1):
        pl.semaphore_signal(barrier, inc=1, device_id=(dev(-step),), device_id_type=MESH)

    def greet(s, carry):
        pl.semaphore_signal(barrier, inc=1, device_id=(in_line(lax.rem(pos + s, SIDE)),), device_id_type=MESH)
        return carry

    lax.fori_loop(1, SIDE, greet, 0)

    def greet_across(s, carry):
        pl.semaphore_signal(barrier, inc=1, device_id=(across(lax.rem(plane + s, side)),), device_id_type=MESH)
        return carry

    lax.fori_loop(1, side, greet_across, 0)
    pl.semaphore_wait(barrier, REACH + SIDE - 1 + side - 1)

    copies = []
    for m in range(1, REACH + 1):
        copies.append(
            pltpu.make_async_remote_copy(
                colp.at[pl.ds(8 * m, 8)], cbuf.at[m], s1.at[m], r1.at[m], device_id=(dev(m),), device_id_type=MESH
            )
        )
    for copy in copies:
        copy.start()
    arbuf[128:240] = part[...]
    arbuf[240:256] = jnp.zeros((16, 128), F32)
    where_block = lane_block(8)
    rows = rowg[...]
    for b in range(4):
        vbuf[1, pl.ds(b, 8, stride=4), :] = jnp.where(where_block == 1, pltpu.roll(rows, (32 - 32 * b) % 128, 1) if b != 1 else rows, 0.0)
    for copy in copies:
        copy.wait()
    own = colp[0:8]
    for m in range(1, REACH + 1):
        own = own + cbuf[m]
    for b in range(4):
        vbuf[0, 8 * b : 8 * b + 8] = jnp.where(where_block == 0, pltpu.roll(own, (128 - 32 * b) % 128, 1) if b else own, 0.0)
    both = vbuf[0] + vbuf[1]
    vout[...] = both
    high, low = split(both)
    turned_high, turned_low = split(pltpu.roll(both, 64, 1))
    f = feat[...]
    arbuf[0:128] = dot_t(
        jnp.concatenate([f[:, 0:128], f[:, 0:128], f[:, 128:256], f[:, 128:256]], axis=0),
        jnp.concatenate([high, low, turned_high, turned_low], axis=0),
    )

    def chunk(q):
        return pl.ds(pl.multiple_of(q * PART, PART), PART)

    def scatter(s, start):
        q = lax.rem(pos + s, SIDE)
        return pltpu.make_async_remote_copy(
            arbuf.at[chunk(q)], rsbuf.at[s], s2.at[s], r2.at[s], device_id=(in_line(q),), device_id_type=MESH
        )

    def across_copy(s):
        q = lax.rem(plane + s, side)
        return pltpu.make_async_remote_copy(
            mine, bbuf.at[plane], s3.at[s], r3.at[s], device_id=(across(q),), device_id_type=MESH
        )

    def spread_copy(s):
        q = lax.rem(pos + s, SIDE)
        return pltpu.make_async_remote_copy(
            gbuf.at[chunk(pos)], gbuf.at[chunk(pos)], s4.at[s], r4.at[s], device_id=(in_line(q),), device_id_type=MESH
        )

    def run(count, make):
        def begin(s, carry):
            make(s).start()
            return carry

        lax.fori_loop(1, count, begin, 0)

        def end(s, carry):
            make(s).wait()
            return carry

        lax.fori_loop(1, count, end, 0)

    run(SIDE, lambda s: scatter(s, 0))
    total = arbuf[chunk(pos), :]
    for s in range(1, SIDE):
        total = total + rsbuf[s]
    mine[...] = total
    bbuf[plane] = total
    run(side, across_copy)
    total = bbuf[0]
    for q in range(1, side):
        total = total + bbuf[q]
    gbuf[chunk(pos), :] = total
    run(SIDE, spread_copy)
    red[...] = gbuf[...]


def finish_kernel(red, vin, row_proj, col_proj, k2, ro, gfeat, grow, gcol, gone, gtwo, gread):
    v = vin[...]
    high, low = split(v)
    gfeat[...] = (
        dot_nt(high[:, 0:32], col_proj[...])
        + dot_nt(low[:, 0:32], col_proj[...])
        + dot_nt(high[:, 32:64], row_proj[...])
        + dot_nt(low[:, 32:64], row_proj[...])
    )
    weights = red[0:128]
    gcol[0:128] = weights[:, 0:32]
    grow[0:128] = weights[:, 32:64]
    gcol[128:256] = weights[:, 64:96]
    grow[128:256] = weights[:, 96:128]
    for group in range(3):
        block = red[128 + 32 * group : 160 + 32 * group].T
        count = 128 if group < 2 else 32
        gone[128 * group : 128 * group + count] = block[0:count]
    taps = red[224:240]
    taps = taps + pltpu.roll(taps, 64, 1)
    taps = taps + pltpu.roll(taps, 32, 1)
    by_channel = taps.T
    read = ro[...].astype(F32)
    total = taps[9:10, 0:32]
    for tap in range(9):
        column = by_channel[0:32, tap : tap + 1]
        gtwo[32 * tap : 32 * tap + 32] = column * read
        total = total + jnp.sum(column * k2[32 * tap : 32 * tap + 32].astype(F32), axis=0, keepdims=True)
    gread[...] = total


def shards(n, features, row_proj, col_proj, first_filter, second_filter, readout, target):
    side = n // SIDE
    vmem = pl.BlockSpec(memory_space=pltpu.VMEM)

    def shape(*dims):
        return jax.ShapeDtypeStruct(dims, F32)

    k1 = first_filter.reshape(9 * PAIR, PAIR)
    k2 = second_filter.reshape(9 * PAIR, PAIR)
    ro = readout.reshape(1, PAIR)
    colw, roww, targ = pl.pallas_call(
        functools.partial(gather_kernel, n),
        out_shape=(shape(88, 128), shape(24, 128), shape(48, 256)),
        in_specs=[vmem] * 4,
        out_specs=(vmem,) * 3,
        scratch_shapes=[
            pltpu.VMEM((1, 32, 128), F32),
            pltpu.VMEM((16, 128), F32),
            pltpu.VMEM((AHEAD + 2, 16, 128), F32),
            pltpu.VMEM((8, 256), F32),
            pltpu.VMEM((8, 256), F32),
            SEM((AHEAD + 2,)),
            SEM((AHEAD + 2,)),
            SEM((2,)),
            SEM((2,)),
        ],
        compiler_params=pltpu.CompilerParams(collective_id=0, has_side_effects=True),
        name="gather_window",
    )(features, row_proj, col_proj, target)

    def field(groups):
        return pltpu.VMEM((groups, LENGTH, 128), F32)

    part, colp, rowg = pl.pallas_call(
        functools.partial(band_kernel, n * ROWS),
        out_shape=(shape(112, 128), shape(72, 128), shape(8, 128)),
        in_specs=[vmem] * 6,
        out_specs=(vmem,) * 3,
        scratch_shapes=[
            pltpu.VMEM((1536, 256), BF16),
            pltpu.VMEM((1536, 256), BF16),
            pltpu.VMEM((72, 128), F32),
            pltpu.VMEM((8, 128), F32),
            pltpu.VMEM((LENGTH, 128), F32),
            pltpu.VMEM((LENGTH, 128), jnp.int32),
            pltpu.VMEM((LENGTH, 128), F32),
            field(GROUPS + 2),
        ]
        + [field(GROUPS)] * 7
        + [
            pltpu.VMEM((WIDE, 1536), BF16),
            pltpu.VMEM((2 * WIDE, 1536), BF16),
            pltpu.VMEM((2 * WIDE, 256), F32),
            pltpu.VMEM((WIDE, 512), BF16),
            pltpu.VMEM((WIDE, 1152), BF16),
            pltpu.VMEM((WIDE, 256), BF16),
            pltpu.VMEM((256, 1152), F32),
            pltpu.VMEM((80, 128), F32),
            pltpu.VMEM((LENGTH, 128), F32),
            pltpu.VMEM((288, 256), F32),
        ],
        compiler_params=pltpu.CompilerParams(vmem_limit_bytes=48 * 1024 * 1024),
        name="band_gradients",
    )(colw, roww, targ, k1, k2, ro)

    red, v = pl.pallas_call(
        functools.partial(reduce_kernel, n),
        out_shape=(shape(256, 128), shape(32, 128)),
        in_specs=[vmem] * 4,
        out_specs=(vmem,) * 2,
        scratch_shapes=[
            pltpu.VMEM((REACH + 1, 8, 128), F32),
            pltpu.VMEM((2, 32, 128), F32),
            pltpu.VMEM((256, 128), F32),
            pltpu.VMEM((SIDE, PART, 128), F32),
            pltpu.VMEM((side, PART, 128), F32),
            pltpu.VMEM((PART, 128), F32),
            pltpu.VMEM((256, 128), F32),
            SEM((REACH + 1,)),
            SEM((REACH + 1,)),
            SEM((SIDE,)),
            SEM((SIDE,)),
            SEM((side,)),
            SEM((side,)),
            SEM((SIDE,)),
            SEM((SIDE,)),
        ],
        compiler_params=pltpu.CompilerParams(collective_id=1, has_side_effects=True),
        name="reduce_gradients",
    )(features, part, colp, rowg)

    gfeat, grow, gcol, gone, gtwo, gread = pl.pallas_call(
        finish_kernel,
        out_shape=(shape(ROWS, 256), shape(256, 32), shape(256, 32), shape(288, 32), shape(288, 32), shape(1, 32)),
        in_specs=[vmem] * 6,
        out_specs=(vmem,) * 6,
        name="finish",
    )(red, v, row_proj, col_proj, k2, ro)
    return gfeat, grow, gcol, gone.reshape(3, 3, PAIR, PAIR), gtwo.reshape(3, 3, PAIR, PAIR), gread.reshape(PAIR)


def solution(mesh):
    n = mesh.shape["diag"]
    in_specs = (P("diag", None), P(), P(), P(), P(), P(), P("diag", None))
    out_specs = (P("diag", None), P(), P(), P(), P(), P())
    return jax.shard_map(
        functools.partial(shards, n), mesh=mesh, in_specs=in_specs, out_specs=out_specs, check_vma=False
    )
```

```python
import functools
import math

import jax
import jax.numpy as jnp
from jax import lax
from jax.experimental import pallas as pl
from jax.experimental.pallas import tpu as pltpu
from jax.sharding import PartitionSpec as P

MESH = pl.DeviceIdType.MESH
F32, BF16 = jnp.float32, jnp.bfloat16

ROWS = 32
BAND = 256
PAIR = 32
HALO = 12
GROUPS = (ROWS + 2 * HALO) // 4
FIRST_OWN, LAST_OWN = 3, 10
PAD = 16
LENGTH = 352
WIDE, SPAN, CHUNK = 272, 264, 88
AHEAD = 9
REACH = 8
C0 = math.sqrt(2.0 / math.pi)
C1 = C0 * 0.044715
SIDE = 16
PART = 16
SEM = pltpu.SemaphoreType.DMA


def iota(shape, dim):
    return lax.broadcasted_iota(jnp.int32, shape, dim)


def lane_block(rows):
    return lax.shift_right_logical(iota((rows, 128), 1), 5)


def gelu_and_slope(x):
    square = x * x
    t = jnp.tanh(x * (C0 + C1 * square))
    h = 0.5 * x
    act = h + h * t
    slope = (0.5 + 0.5 * t) + h * (1.0 - t * t) * (C0 + 3.0 * C1 * square)
    return act.astype(BF16).astype(F32), slope


def split(x):
    high = x.astype(BF16)
    return high, (x - high.astype(F32)).astype(BF16)


def fold(x):
    total = x[0:8]
    for i in range(1, x.shape[0] // 8):
        total = total + x[8 * i : 8 * i + 8]
    return total


def dot(a, b):
    return jnp.dot(a, b, preferred_element_type=F32)


def dot_t(a, b):
    return lax.dot_general(a, b, (((0,), (0,)), ((), ())), preferred_element_type=F32)


def dot_nt(a, b):
    return lax.dot_general(a, b, (((1,), (1,)), ((), ())), preferred_element_type=F32)


def repeater(lanes):
    return (jnp.bitwise_and(iota((PAIR, lanes), 1), 31) == iota((PAIR, lanes), 0)).astype(F32).astype(BF16)


def spread(block):
    turned = [block] + [pltpu.roll(block, 32 * s, 1) for s in (1, 2, 3)]
    where_block = lane_block(8)
    outs = []
    for b in range(4):
        value = turned[(3 - b) % 4]
        for other in range(3):
            value = jnp.where(where_block == other, turned[(other - b) % 4], value)
        outs.append(value)
    return outs


def step_kernel(
    n, feat, row_t, col_t, target, k1, k2, ro, red, vout,
    proj, sbuf, rbuf, tlow, thigh, roww, w1, wa, w2, rol, colr, mk, ts, act0, f0, d0, act1, f1, d1, mis, g1,
    lhs, lhs2, res, qbuf, xall, gall, fg, tacc, colacc, tiles, colp, rowg, cbuf, vbuf, arbuf, rsbuf, bbuf, mine, gbuf,
    ss, rs, s1, r1, s2, r2, s3, r3, s4, r4,
):
    me = lax.axis_index("diag")
    start = me * ROWS
    side = n // SIDE
    pos = lax.rem(me, SIDE)
    first = me - pos
    plane = lax.div(me, SIDE)

    def dev(step):
        return lax.rem(me + step + n, n)

    def in_line(q):
        return first + q

    def across(q):
        return q * SIDE + pos

    barrier = pltpu.get_barrier_semaphore()
    for step in (-1,) + tuple(range(1, AHEAD + 1)) + tuple(range(-REACH, 0)):
        pl.semaphore_signal(barrier, inc=1, device_id=(dev(step),), device_id_type=MESH)

    def greet(s, carry):
        pl.semaphore_signal(barrier, inc=1, device_id=(in_line(lax.rem(pos + s, SIDE)),), device_id_type=MESH)
        return carry

    lax.fori_loop(1, SIDE, greet, 0)

    def greet_across(s, carry):
        pl.semaphore_signal(barrier, inc=1, device_id=(across(lax.rem(plane + s, side)),), device_id_type=MESH)
        return carry

    lax.fori_loop(1, side, greet_across, 0)

    proj[...] = dot_nt(feat[...], jnp.concatenate([row_t[...]] * 4, axis=0))
    cc = dot_nt(feat[...], jnp.concatenate([col_t[...]] * 4, axis=0))
    where_block = lane_block(8)
    row_c = jnp.zeros((8, 128), F32)
    col_c = jnp.zeros((8, 128), F32)
    for b in range(4):
        row_c = jnp.where(where_block == b, proj[pl.ds(b, 8, stride=4), :], row_c)
        col_c = jnp.where(where_block == b, cc[8 * b : 8 * b + 8], col_c)
    sbuf[0:8] = col_c
    sbuf[8:16] = row_c
    pl.semaphore_wait(barrier, AHEAD + 1 + REACH + SIDE - 1 + side - 1)
    gathers = []
    for slot, step in ((0, 1), (2, -1)):
        gathers.append(
            pltpu.make_async_remote_copy(sbuf, rbuf.at[slot], ss.at[slot], rs.at[slot], device_id=(dev(step),), device_id_type=MESH)
        )
    for m in range(3, AHEAD + 2):
        gathers.append(
            pltpu.make_async_remote_copy(
                sbuf.at[pl.ds(0, 8)], rbuf.at[m, pl.ds(0, 8)], ss.at[m], rs.at[m], device_id=(dev(1 - m),), device_id_type=MESH
            )
        )
    gathers.append(
        pltpu.make_async_remote_copy(
            target.at[pl.ds(24, 8)], tlow, ss.at[AHEAD + 2], rs.at[AHEAD + 2], device_id=(dev(1),), device_id_type=MESH
        )
    )
    gathers.append(
        pltpu.make_async_remote_copy(
            target.at[pl.ds(0, 8)], thigh, ss.at[AHEAD + 3], rs.at[AHEAD + 3], device_id=(dev(-1),), device_id_type=MESH
        )
    )
    for copy in gathers:
        copy.start()

    rep8 = repeater(256)
    where_out = lax.shift_right_logical(iota((PAIR, 256), 1), 5)

    def build(weights, sign):
        for q in range(3):
            for place, ri in enumerate((8, 9, -2, -1, 0, 1, 2, 3, 4, 5, 6, 7)):
                value = jnp.zeros((PAIR, 256), F32)
                for p in range(3):
                    tap = 3 * p + q
                    ro_here = ri - sign * 2 * (p - 1)
                    if 0 <= ro_here < 8:
                        value = jnp.where(where_out == ro_here, tiles[32 * tap : 32 * tap + 32], value)
                row = (q * 12 + place) * 32
                weights[row : row + 32] = value.astype(BF16)

    tiles[...] = dot(k1[...], rep8)
    build(w1, 1)
    for tap in range(9):
        tiles[32 * tap : 32 * tap + 32] = dot_t(k1[32 * tap : 32 * tap + 32], rep8)
    build(wa, -1)
    ro8 = jnp.broadcast_to(ro[...].astype(F32), (8, PAIR)).astype(BF16)
    rol[...] = dot(ro8, repeater(128))
    for tap in range(9):
        taps = k2[32 * tap : 32 * tap + 32]
        w2[8 * tap : 8 * tap + 8] = dot_nt(ro8, jnp.concatenate([taps] * 4, axis=0))

    act0[0] = jnp.zeros((LENGTH, 128), F32)
    act0[GROUPS + 1] = jnp.zeros((LENGTH, 128), F32)
    colacc[...] = jnp.zeros((LENGTH, 128), F32)
    tacc[...] = jnp.zeros((80, 128), F32)
    ts[...] = jnp.zeros((LENGTH, 128), F32)
    arbuf[240:256] = jnp.zeros((16, 128), F32)
    column = iota((LENGTH, 128), 0) - PAD
    mk[...] = jnp.where(column + (start - HALO) < n * ROWS, column - lane_block(LENGTH), 1 << 20)

    for copy in gathers:
        copy.wait()
    for m in range(AHEAD + 2):
        for b, value in enumerate(spread(col_c if m == 1 else rbuf[m, 0:8])):
            row = 32 * (m - 1) + 8 * b + HALO + PAD
            if row >= 0 and row + 8 <= LENGTH:
                colr[row : row + 8] = value
    roww[0:8] = rbuf[0, 8:16]
    roww[8:16] = row_c
    roww[16:24] = rbuf[2, 8:16]
    wide = jnp.concatenate([tlow[...], target[...], thigh[...]], axis=0)
    wide = jnp.concatenate([wide, jnp.zeros((48, 128), F32)], axis=1)
    wide = jnp.concatenate([wide, jnp.zeros((80, 384), F32)], axis=0)
    sheared = pltpu.roll(wide, 0, 1, stride=1, stride_axis=0)
    ts[4 + PAD : 4 + PAD + 312] = sheared.T[0:312]

    def first_column(u):
        return pl.multiple_of(8 * lax.shift_right_logical(u, 1), 8)

    def mask_at(u, row, count):
        k = mk[pl.ds(row, count), :] - 4 * u
        limit = jnp.where(start + 4 * u - HALO >= 0, BAND, 0)
        return jnp.logical_and(k >= 0, k < limit)

    def clear_sides(buffer, index, base):
        buffer[index, pl.ds(base, 16), :] = jnp.zeros((16, 128), F32)
        buffer[index, pl.ds(base + PAD + SPAN, 24), :] = jnp.zeros((24, 128), F32)

    left = lane_block(WIDE) < 2

    def pieces(buffer, index, row):
        ends = jnp.where(left, buffer[index + 3, pl.ds(row, WIDE), :], buffer[index, pl.ds(row, WIDE), :])
        return ends, buffer[index + 1, pl.ds(row, WIDE), :], buffer[index + 2, pl.ds(row, WIDE), :]

    def make_field(u, carry):
        base = first_column(u)
        clear_sides(act0, u + 1, base)
        row_here = roww[pl.ds(u + 5, 1), :]
        for ch in range(3):
            row = base + PAD + CHUNK * ch
            mask = mask_at(u, row, CHUNK)
            x = jnp.where(mask, row_here + colr[pl.ds(row, CHUNK), :], 0.0)
            f0[u, pl.ds(row, CHUNK), :] = x
            act, slope = gelu_and_slope(x)
            act0[u + 1, pl.ds(row, CHUNK), :] = act
            d0[u, pl.ds(row, CHUNK), :] = jnp.where(mask, slope, 0.0)
        return carry

    lax.fori_loop(0, GROUPS, make_field, 0)

    def first_conv(v, carry):
        base = pl.multiple_of(8 * v, 8)
        for q in range(3):
            for d, piece in enumerate(pieces(act0, 2 * v, base + PAD + 2 * (q - 1))):
                lhs[:, 128 * (3 * q + d) : 128 * (3 * q + d + 1)] = piece.astype(BF16)
        res[0:WIDE] = dot(lhs[...], w1[...])
        for h in range(2):
            u = 2 * v + h
            clear_sides(act1, u, base)
            for ch in range(3):
                row = base + PAD + CHUNK * ch
                conv = res[CHUNK * ch : CHUNK * ch + CHUNK, 128 * h : 128 * h + 128]
                mask = mask_at(u, row, CHUNK)
                x = jnp.where(mask, f0[u, pl.ds(row, CHUNK), :] + conv, 0.0)
                f1[u, pl.ds(row, CHUNK), :] = x
                act, slope = gelu_and_slope(x)
                act1[u, pl.ds(row, CHUNK), :] = act
                d1[u, pl.ds(row, CHUNK), :] = jnp.where(mask, slope, 0.0)
        return carry

    lax.fori_loop(0, GROUPS // 2, first_conv, 0)

    bins = lax.shift_right_logical(iota((128, 128), 0), 5)
    ones = (bins == lane_block(128)).astype(F32).astype(BF16)

    def make_misfit(u, carry):
        base = first_column(u)
        clear_sides(mis, u, base)
        for ch in range(3):
            row = base + PAD + CHUNK * ch
            value = rol[0:1] * f1[u, pl.ds(row, CHUNK), :]
            for p in range(3):
                for q in range(3):
                    tap = 3 * p + q
                    value = value + w2[8 * tap : 8 * tap + 1] * act1[u + p - 1, pl.ds(row + 4 * (q - 1), CHUNK), :]
            res[CHUNK * ch : CHUNK * ch + CHUNK, 0:128] = value
        high, low = split(res[0:WIDE, 0:128])
        qbuf[:, 0:128] = high
        qbuf[:, 128:256] = low
        high, low = split(ts[pl.ds(base + PAD, WIDE), :])
        qbuf[:, 256:384] = high
        qbuf[:, 384:512] = low
        pick = jnp.where(iota((128, 128), 0) == 4 * u - 4 + lane_block(128), -1.0, 0.0).astype(BF16)
        res[0:WIDE, 128:256] = dot(qbuf[...], jnp.concatenate([ones, ones, pick, pick], axis=0))
        for ch in range(3):
            row = base + PAD + CHUNK * ch
            value = res[CHUNK * ch : CHUNK * ch + CHUNK, 128:256] * (1.0 / BAND)
            mis[u, pl.ds(row, CHUNK), :] = jnp.where(mask_at(u, row, CHUNK), value, 0.0)
        return carry

    lax.fori_loop(1, GROUPS - 1, make_misfit, 0)

    def make_cotangent(u, carry):
        base = first_column(u)
        clear_sides(g1, u, base)
        sums = [None] * 10
        for ch in range(3):
            row = base + PAD + CHUNK * ch
            act = act1[u, pl.ds(row, CHUNK), :]
            back = None
            for p in range(3):
                for q in range(3):
                    tap = 3 * p + q
                    m = mis[u - (p - 1), pl.ds(row - 4 * (q - 1), CHUNK), :]
                    term = w2[8 * tap : 8 * tap + 1] * m
                    back = term if back is None else back + term
                    part = fold(act * m)
                    sums[tap] = part if sums[tap] is None else sums[tap] + part
            m = mis[u, pl.ds(row, CHUNK), :]
            part = fold(m * f1[u, pl.ds(row, CHUNK), :])
            sums[9] = part if sums[9] is None else sums[9] + part
            g1[u, pl.ds(row, CHUNK), :] = rol[0:1] * m + d1[u, pl.ds(row, CHUNK), :] * back
        for tap in range(10):
            source = u - (tap // 3 - 1) if tap < 9 else u
            own = jnp.logical_and(source >= FIRST_OWN, source <= LAST_OWN)
            tacc[8 * tap : 8 * tap + 8] += jnp.where(own, sums[tap], 0.0)
        return carry

    lax.fori_loop(2, GROUPS - 2, make_cotangent, 0)

    def first_adjoint(w, carry):
        base = pl.multiple_of(8 * w + 8, 8)
        for q in range(3):
            for d, piece in enumerate(pieces(g1, 2 * w + 2, base + PAD - 2 * (q - 1))):
                high, low = split(piece)
                lanes = slice(128 * (3 * q + d), 128 * (3 * q + d + 1))
                lhs2[0:WIDE, lanes] = high
                lhs2[WIDE : 2 * WIDE, lanes] = low
        res[...] = dot(lhs2[...], wa[...])
        for h in range(2):
            u = 2 * w + 3 + h
            total_row = None
            for ch in range(3):
                at = CHUNK * ch + 8 * h
                row = base + PAD + at
                lanes = slice(128 * h, 128 * h + 128)
                back = res[at : at + CHUNK, lanes] + res[WIDE + at : WIDE + at + CHUNK, lanes]
                value = g1[u, pl.ds(row, CHUNK), :] + d0[u, pl.ds(row, CHUNK), :] * back
                colacc[pl.ds(row, CHUNK), :] += value
                part = fold(value)
                total_row = part if total_row is None else total_row + part
            rowg[pl.ds(u - 3, 1), :] = jnp.sum(total_row, axis=0, keepdims=True)
        return carry

    lax.fori_loop(0, 4, first_adjoint, 0)

    where_block = lane_block(8)
    for m in range(REACH + 1):
        packed = jnp.zeros((8, 128), F32)
        for b in range(4):
            row = 32 * m + 8 * b + HALO + PAD
            value = colacc[row : row + 8]
            value = value + pltpu.roll(value, 64, 1)
            value = value + pltpu.roll(value, 32, 1)
            packed = jnp.where(where_block == b, value, packed)
        colp[8 * m : 8 * m + 8] = packed
    columns = []
    for m in range(1, REACH + 1):
        columns.append(
            pltpu.make_async_remote_copy(
                colp.at[pl.ds(8 * m, 8)], cbuf.at[m], s1.at[m], r1.at[m], device_id=(dev(m),), device_id_type=MESH
            )
        )
    for copy in columns:
        copy.start()

    def collect(u, carry):
        base = first_column(u)
        at = pl.multiple_of(WIDE * (u - FIRST_OWN), 16)
        high, low = split(g1[u, pl.ds(base + PAD, WIDE), :])
        gall[pl.ds(at, WIDE), 0:128] = high
        gall[pl.ds(at, WIDE), 128:256] = low
        for q in range(3):
            for d in range(3):
                piece = act0[u + d, pl.ds(base + PAD + 2 * (q - 1), WIDE), :]
                xall[pl.ds(at, WIDE), 128 * (3 * q + d) : 128 * (3 * q + d + 1)] = piece.astype(BF16)
        return carry

    lax.fori_loop(FIRST_OWN, LAST_OWN + 1, collect, 0)
    fg[...] = dot_t(gall[...], xall[...])

    where_block = lane_block(32)
    for group in range(3):
        packed = jnp.zeros((32, 128), F32)
        for place in range(4):
            tap = 4 * group + place
            if tap > 8:
                continue
            p, q = tap // 3 - 1, tap % 3
            value = jnp.zeros((32, 128), F32)
            for b in range(4):
                source = b + 2 * p
                lanes = 128 * (3 * q + source // 4 + 1)
                both = fg[32 * b : 32 * b + 32, lanes : lanes + 128] + fg[128 + 32 * b : 160 + 32 * b, lanes : lanes + 128]
                value = value + jnp.where(where_block == source % 4, both, 0.0)
            value = value + pltpu.roll(value, 64, 1)
            value = value + pltpu.roll(value, 32, 1)
            packed = jnp.where(where_block == place, value, packed)
        arbuf[128 + 32 * group : 160 + 32 * group] = packed
    for tap in range(10):
        arbuf[224 + tap : 225 + tap] = jnp.sum(tacc[8 * tap : 8 * tap + 8], axis=0, keepdims=True)

    where_block = lane_block(8)
    rows = rowg[...]
    for b in range(4):
        vbuf[1, pl.ds(b, 8, stride=4), :] = jnp.where(where_block == 1, pltpu.roll(rows, (32 - 32 * b) % 128, 1) if b != 1 else rows, 0.0)
    for copy in columns:
        copy.wait()
    own = colp[0:8]
    for m in range(1, REACH + 1):
        own = own + cbuf[m]
    for b in range(4):
        vbuf[0, 8 * b : 8 * b + 8] = jnp.where(where_block == 0, pltpu.roll(own, (128 - 32 * b) % 128, 1) if b else own, 0.0)
    both = vbuf[0] + vbuf[1]
    vout[...] = both
    high, low = split(both)
    by_feature = dot_t(jnp.concatenate([high, low], axis=0), jnp.concatenate([feat[...]] * 2, axis=0))
    arbuf[0:64] = by_feature[0:64, 0:128]
    arbuf[64:128] = by_feature[0:64, 128:256]

    def chunk(q):
        return pl.ds(pl.multiple_of(q * PART, PART), PART)

    def scatter(s):
        q = lax.rem(pos + s, SIDE)
        return pltpu.make_async_remote_copy(
            arbuf.at[chunk(q)], rsbuf.at[s], s2.at[s], r2.at[s], device_id=(in_line(q),), device_id_type=MESH
        )

    def across_copy(s):
        q = lax.rem(plane + s, side)
        return pltpu.make_async_remote_copy(
            mine, bbuf.at[plane], s3.at[s], r3.at[s], device_id=(across(q),), device_id_type=MESH
        )

    def spread_copy(s):
        q = lax.rem(pos + s, SIDE)
        return pltpu.make_async_remote_copy(
            gbuf.at[chunk(pos)], gbuf.at[chunk(pos)], s4.at[s], r4.at[s], device_id=(in_line(q),), device_id_type=MESH
        )

    def run(count, make):
        def begin(s, carry):
            make(s).start()
            return carry

        lax.fori_loop(1, count, begin, 0)

        def end(s, carry):
            make(s).wait()
            return carry

        lax.fori_loop(1, count, end, 0)

    run(SIDE, scatter)
    total = arbuf[chunk(pos), :]
    for s in range(1, SIDE):
        total = total + rsbuf[s]
    mine[...] = total
    bbuf[plane] = total
    run(side, across_copy)
    total = bbuf[0]
    for q in range(1, side):
        total = total + bbuf[q]
    gbuf[chunk(pos), :] = total
    run(SIDE, spread_copy)
    red[...] = gbuf[...]


def finish_kernel(red, vin, row_t, col_t, k2, ro, gfeat, grow, gcol, gone, gtwo, gread):
    high, low = split(vin[...])
    both = jnp.concatenate([col_t[...], row_t[...]], axis=0)
    gfeat[...] = dot(high[:, 0:64], both) + dot(low[:, 0:64], both)
    gcol[:, 0:128] = red[0:32]
    gcol[:, 128:256] = red[64:96]
    grow[:, 0:128] = red[32:64]
    grow[:, 128:256] = red[96:128]
    for group in range(3):
        block = red[128 + 32 * group : 160 + 32 * group].T
        count = 128 if group < 2 else 32
        gone[128 * group : 128 * group + count] = block[0:count]
    taps = red[224:240]
    taps = taps + pltpu.roll(taps, 64, 1)
    taps = taps + pltpu.roll(taps, 32, 1)
    by_channel = taps.T
    read = ro[...].astype(F32)
    total = taps[9:10, 0:32]
    for tap in range(9):
        column = by_channel[0:32, tap : tap + 1]
        gtwo[32 * tap : 32 * tap + 32] = column * read
        total = total + jnp.sum(column * k2[32 * tap : 32 * tap + 32].astype(F32), axis=0, keepdims=True)
    gread[...] = total


def shards(n, features, row_proj, col_proj, first_filter, second_filter, readout, target):
    side = n // SIDE
    vmem = pl.BlockSpec(memory_space=pltpu.VMEM)

    def shape(*dims):
        return jax.ShapeDtypeStruct(dims, F32)

    def real(*dims):
        return pltpu.VMEM(dims, F32)

    def half(*dims):
        return pltpu.VMEM(dims, BF16)

    k1 = first_filter.reshape(9 * PAIR, PAIR)
    k2 = second_filter.reshape(9 * PAIR, PAIR)
    ro = readout.reshape(1, PAIR)
    row_t, col_t = row_proj.T, col_proj.T
    scratch = dict(
        proj=real(32, 128), sbuf=real(16, 128), rbuf=real(AHEAD + 2, 16, 128), tlow=real(8, 256), thigh=real(8, 256),
        roww=real(24, 128), w1=half(1152, 256), wa=half(1152, 256), w2=real(72, 128), rol=real(8, 128),
        colr=real(LENGTH, 128), mk=pltpu.VMEM((LENGTH, 128), jnp.int32), ts=real(LENGTH, 128),
        act0=real(GROUPS + 2, LENGTH, 128), f0=real(GROUPS, LENGTH, 128), d0=real(GROUPS, LENGTH, 128),
        act1=real(GROUPS, LENGTH, 128), f1=real(GROUPS, LENGTH, 128), d1=real(GROUPS, LENGTH, 128),
        mis=real(GROUPS, LENGTH, 128), g1=real(GROUPS, LENGTH, 128),
        lhs=half(WIDE, 1152), lhs2=half(2 * WIDE, 1152), res=real(2 * WIDE, 256), qbuf=half(WIDE, 512),
        xall=half(8 * WIDE, 1152), gall=half(8 * WIDE, 256), fg=real(256, 1152), tacc=real(80, 128),
        colacc=real(LENGTH, 128), tiles=real(288, 256), colp=real(72, 128), rowg=real(8, 128),
        cbuf=real(REACH + 1, 8, 128), vbuf=real(2, 32, 128), arbuf=real(256, 128), rsbuf=real(SIDE, PART, 128),
        bbuf=real(side, PART, 128), mine=real(PART, 128), gbuf=real(256, 128),
        ss=SEM((AHEAD + 4,)), rs=SEM((AHEAD + 4,)), s1=SEM((REACH + 1,)), r1=SEM((REACH + 1,)),
        s2=SEM((SIDE,)), r2=SEM((SIDE,)), s3=SEM((side,)), r3=SEM((side,)), s4=SEM((SIDE,)), r4=SEM((SIDE,)),
    )
    red, v = pl.pallas_call(
        functools.partial(step_kernel, n),
        out_shape=(shape(256, 128), shape(32, 128)),
        in_specs=[vmem] * 7,
        out_specs=(vmem,) * 2,
        scratch_shapes=list(scratch.values()),
        compiler_params=pltpu.CompilerParams(
            collective_id=0, has_side_effects=True, vmem_limit_bytes=52 * 1024 * 1024
        ),
        name="step",
    )(features, row_t, col_t, target, k1, k2, ro)

    gfeat, grow, gcol, gone, gtwo, gread = pl.pallas_call(
        finish_kernel,
        out_shape=(shape(ROWS, 256), shape(32, 256), shape(32, 256), shape(288, 32), shape(288, 32), shape(1, 32)),
        in_specs=[vmem] * 6,
        out_specs=(vmem,) * 6,
        name="finish",
    )(red, v, row_t, col_t, k2, ro)
    return gfeat, grow.T, gcol.T, gone.reshape(3, 3, PAIR, PAIR), gtwo.reshape(3, 3, PAIR, PAIR), gread.reshape(PAIR)


def solution(mesh):
    n = mesh.shape["diag"]
    in_specs = (P("diag", None), P(), P(), P(), P(), P(), P("diag", None))
    out_specs = (P("diag", None), P(), P(), P(), P(), P())
    return jax.shard_map(
        functools.partial(shards, n), mesh=mesh, in_specs=in_specs, out_specs=out_specs, check_vma=False
    )
```

```python
import functools
import math

import jax
import jax.numpy as jnp
from jax import lax
from jax.experimental import pallas as pl
from jax.experimental.pallas import tpu as pltpu
from jax.sharding import PartitionSpec as P

MESH = pl.DeviceIdType.MESH
F32, BF16 = jnp.float32, jnp.bfloat16

ROWS = 32
BAND = 256
PAIR = 32
HALO = 12
GROUPS = (ROWS + 2 * HALO) // 4
FIRST_OWN, LAST_OWN = 3, 10
PAD = 16
LENGTH = 352
WIDE, SPAN, CHUNK = 272, 264, 88
AHEAD = 9
REACH = 8
C0 = math.sqrt(2.0 / math.pi)
C1 = C0 * 0.044715
SIDE = 16
LINE = 8
PART = 16
SEM = pltpu.SemaphoreType.DMA


def iota(shape, dim):
    return lax.broadcasted_iota(jnp.int32, shape, dim)


def lane_block(rows):
    return lax.shift_right_logical(iota((rows, 128), 1), 5)


def gelu_and_slope(x):
    square = x * x
    t = jnp.tanh(x * (C0 + C1 * square))
    h = 0.5 * x
    act = h + h * t
    slope = (0.5 + 0.5 * t) + h * (1.0 - t * t) * (C0 + 3.0 * C1 * square)
    return act.astype(BF16).astype(F32), slope


def split(x):
    high = x.astype(BF16)
    return high, (x - high.astype(F32)).astype(BF16)


def fold(x):
    total = x[0:8]
    for i in range(1, x.shape[0] // 8):
        total = total + x[8 * i : 8 * i + 8]
    return total


def dot(a, b):
    return jnp.dot(a, b, preferred_element_type=F32)


def dot_t(a, b):
    return lax.dot_general(a, b, (((0,), (0,)), ((), ())), preferred_element_type=F32)


def dot_nt(a, b):
    return lax.dot_general(a, b, (((1,), (1,)), ((), ())), preferred_element_type=F32)


def repeater(lanes):
    return (jnp.bitwise_and(iota((PAIR, lanes), 1), 31) == iota((PAIR, lanes), 0)).astype(F32).astype(BF16)


def spread(block):
    turned = [block] + [pltpu.roll(block, 32 * s, 1) for s in (1, 2, 3)]
    where_block = lane_block(8)
    outs = []
    for b in range(4):
        value = turned[(3 - b) % 4]
        for other in range(3):
            value = jnp.where(where_block == other, turned[(other - b) % 4], value)
        outs.append(value)
    return outs


def step_kernel(
    n, feat_in, row_in, col_in, target_in, k1_in, k2_in, ro, red,
    feat, row_t, col_t, target, k1, k2,
    proj, sbuf, rbuf, tlow, thigh, roww, w1, wa, w2, rol, colr, mk, ts, act0, f0, d0, act1, f1, d1, mis, g1,
    lhs, lhs2, k2t, res, qbuf, xall, gall, fg, tacc, colacc, tiles, colp, rowg, cbuf, vbuf, arbuf, pairbuf, halfbuf, rsbuf, bbuf, mine, gbuf,
    loads, ss, rs, s1, r1, s2, r2, s3, r3, s4, r4, s5, r5,
):
    me = lax.axis_index("diag")
    start = me * ROWS
    side = n // SIDE
    pos = lax.rem(me, SIDE)
    core = lax.rem(me, 2)
    depth = lax.div(pos, 2)
    plane = lax.div(me, SIDE)
    partner = me + 1 - 2 * core

    def dev(step):
        return lax.rem(me + step + n, n)

    def in_line(q):
        return me + 2 * (q - depth)

    def across(q):
        return q * SIDE + pos

    fetches = [
        pltpu.make_async_copy(source, place, loads.at[i])
        for i, (source, place) in enumerate(
            ((feat_in, feat), (row_in, row_t), (col_in, col_t), (k1_in, k1), (k2_in, k2), (target_in, target))
        )
    ]
    for fetch in fetches:
        fetch.start()

    barrier = pltpu.get_barrier_semaphore()
    for step in (-1,) + tuple(range(1, AHEAD + 1)) + tuple(range(-REACH, 0)):
        pl.semaphore_signal(barrier, inc=1, device_id=(dev(step),), device_id_type=MESH)

    def greet(s, carry):
        pl.semaphore_signal(barrier, inc=1, device_id=(in_line(lax.rem(depth + s, LINE)),), device_id_type=MESH)
        return carry

    lax.fori_loop(1, LINE, greet, 0)
    pl.semaphore_signal(barrier, inc=1, device_id=(partner,), device_id_type=MESH)

    def greet_across(s, carry):
        pl.semaphore_signal(barrier, inc=1, device_id=(across(lax.rem(plane + s, side)),), device_id_type=MESH)
        return carry

    lax.fori_loop(1, side, greet_across, 0)

    for fetch in fetches[0:3]:
        fetch.wait()
    proj[...] = dot_nt(feat[...], jnp.concatenate([row_t[...]] * 4, axis=0))
    cc = dot_nt(feat[...], jnp.concatenate([col_t[...]] * 4, axis=0))
    where_block = lane_block(8)
    row_c = jnp.zeros((8, 128), F32)
    col_c = jnp.zeros((8, 128), F32)
    for b in range(4):
        row_c = jnp.where(where_block == b, proj[pl.ds(b, 8, stride=4), :], row_c)
        col_c = jnp.where(where_block == b, cc[8 * b : 8 * b + 8], col_c)
    sbuf[0:8] = col_c
    sbuf[8:16] = row_c
    pl.semaphore_wait(barrier, AHEAD + 1 + REACH + LINE + side - 1)
    gathers = []
    for slot, step in ((0, 1), (2, -1)):
        gathers.append(
            pltpu.make_async_remote_copy(sbuf, rbuf.at[slot], ss.at[slot], rs.at[slot], device_id=(dev(step),), device_id_type=MESH)
        )
    for m in range(3, AHEAD + 2):
        gathers.append(
            pltpu.make_async_remote_copy(
                sbuf.at[pl.ds(0, 8)], rbuf.at[m, pl.ds(0, 8)], ss.at[m], rs.at[m], device_id=(dev(1 - m),), device_id_type=MESH
            )
        )
    gathers.append(
        pltpu.make_async_remote_copy(
            target_in.at[pl.ds(24, 8)], tlow, ss.at[AHEAD + 2], rs.at[AHEAD + 2], device_id=(dev(1),), device_id_type=MESH
        )
    )
    gathers.append(
        pltpu.make_async_remote_copy(
            target_in.at[pl.ds(0, 8)], thigh, ss.at[AHEAD + 3], rs.at[AHEAD + 3], device_id=(dev(-1),), device_id_type=MESH
        )
    )
    for copy in gathers:
        copy.start()

    for fetch in fetches[3:6]:
        fetch.wait()
    rep8 = repeater(256)
    where_out = lax.shift_right_logical(iota((PAIR, 256), 1), 5)

    def build(weights, sign):
        for q in range(3):
            for place, ri in enumerate((8, 9, -2, -1, 0, 1, 2, 3, 4, 5, 6, 7)):
                value = jnp.zeros((PAIR, 256), F32)
                for p in range(3):
                    tap = 3 * p + q
                    ro_here = ri - sign * 2 * (p - 1)
                    if 0 <= ro_here < 8:
                        value = jnp.where(where_out == ro_here, tiles[32 * tap : 32 * tap + 32], value)
                row = (q * 12 + place) * 32
                weights[row : row + 32] = value.astype(BF16)

    tiles[...] = dot(k1[...], rep8)
    build(w1, 1)
    for tap in range(9):
        tiles[32 * tap : 32 * tap + 32] = dot_t(k1[32 * tap : 32 * tap + 32], rep8)
    build(wa, -1)
    ro8 = jnp.broadcast_to(ro[...].astype(F32), (8, PAIR)).astype(BF16)
    rol[...] = dot(ro8, repeater(128))
    for tap in range(9):
        for b in range(4):
            row = 128 * tap + 32 * b
            k2t[row : row + 32] = k2[32 * tap : 32 * tap + 32]
        w2[8 * tap : 8 * tap + 8] = dot_nt(ro8, k2t[128 * tap : 128 * tap + 128])
    gbuf[320:328] = rol[...]

    act0[0] = jnp.zeros((LENGTH, 128), F32)
    act0[GROUPS + 1] = jnp.zeros((LENGTH, 128), F32)
    colacc[...] = jnp.zeros((LENGTH, 128), F32)
    tacc[...] = jnp.zeros((80, 128), F32)
    ts[...] = jnp.zeros((LENGTH, 128), F32)
    arbuf[224:256] = jnp.zeros((32, 128), F32)
    column = iota((LENGTH, 128), 0) - PAD
    mk[...] = jnp.where(column + (start - HALO) < n * ROWS, column - lane_block(LENGTH), 1 << 20)

    for copy in gathers:
        copy.wait()
    for m in range(AHEAD + 2):
        for b, value in enumerate(spread(col_c if m == 1 else rbuf[m, 0:8])):
            row = 32 * (m - 1) + 8 * b + HALO + PAD
            if row >= 0 and row + 8 <= LENGTH:
                colr[row : row + 8] = value
    roww[0:8] = rbuf[0, 8:16]
    roww[8:16] = row_c
    roww[16:24] = rbuf[2, 8:16]
    wide = jnp.concatenate([tlow[...], target[...], thigh[...]], axis=0)
    wide = jnp.concatenate([wide, jnp.zeros((48, 128), F32)], axis=1)
    wide = jnp.concatenate([wide, jnp.zeros((80, 384), F32)], axis=0)
    sheared = pltpu.roll(wide, 0, 1, stride=1, stride_axis=0)
    ts[4 + PAD : 4 + PAD + 312] = sheared.T[0:312]

    def first_column(u):
        return pl.multiple_of(8 * lax.shift_right_logical(u, 1), 8)

    def mask_at(u, row, count):
        k = mk[pl.ds(row, count), :] - 4 * u
        limit = jnp.where(start + 4 * u - HALO >= 0, BAND, 0)
        return jnp.logical_and(k >= 0, k < limit)

    def clear_sides(buffer, index, base):
        buffer[index, pl.ds(base, 16), :] = jnp.zeros((16, 128), F32)
        buffer[index, pl.ds(base + PAD + SPAN, 24), :] = jnp.zeros((24, 128), F32)

    left = lane_block(WIDE) < 2

    def pieces(buffer, index, row):
        ends = jnp.where(left, buffer[index + 3, pl.ds(row, WIDE), :], buffer[index, pl.ds(row, WIDE), :])
        return ends, buffer[index + 1, pl.ds(row, WIDE), :], buffer[index + 2, pl.ds(row, WIDE), :]

    def make_field(u, carry):
        base = first_column(u)
        clear_sides(act0, u + 1, base)
        row_here = roww[pl.ds(u + 5, 1), :]
        for ch in range(3):
            row = base + PAD + CHUNK * ch
            mask = mask_at(u, row, CHUNK)
            x = jnp.where(mask, row_here + colr[pl.ds(row, CHUNK), :], 0.0)
            f0[u, pl.ds(row, CHUNK), :] = x
            act, slope = gelu_and_slope(x)
            act0[u + 1, pl.ds(row, CHUNK), :] = act
            d0[u, pl.ds(row, CHUNK), :] = jnp.where(mask, slope, 0.0)
        return carry

    lax.fori_loop(0, GROUPS, make_field, 0)

    def first_conv(v, carry):
        base = pl.multiple_of(8 * v, 8)
        for q in range(3):
            for d, piece in enumerate(pieces(act0, 2 * v, base + PAD + 2 * (q - 1))):
                lhs[:, 128 * (3 * q + d) : 128 * (3 * q + d + 1)] = piece.astype(BF16)
        res[0:WIDE] = dot(lhs[...], w1[...])
        for h in range(2):
            u = 2 * v + h
            clear_sides(act1, u, base)
            for ch in range(3):
                row = base + PAD + CHUNK * ch
                conv = res[CHUNK * ch : CHUNK * ch + CHUNK, 128 * h : 128 * h + 128]
                mask = mask_at(u, row, CHUNK)
                x = jnp.where(mask, f0[u, pl.ds(row, CHUNK), :] + conv, 0.0)
                f1[u, pl.ds(row, CHUNK), :] = x
                act, slope = gelu_and_slope(x)
                act1[u, pl.ds(row, CHUNK), :] = act
                d1[u, pl.ds(row, CHUNK), :] = jnp.where(mask, slope, 0.0)
        return carry

    lax.fori_loop(0, GROUPS // 2, first_conv, 0)

    bins = lax.shift_right_logical(iota((128, 128), 0), 5)
    ones = (bins == lane_block(128)).astype(F32).astype(BF16)

    def make_misfit(u, carry):
        base = first_column(u)
        clear_sides(mis, u, base)
        for ch in range(3):
            row = base + PAD + CHUNK * ch
            value = rol[0:1] * f1[u, pl.ds(row, CHUNK), :]
            for p in range(3):
                for q in range(3):
                    tap = 3 * p + q
                    value = value + w2[8 * tap : 8 * tap + 1] * act1[u + p - 1, pl.ds(row + 4 * (q - 1), CHUNK), :]
            res[CHUNK * ch : CHUNK * ch + CHUNK, 0:128] = value
        high, low = split(res[0:WIDE, 0:128])
        qbuf[:, 0:128] = high
        qbuf[:, 128:256] = low
        high, low = split(ts[pl.ds(base + PAD, WIDE), :])
        qbuf[:, 256:384] = high
        qbuf[:, 384:512] = low
        pick = jnp.where(iota((128, 128), 0) == 4 * u - 4 + lane_block(128), -1.0, 0.0).astype(BF16)
        res[0:WIDE, 128:256] = dot(qbuf[...], jnp.concatenate([ones, ones, pick, pick], axis=0))
        for ch in range(3):
            row = base + PAD + CHUNK * ch
            value = res[CHUNK * ch : CHUNK * ch + CHUNK, 128:256] * (1.0 / BAND)
            mis[u, pl.ds(row, CHUNK), :] = jnp.where(mask_at(u, row, CHUNK), value, 0.0)
        return carry

    lax.fori_loop(1, GROUPS - 1, make_misfit, 0)

    def make_cotangent(u, carry):
        base = first_column(u)
        clear_sides(g1, u, base)
        sums = [None] * 10
        for ch in range(3):
            row = base + PAD + CHUNK * ch
            act = act1[u, pl.ds(row, CHUNK), :]
            back = None
            for p in range(3):
                for q in range(3):
                    tap = 3 * p + q
                    m = mis[u - (p - 1), pl.ds(row - 4 * (q - 1), CHUNK), :]
                    term = w2[8 * tap : 8 * tap + 1] * m
                    back = term if back is None else back + term
                    part = fold(act * m)
                    sums[tap] = part if sums[tap] is None else sums[tap] + part
            m = mis[u, pl.ds(row, CHUNK), :]
            part = fold(m * f1[u, pl.ds(row, CHUNK), :])
            sums[9] = part if sums[9] is None else sums[9] + part
            g1[u, pl.ds(row, CHUNK), :] = rol[0:1] * m + d1[u, pl.ds(row, CHUNK), :] * back
        for tap in range(10):
            source = u - (tap // 3 - 1) if tap < 9 else u
            own = jnp.logical_and(source >= FIRST_OWN, source <= LAST_OWN)
            tacc[8 * tap : 8 * tap + 8] += jnp.where(own, sums[tap], 0.0)
        return carry

    lax.fori_loop(2, GROUPS - 2, make_cotangent, 0)

    def first_adjoint(w, carry):
        base = pl.multiple_of(8 * w + 8, 8)
        for q in range(3):
            for d, piece in enumerate(pieces(g1, 2 * w + 2, base + PAD - 2 * (q - 1))):
                high, low = split(piece)
                lanes = slice(128 * (3 * q + d), 128 * (3 * q + d + 1))
                lhs2[0:WIDE, lanes] = high
                lhs2[WIDE : 2 * WIDE, lanes] = low
        res[...] = dot(lhs2[...], wa[...])
        for h in range(2):
            u = 2 * w + 3 + h
            total_row = None
            for ch in range(3):
                at = CHUNK * ch + 8 * h
                row = base + PAD + at
                lanes = slice(128 * h, 128 * h + 128)
                back = res[at : at + CHUNK, lanes] + res[WIDE + at : WIDE + at + CHUNK, lanes]
                value = g1[u, pl.ds(row, CHUNK), :] + d0[u, pl.ds(row, CHUNK), :] * back
                colacc[pl.ds(row, CHUNK), :] += value
                part = fold(value)
                total_row = part if total_row is None else total_row + part
            rowg[pl.ds(u - 3, 1), :] = jnp.sum(total_row, axis=0, keepdims=True)
        return carry

    lax.fori_loop(0, 4, first_adjoint, 0)

    where_block = lane_block(8)
    for m in range(REACH + 1):
        packed = jnp.zeros((8, 128), F32)
        for b in range(4):
            row = 32 * m + 8 * b + HALO + PAD
            value = colacc[row : row + 8]
            value = value + pltpu.roll(value, 64, 1)
            value = value + pltpu.roll(value, 32, 1)
            packed = jnp.where(where_block == b, value, packed)
        colp[8 * m : 8 * m + 8] = packed
    columns = []
    for m in range(1, REACH + 1):
        columns.append(
            pltpu.make_async_remote_copy(
                colp.at[pl.ds(8 * m, 8)], cbuf.at[m], s1.at[m], r1.at[m], device_id=(dev(m),), device_id_type=MESH
            )
        )
    for copy in columns:
        copy.start()

    def collect(u, carry):
        base = first_column(u)
        at = pl.multiple_of(WIDE * (u - FIRST_OWN), 16)
        high, low = split(g1[u, pl.ds(base + PAD, WIDE), :])
        gall[pl.ds(at, WIDE), 0:128] = high
        gall[pl.ds(at, WIDE), 128:256] = low
        for q in range(3):
            for d in range(3):
                piece = act0[u + d, pl.ds(base + PAD + 2 * (q - 1), WIDE), :]
                xall[pl.ds(at, WIDE), 128 * (3 * q + d) : 128 * (3 * q + d + 1)] = piece.astype(BF16)
        return carry

    lax.fori_loop(FIRST_OWN, LAST_OWN + 1, collect, 0)
    fg[...] = dot_t(gall[...], xall[...])

    where_block = lane_block(32)
    for group in range(3):
        packed = jnp.zeros((32, 128), F32)
        for place in range(4):
            tap = 4 * group + place
            if tap > 8:
                continue
            p, q = tap // 3 - 1, tap % 3
            value = jnp.zeros((32, 128), F32)
            for b in range(4):
                source = b + 2 * p
                lanes = 128 * (3 * q + source // 4 + 1)
                both = fg[32 * b : 32 * b + 32, lanes : lanes + 128] + fg[128 + 32 * b : 160 + 32 * b, lanes : lanes + 128]
                value = value + jnp.where(where_block == source % 4, both, 0.0)
            value = value + pltpu.roll(value, 64, 1)
            value = value + pltpu.roll(value, 32, 1)
            packed = jnp.where(where_block == place, value, packed)
        arbuf[128 + 32 * group : 160 + 32 * group] = packed
    for tap in range(10):
        arbuf[224 + tap : 225 + tap] = jnp.sum(tacc[8 * tap : 8 * tap + 8], axis=0, keepdims=True)
    sums = arbuf[224:240]
    sums = sums + pltpu.roll(sums, 64, 1)
    arbuf[224:240] = sums + pltpu.roll(sums, 32, 1)
    high, low = split(jnp.concatenate([tacc[8 * tap : 8 * tap + 8] for tap in range(9)], axis=1))
    by_read = jnp.sum(dot(high, k2t[...]) + dot(low, k2t[...]), axis=0, keepdims=True)
    arbuf[233:234, 0:32] = arbuf[233:234, 0:32] + by_read

    where_block = lane_block(8)
    rows = rowg[...]
    for b in range(4):
        vbuf[1, pl.ds(b, 8, stride=4), :] = jnp.where(where_block == 1, pltpu.roll(rows, (32 - 32 * b) % 128, 1) if b != 1 else rows, 0.0)
    for copy in columns:
        copy.wait()
    own = colp[0:8]
    for m in range(1, REACH + 1):
        own = own + cbuf[m]
    for b in range(4):
        vbuf[0, 8 * b : 8 * b + 8] = jnp.where(where_block == 0, pltpu.roll(own, (128 - 32 * b) % 128, 1) if b else own, 0.0)
    both = vbuf[0] + vbuf[1]
    high, low = split(both)
    by_feature = dot_t(jnp.concatenate([high, low], axis=0), jnp.concatenate([feat[...]] * 2, axis=0))
    arbuf[0:64] = by_feature[0:64, 0:128]
    arbuf[64:128] = by_feature[0:64, 128:256]

    def chunk(q):
        return pl.ds(pl.multiple_of(q * PART, PART), PART)

    exchange = pltpu.make_async_remote_copy(
        arbuf.at[pl.ds(pl.multiple_of(128 * (1 - core), 128), 128)], pairbuf, s5.at[0], r5.at[0],
        device_id=(partner,), device_id_type=MESH,
    )
    exchange.start()
    weights = jnp.concatenate([col_t[...], row_t[...]], axis=0)
    by_bin = dot(high[:, 0:64], weights) + dot(low[:, 0:64], weights)
    gbuf[256:288] = by_bin[:, 0:128]
    gbuf[288:320] = by_bin[:, 128:256]
    exchange.wait()
    own_half = pl.ds(pl.multiple_of(128 * core, 128), 128)
    halfbuf[...] = arbuf[own_half, :] + pairbuf[...]

    def scatter(s):
        q = lax.rem(depth + s, LINE)
        return pltpu.make_async_remote_copy(
            halfbuf.at[chunk(q)], rsbuf.at[s], s2.at[s], r2.at[s], device_id=(in_line(q),), device_id_type=MESH
        )

    def across_copy(s):
        q = lax.rem(plane + s, side)
        return pltpu.make_async_remote_copy(
            mine, bbuf.at[plane], s3.at[s], r3.at[s], device_id=(across(q),), device_id_type=MESH
        )

    here = chunk(LINE * core + depth)

    def spread_copy(s):
        q = lax.rem(depth + s, LINE)
        return pltpu.make_async_remote_copy(
            gbuf.at[here], gbuf.at[here], s4.at[s], r4.at[s], device_id=(in_line(q),), device_id_type=MESH
        )

    def run(count, make):
        copies = [make(s) for s in range(1, count)]
        for copy in copies:
            copy.start()
        for copy in copies:
            copy.wait()

    run(LINE, scatter)
    total = halfbuf[chunk(depth), :]
    for s in range(1, LINE):
        total = total + rsbuf[s]
    mine[...] = total
    bbuf[plane] = total
    run(side, across_copy)
    total = bbuf[0]
    for q in range(1, side):
        total = total + bbuf[q]
    gbuf[here, :] = total
    run(LINE, spread_copy)
    back = pltpu.make_async_remote_copy(
        gbuf.at[own_half], gbuf.at[own_half], s5.at[1], r5.at[1], device_id=(partner,), device_id_type=MESH
    )
    back.start()
    back.wait()
    store = pltpu.make_async_copy(gbuf, red, loads.at[6])
    store.start()
    store.wait()


def finish_kernel(red_in, gfeat, grow, gcol, gone, gtwo, gread, red, sem):
    load = pltpu.make_async_copy(red_in, red, sem.at[0])
    load.start()
    load.wait()
    gfeat[:, 0:128] = red[256:288]
    gfeat[:, 128:256] = red[288:320]
    gcol[:, 0:128] = red[0:32]
    gcol[:, 128:256] = red[64:96]
    grow[:, 0:128] = red[32:64]
    grow[:, 128:256] = red[96:128]
    for group in range(3):
        block = red[128 + 32 * group : 160 + 32 * group].T
        count = 128 if group < 2 else 32
        gone[128 * group : 128 * group + count] = block[0:count]
    by_channel = red[224:240].T
    read = red[320:321, 0:32]
    for tap in range(9):
        gtwo[32 * tap : 32 * tap + 32] = by_channel[0:32, tap : tap + 1] * read
    gread[...] = red[233:234, 0:32]


def shards(n, features, row_proj, col_proj, first_filter, second_filter, readout, target):
    side = n // SIDE
    vmem = pl.BlockSpec(memory_space=pltpu.VMEM)

    def shape(*dims):
        return jax.ShapeDtypeStruct(dims, F32)

    def real(*dims):
        return pltpu.VMEM(dims, F32)

    def half(*dims):
        return pltpu.VMEM(dims, BF16)

    k1 = first_filter.reshape(9 * PAIR, PAIR)
    k2 = second_filter.reshape(9 * PAIR, PAIR)
    ro = readout.reshape(1, PAIR)
    row_t, col_t = row_proj.T, col_proj.T
    hbm = pl.BlockSpec(memory_space=pltpu.HBM)
    scratch = dict(
        feat=half(ROWS, 256), row_t=half(PAIR, 256), col_t=half(PAIR, 256), target=real(ROWS, 256), k1=half(288, PAIR), k2=half(288, PAIR),
        proj=real(32, 128), sbuf=real(16, 128), rbuf=real(AHEAD + 2, 16, 128), tlow=real(8, 256), thigh=real(8, 256),
        roww=real(24, 128), w1=half(1152, 256), wa=half(1152, 256), w2=real(72, 128), rol=real(8, 128),
        colr=real(LENGTH, 128), mk=pltpu.VMEM((LENGTH, 128), jnp.int32), ts=real(LENGTH, 128),
        act0=real(GROUPS + 2, LENGTH, 128), f0=real(GROUPS, LENGTH, 128), d0=real(GROUPS, LENGTH, 128),
        act1=real(GROUPS, LENGTH, 128), f1=real(GROUPS, LENGTH, 128), d1=real(GROUPS, LENGTH, 128),
        mis=real(GROUPS, LENGTH, 128), g1=real(GROUPS, LENGTH, 128),
        lhs=half(WIDE, 1152), lhs2=half(2 * WIDE, 1152), k2t=half(1152, PAIR), res=real(2 * WIDE, 256), qbuf=half(WIDE, 512),
        xall=half(8 * WIDE, 1152), gall=half(8 * WIDE, 256), fg=real(256, 1152), tacc=real(80, 128),
        colacc=real(LENGTH, 128), tiles=real(288, 256), colp=real(72, 128), rowg=real(8, 128),
        cbuf=real(REACH + 1, 8, 128), vbuf=real(2, 32, 128), arbuf=real(256, 128), pairbuf=real(128, 128), halfbuf=real(128, 128), rsbuf=real(LINE, PART, 128),
        bbuf=real(side, PART, 128), mine=real(PART, 128), gbuf=real(328, 128), loads=SEM((7,)),
        ss=SEM((AHEAD + 4,)), rs=SEM((AHEAD + 4,)), s1=SEM((REACH + 1,)), r1=SEM((REACH + 1,)),
        s2=SEM((LINE,)), r2=SEM((LINE,)), s3=SEM((side,)), r3=SEM((side,)), s4=SEM((LINE,)), r4=SEM((LINE,)), s5=SEM((2,)), r5=SEM((2,)),
    )
    red = pl.pallas_call(
        functools.partial(step_kernel, n),
        out_shape=shape(328, 128),
        in_specs=[hbm] * 6 + [vmem],
        out_specs=hbm,
        scratch_shapes=list(scratch.values()),
        compiler_params=pltpu.CompilerParams(
            collective_id=0, has_side_effects=True, vmem_limit_bytes=60 * 1024 * 1024
        ),
        name="step",
    )(features, row_t, col_t, target, k1, k2, ro)

    gfeat, grow, gcol, gone, gtwo, gread = pl.pallas_call(
        finish_kernel,
        out_shape=(shape(ROWS, 256), shape(32, 256), shape(32, 256), shape(288, 32), shape(288, 32), shape(1, 32)),
        in_specs=[hbm],
        out_specs=(vmem,) * 6,
        scratch_shapes=[real(328, 128), SEM((1,))],
        name="finish",
    )(red)
    return gfeat, grow.T, gcol.T, gone.reshape(3, 3, PAIR, PAIR), gtwo.reshape(3, 3, PAIR, PAIR), gread.reshape(PAIR)


def solution(mesh):
    n = mesh.shape["diag"]
    in_specs = (P("diag", None), P(), P(), P(), P(), P(), P("diag", None))
    out_specs = (P("diag", None), P(), P(), P(), P(), P())
    return jax.shard_map(
        functools.partial(shards, n), mesh=mesh, in_specs=in_specs, out_specs=out_specs, check_vma=False
    )
```

```python
import functools
import math

import jax
import jax.numpy as jnp
from jax import lax
from jax.experimental import pallas as pl
from jax.experimental.pallas import tpu as pltpu
from jax.sharding import PartitionSpec as P

MESH = pl.DeviceIdType.MESH
F32, BF16 = jnp.float32, jnp.bfloat16

ROWS = 32
BAND = 256
PAIR = 32
HALO = 12
GROUPS = (ROWS + 2 * HALO) // 4
FIRST_OWN, LAST_OWN = 3, 10
PAD = 16
LENGTH = 352
WIDE, SPAN, CHUNK = 272, 264, 88
AHEAD = 9
REACH = 8
C0 = math.sqrt(2.0 / math.pi)
C1 = C0 * 0.044715
SIDE = 16
LINE = 8
PART = 16
SEM = pltpu.SemaphoreType.DMA


def iota(shape, dim):
    return lax.broadcasted_iota(jnp.int32, shape, dim)


def lane_block(rows):
    return lax.shift_right_logical(iota((rows, 128), 1), 5)


def gelu(x, with_slope):
    cubic = C1 * (x * x)
    s = 0.5 * jnp.tanh(x * (cubic + C0)) + 0.5
    value = x * s
    slope = s + value * (1.0 - s) * (6.0 * cubic + 2.0 * C0) if with_slope else None
    return value.astype(BF16).astype(F32), slope


def split(x):
    high = x.astype(BF16)
    return high, (x - high.astype(F32)).astype(BF16)


def fold(x):
    total = x[0:8]
    for i in range(1, x.shape[0] // 8):
        total = total + x[8 * i : 8 * i + 8]
    return total


def dot(a, b):
    return jnp.dot(a, b, preferred_element_type=F32)


def dot_t(a, b):
    return lax.dot_general(a, b, (((0,), (0,)), ((), ())), preferred_element_type=F32)


def dot_nt(a, b):
    return lax.dot_general(a, b, (((1,), (1,)), ((), ())), preferred_element_type=F32)


def repeater(lanes):
    return (jnp.bitwise_and(iota((PAIR, lanes), 1), 31) == iota((PAIR, lanes), 0)).astype(F32).astype(BF16)


def spread(block):
    turned = [block] + [pltpu.roll(block, 32 * s, 1) for s in (1, 2, 3)]
    where_block = lane_block(8)
    outs = []
    for b in range(4):
        value = turned[(3 - b) % 4]
        for other in range(3):
            value = jnp.where(where_block == other, turned[(other - b) % 4], value)
        outs.append(value)
    return outs


def step_kernel(
    n, feat_in, row_in, col_in, target_in, k1_in, k2_in, ro, red,
    feat, row_t, col_t, target, k1, k2,
    proj, sbuf, rbuf, tlow, thigh, roww, w1, wa, w2, rol, colr, mk, ts, act0, d0, act1, f1, d1, mis, g1,
    lhs, lhs2, k2t, res, qbuf, xall, gall, fg, tacc, colacc, tiles, colp, rowg, cbuf, vbuf, arbuf, pairbuf, halfbuf, rsbuf, bbuf, mine, gbuf,
    loads, ss, rs, s1, r1, s2, r2, s3, r3, s4, r4, s5, r5,
):
    me = lax.axis_index("diag")
    start = me * ROWS
    side = n // SIDE
    pos = lax.rem(me, SIDE)
    core = lax.rem(me, 2)
    depth = lax.div(pos, 2)
    plane = lax.div(me, SIDE)
    partner = me + 1 - 2 * core

    def dev(step):
        return lax.rem(me + step + n, n)

    def in_line(q):
        return me + 2 * (q - depth)

    def across(q):
        return q * SIDE + pos

    fetches = [
        pltpu.make_async_copy(source, place, loads.at[i])
        for i, (source, place) in enumerate(
            ((feat_in, feat), (row_in, row_t), (col_in, col_t), (k1_in, k1), (k2_in, k2), (target_in, target))
        )
    ]
    for fetch in fetches:
        fetch.start()

    barrier = pltpu.get_barrier_semaphore()
    for step in (-1,) + tuple(range(1, AHEAD + 1)) + tuple(range(-REACH, 0)):
        pl.semaphore_signal(barrier, inc=1, device_id=(dev(step),), device_id_type=MESH)

    def greet(s, carry):
        pl.semaphore_signal(barrier, inc=1, device_id=(in_line(lax.rem(depth + s, LINE)),), device_id_type=MESH)
        return carry

    lax.fori_loop(1, LINE, greet, 0)
    pl.semaphore_signal(barrier, inc=1, device_id=(partner,), device_id_type=MESH)

    def greet_across(s, carry):
        pl.semaphore_signal(barrier, inc=1, device_id=(across(lax.rem(plane + s, side)),), device_id_type=MESH)
        return carry

    lax.fori_loop(1, side, greet_across, 0)

    for fetch in fetches[0:3]:
        fetch.wait()
    proj[...] = dot_nt(feat[...], jnp.concatenate([row_t[...]] * 4, axis=0))
    cc = dot_nt(feat[...], jnp.concatenate([col_t[...]] * 4, axis=0))
    where_block = lane_block(8)
    row_c = jnp.zeros((8, 128), F32)
    col_c = jnp.zeros((8, 128), F32)
    for b in range(4):
        row_c = jnp.where(where_block == b, proj[pl.ds(b, 8, stride=4), :], row_c)
        col_c = jnp.where(where_block == b, cc[8 * b : 8 * b + 8], col_c)
    sbuf[0:8] = col_c
    sbuf[8:16] = row_c
    pl.semaphore_wait(barrier, AHEAD + 1 + REACH + LINE + side - 1)
    gathers = []
    for slot, step in ((0, 1), (2, -1)):
        gathers.append(
            pltpu.make_async_remote_copy(sbuf, rbuf.at[slot], ss.at[slot], rs.at[slot], device_id=(dev(step),), device_id_type=MESH)
        )
    for m in range(3, AHEAD + 2):
        gathers.append(
            pltpu.make_async_remote_copy(
                sbuf.at[pl.ds(0, 8)], rbuf.at[m, pl.ds(0, 8)], ss.at[m], rs.at[m], device_id=(dev(1 - m),), device_id_type=MESH
            )
        )
    gathers.append(
        pltpu.make_async_remote_copy(
            target_in.at[pl.ds(24, 8)], tlow, ss.at[AHEAD + 2], rs.at[AHEAD + 2], device_id=(dev(1),), device_id_type=MESH
        )
    )
    gathers.append(
        pltpu.make_async_remote_copy(
            target_in.at[pl.ds(0, 8)], thigh, ss.at[AHEAD + 3], rs.at[AHEAD + 3], device_id=(dev(-1),), device_id_type=MESH
        )
    )
    for copy in gathers:
        copy.start()

    for fetch in fetches[3:6]:
        fetch.wait()
    rep8 = repeater(256)
    where_out = lax.shift_right_logical(iota((PAIR, 256), 1), 5)

    def build(weights, sign):
        for q in range(3):
            for place, ri in enumerate((8, 9, -2, -1, 0, 1, 2, 3, 4, 5, 6, 7)):
                value = jnp.zeros((PAIR, 256), F32)
                for p in range(3):
                    tap = 3 * p + q
                    ro_here = ri - sign * 2 * (p - 1)
                    if 0 <= ro_here < 8:
                        value = jnp.where(where_out == ro_here, tiles[32 * tap : 32 * tap + 32], value)
                row = (q * 12 + place) * 32
                weights[row : row + 32] = value.astype(BF16)

    tiles[...] = dot(k1[...], rep8)
    build(w1, 1)
    for tap in range(9):
        tiles[32 * tap : 32 * tap + 32] = dot_t(k1[32 * tap : 32 * tap + 32], rep8)
    build(wa, -1)
    ro8 = jnp.broadcast_to(ro[...].astype(F32), (8, PAIR)).astype(BF16)
    rol[...] = dot(ro8, repeater(128))
    for tap in range(9):
        for b in range(4):
            row = 128 * tap + 32 * b
            k2t[row : row + 32] = k2[32 * tap : 32 * tap + 32]
        w2[8 * tap : 8 * tap + 8] = dot_nt(ro8, k2t[128 * tap : 128 * tap + 128])
    gbuf[320:328] = rol[...]

    act0[0] = jnp.zeros((LENGTH, 128), F32)
    act0[GROUPS + 1] = jnp.zeros((LENGTH, 128), F32)
    colacc[...] = jnp.zeros((LENGTH, 128), F32)
    tacc[...] = jnp.zeros((80, 128), F32)
    ts[...] = jnp.zeros((LENGTH, 128), F32)
    arbuf[224:256] = jnp.zeros((32, 128), F32)
    column = iota((LENGTH, 128), 0) - PAD
    mk[...] = jnp.where(column + (start - HALO) < n * ROWS, column - lane_block(LENGTH), 1 << 20)

    for copy in gathers:
        copy.wait_recv()
    for m in range(AHEAD + 2):
        for b, value in enumerate(spread(col_c if m == 1 else rbuf[m, 0:8])):
            row = 32 * (m - 1) + 8 * b + HALO + PAD
            if row >= 0 and row + 8 <= LENGTH:
                colr[row : row + 8] = value
    roww[0:8] = rbuf[0, 8:16]
    roww[8:16] = row_c
    roww[16:24] = rbuf[2, 8:16]
    wide = jnp.concatenate([tlow[...], target[...], thigh[...]], axis=0)
    wide = jnp.concatenate([wide, jnp.zeros((48, 128), F32)], axis=1)
    wide = jnp.concatenate([wide, jnp.zeros((80, 384), F32)], axis=0)
    sheared = pltpu.roll(wide, 0, 1, stride=1, stride_axis=0)
    ts[4 + PAD : 4 + PAD + 312] = sheared.T[0:312]

    def first_column(u):
        return pl.multiple_of(8 * lax.shift_right_logical(u, 1), 8)

    def mask_at(u, row, count):
        shift = 4 * u - jnp.where(start + 4 * u - HALO >= 0, 0, 1 << 20)
        return jnp.bitwise_and(mk[pl.ds(row, count), :] - shift, -BAND) == 0

    def clear_sides(buffer, index, base):
        buffer[index, pl.ds(base, 16), :] = jnp.zeros((16, 128), F32)
        buffer[index, pl.ds(base + PAD + SPAN, 24), :] = jnp.zeros((24, 128), F32)

    left = lane_block(WIDE) < 2

    def pieces(buffer, index, row):
        ends = jnp.where(left, buffer[index + 3, pl.ds(row, WIDE), :], buffer[index, pl.ds(row, WIDE), :])
        return ends, buffer[index + 1, pl.ds(row, WIDE), :], buffer[index + 2, pl.ds(row, WIDE), :]

    def make_field(with_slope, u, carry):
        base = first_column(u)
        clear_sides(act0, u + 1, base)
        row_here = roww[pl.ds(u + 5, 1), :]
        for ch in range(3):
            row = base + PAD + CHUNK * ch
            mask = mask_at(u, row, CHUNK)
            x = jnp.where(mask, row_here + colr[pl.ds(row, CHUNK), :], 0.0)
            act, slope = gelu(x, with_slope)
            act0[u + 1, pl.ds(row, CHUNK), :] = act
            if with_slope:
                d0[u, pl.ds(row, CHUNK), :] = jnp.where(mask, slope, 0.0)
        return carry

    for begin, end, with_slope in ((0, 3, False), (3, 11, True), (11, 14, False)):
        lax.fori_loop(begin, end, functools.partial(make_field, with_slope), 0)

    def first_conv(with_slope, v, carry):
        base = pl.multiple_of(8 * v, 8)
        for q in range(3):
            for d, piece in enumerate(pieces(act0, 2 * v, base + PAD + 2 * (q - 1))):
                lhs[:, 128 * (3 * q + d) : 128 * (3 * q + d + 1)] = piece.astype(BF16)
        res[0:WIDE] = dot(lhs[...], w1[...])
        for h in range(2):
            u = 2 * v + h
            clear_sides(act1, u, base)
            row_here = roww[pl.ds(u + 5, 1), :]
            for ch in range(3):
                row = base + PAD + CHUNK * ch
                conv = res[CHUNK * ch : CHUNK * ch + CHUNK, 128 * h : 128 * h + 128]
                mask = mask_at(u, row, CHUNK)
                x = jnp.where(mask, (row_here + colr[pl.ds(row, CHUNK), :]) + conv, 0.0)
                act, slope = gelu(x, with_slope)
                act1[u, pl.ds(row, CHUNK), :] = act
                f1[u, pl.ds(row, CHUNK), :] = x
                if with_slope:
                    d1[u, pl.ds(row, CHUNK), :] = jnp.where(mask, slope, 0.0)
        return carry

    for begin, end, with_slope in ((0, 1, False), (1, 6, True), (6, 7, False)):
        lax.fori_loop(begin, end, functools.partial(first_conv, with_slope), 0)

    bins = lax.shift_right_logical(iota((128, 128), 0), 5)
    ones = (bins == lane_block(128)).astype(F32).astype(BF16)

    def make_misfit(u, carry):
        base = first_column(u)
        clear_sides(mis, u, base)
        for at, count in ((0, 96), (96, 96), (192, 80)):
            row = base + PAD + at
            value = rol[0:1] * f1[u, pl.ds(row, count), :]
            for p in range(3):
                for q in range(3):
                    tap = 3 * p + q
                    value = value + w2[8 * tap : 8 * tap + 1] * act1[u + p - 1, pl.ds(row + 4 * (q - 1), count), :]
            high, low = split(value)
            qbuf[at : at + count, 0:128] = high
            qbuf[at : at + count, 128:256] = low
            high, low = split(ts[pl.ds(row, count), :])
            qbuf[at : at + count, 256:384] = high
            qbuf[at : at + count, 384:512] = low
        pick = jnp.where(iota((128, 128), 0) == 4 * u - 4 + lane_block(128), -1.0, 0.0).astype(BF16)
        value = dot(qbuf[...], jnp.concatenate([ones, ones, pick, pick], axis=0)) * (1.0 / BAND)
        for at in range(0, SPAN, CHUNK):
            row = base + PAD + at
            mis[u, pl.ds(row, CHUNK), :] = jnp.where(mask_at(u, row, CHUNK), value[at : at + CHUNK], 0.0)
        return carry

    lax.fori_loop(1, GROUPS - 1, make_misfit, 0)

    def make_cotangent(u, carry):
        base = first_column(u)
        clear_sides(g1, u, base)
        sums = [None] * 10
        for ch in range(3):
            row = base + PAD + CHUNK * ch
            act = act1[u, pl.ds(row, CHUNK), :]
            back = None
            for p in range(3):
                for q in range(3):
                    tap = 3 * p + q
                    m = mis[u - (p - 1), pl.ds(row - 4 * (q - 1), CHUNK), :]
                    term = w2[8 * tap : 8 * tap + 1] * m
                    back = term if back is None else back + term
                    part = fold(act * m)
                    sums[tap] = part if sums[tap] is None else sums[tap] + part
            m = mis[u, pl.ds(row, CHUNK), :]
            part = fold(m * f1[u, pl.ds(row, CHUNK), :])
            sums[9] = part if sums[9] is None else sums[9] + part
            g1[u, pl.ds(row, CHUNK), :] = rol[0:1] * m + d1[u, pl.ds(row, CHUNK), :] * back
        for tap in range(10):
            source = u - (tap // 3 - 1) if tap < 9 else u
            own = jnp.logical_and(source >= FIRST_OWN, source <= LAST_OWN)
            tacc[8 * tap : 8 * tap + 8] += jnp.where(own, sums[tap], 0.0)
        return carry

    lax.fori_loop(2, GROUPS - 2, make_cotangent, 0)

    def first_adjoint(w, carry):
        base = pl.multiple_of(8 * w + 8, 8)
        for q in range(3):
            for d, piece in enumerate(pieces(g1, 2 * w + 2, base + PAD - 2 * (q - 1))):
                high, low = split(piece)
                lanes = slice(128 * (3 * q + d), 128 * (3 * q + d + 1))
                lhs2[0:WIDE, lanes] = high
                lhs2[WIDE : 2 * WIDE, lanes] = low
        res[...] = dot(lhs2[...], wa[...])
        for h in range(2):
            u = 2 * w + 3 + h
            total_row = None
            for ch in range(3):
                at = CHUNK * ch + 8 * h
                row = base + PAD + at
                lanes = slice(128 * h, 128 * h + 128)
                back = res[at : at + CHUNK, lanes] + res[WIDE + at : WIDE + at + CHUNK, lanes]
                value = g1[u, pl.ds(row, CHUNK), :] + d0[u, pl.ds(row, CHUNK), :] * back
                colacc[pl.ds(row, CHUNK), :] += value
                part = fold(value)
                total_row = part if total_row is None else total_row + part
            rowg[pl.ds(u - 3, 1), :] = jnp.sum(total_row, axis=0, keepdims=True)
        return carry

    lax.fori_loop(0, 4, first_adjoint, 0)

    where_block = lane_block(8)
    for m in range(REACH + 1):
        packed = jnp.zeros((8, 128), F32)
        for b in range(4):
            row = 32 * m + 8 * b + HALO + PAD
            value = colacc[row : row + 8]
            value = value + pltpu.roll(value, 64, 1)
            value = value + pltpu.roll(value, 32, 1)
            packed = jnp.where(where_block == b, value, packed)
        colp[8 * m : 8 * m + 8] = packed
    columns = []
    for m in range(1, REACH + 1):
        columns.append(
            pltpu.make_async_remote_copy(
                colp.at[pl.ds(8 * m, 8)], cbuf.at[m], s1.at[m], r1.at[m], device_id=(dev(m),), device_id_type=MESH
            )
        )
    for copy in columns:
        copy.start()

    def collect(u, carry):
        base = first_column(u)
        at = pl.multiple_of(WIDE * (u - FIRST_OWN), 16)
        high, low = split(g1[u, pl.ds(base + PAD, WIDE), :])
        gall[pl.ds(at, WIDE), 0:128] = high
        gall[pl.ds(at, WIDE), 128:256] = low
        for q in range(3):
            for d in range(3):
                piece = act0[u + d, pl.ds(base + PAD + 2 * (q - 1), WIDE), :]
                xall[pl.ds(at, WIDE), 128 * (3 * q + d) : 128 * (3 * q + d + 1)] = piece.astype(BF16)
        return carry

    lax.fori_loop(FIRST_OWN, LAST_OWN + 1, collect, 0)
    fg[...] = dot_t(gall[...], xall[...])

    where_block = lane_block(32)
    for group in range(3):
        packed = jnp.zeros((32, 128), F32)
        for place in range(4):
            tap = 4 * group + place
            if tap > 8:
                continue
            p, q = tap // 3 - 1, tap % 3
            value = jnp.zeros((32, 128), F32)
            for b in range(4):
                source = b + 2 * p
                lanes = 128 * (3 * q + source // 4 + 1)
                both = fg[32 * b : 32 * b + 32, lanes : lanes + 128] + fg[128 + 32 * b : 160 + 32 * b, lanes : lanes + 128]
                value = value + jnp.where(where_block == source % 4, both, 0.0)
            value = value + pltpu.roll(value, 64, 1)
            value = value + pltpu.roll(value, 32, 1)
            packed = jnp.where(where_block == place, value, packed)
        arbuf[128 + 32 * group : 160 + 32 * group] = packed
    for tap in range(10):
        arbuf[224 + tap : 225 + tap] = jnp.sum(tacc[8 * tap : 8 * tap + 8], axis=0, keepdims=True)
    sums = arbuf[224:240]
    sums = sums + pltpu.roll(sums, 64, 1)
    arbuf[224:240] = sums + pltpu.roll(sums, 32, 1)
    high, low = split(jnp.concatenate([tacc[8 * tap : 8 * tap + 8] for tap in range(9)], axis=1))
    by_read = jnp.sum(dot(high, k2t[...]) + dot(low, k2t[...]), axis=0, keepdims=True)
    arbuf[233:234, 0:32] = arbuf[233:234, 0:32] + by_read

    where_block = lane_block(8)
    rows = rowg[...]
    for b in range(4):
        vbuf[1, pl.ds(b, 8, stride=4), :] = jnp.where(where_block == 1, pltpu.roll(rows, (32 - 32 * b) % 128, 1) if b != 1 else rows, 0.0)
    for copy in gathers:
        copy.wait_send()
    for copy in columns:
        copy.wait_recv()
    own = colp[0:8]
    for m in range(1, REACH + 1):
        own = own + cbuf[m]
    for b in range(4):
        vbuf[0, 8 * b : 8 * b + 8] = jnp.where(where_block == 0, pltpu.roll(own, (128 - 32 * b) % 128, 1) if b else own, 0.0)
    both = vbuf[0] + vbuf[1]
    high, low = split(both)
    by_feature = dot_t(jnp.concatenate([high, low], axis=0), jnp.concatenate([feat[...]] * 2, axis=0))
    arbuf[0:64] = by_feature[0:64, 0:128]
    arbuf[64:128] = by_feature[0:64, 128:256]

    def chunk(q):
        return pl.ds(pl.multiple_of(q * PART, PART), PART)

    exchange = pltpu.make_async_remote_copy(
        arbuf.at[pl.ds(pl.multiple_of(128 * (1 - core), 128), 128)], pairbuf, s5.at[0], r5.at[0],
        device_id=(partner,), device_id_type=MESH,
    )
    exchange.start()
    weights = jnp.concatenate([col_t[...], row_t[...]], axis=0)
    by_bin = dot(high[:, 0:64], weights) + dot(low[:, 0:64], weights)
    gbuf[256:288] = by_bin[:, 0:128]
    gbuf[288:320] = by_bin[:, 128:256]
    exchange.wait()
    own_half = pl.ds(pl.multiple_of(128 * core, 128), 128)
    halfbuf[...] = arbuf[own_half, :] + pairbuf[...]

    def scatter(s):
        q = lax.rem(depth + s, LINE)
        return pltpu.make_async_remote_copy(
            halfbuf.at[chunk(q)], rsbuf.at[s], s2.at[s], r2.at[s], device_id=(in_line(q),), device_id_type=MESH
        )

    def across_copy(s):
        q = lax.rem(plane + s, side)
        return pltpu.make_async_remote_copy(
            mine, bbuf.at[plane], s3.at[s], r3.at[s], device_id=(across(q),), device_id_type=MESH
        )

    here = chunk(LINE * core + depth)

    def spread_copy(s):
        q = lax.rem(depth + s, LINE)
        return pltpu.make_async_remote_copy(
            gbuf.at[here], gbuf.at[here], s4.at[s], r4.at[s], device_id=(in_line(q),), device_id_type=MESH
        )

    def run(count, make):
        copies = [make(s) for s in range(1, count)]
        for copy in copies:
            copy.start()
        for copy in sent:
            copy.wait_send()
        sent[:] = copies
        for copy in copies:
            copy.wait_recv()

    sent = columns
    run(LINE, scatter)
    total = halfbuf[chunk(depth), :]
    for s in range(1, LINE):
        total = total + rsbuf[s]
    mine[...] = total
    bbuf[plane] = total
    run(side, across_copy)
    total = bbuf[0]
    for q in range(1, side):
        total = total + bbuf[q]
    gbuf[here, :] = total
    run(LINE, spread_copy)
    back = pltpu.make_async_remote_copy(
        gbuf.at[own_half], gbuf.at[own_half], s5.at[1], r5.at[1], device_id=(partner,), device_id_type=MESH
    )
    back.start()
    for copy in sent:
        copy.wait_send()
    back.wait()
    red[...] = gbuf[...]


def finish_kernel(red, gfeat, grow, gcol, gone, gtwo, gread):
    gfeat[:, 0:128] = red[256:288]
    gfeat[:, 128:256] = red[288:320]
    gcol[:, 0:128] = red[0:32]
    gcol[:, 128:256] = red[64:96]
    grow[:, 0:128] = red[32:64]
    grow[:, 128:256] = red[96:128]
    for group in range(3):
        block = red[128 + 32 * group : 160 + 32 * group].T
        count = 128 if group < 2 else 32
        gone[128 * group : 128 * group + count] = block[0:count]
    by_channel = red[224:240].T
    read = red[320:321, 0:32]
    for tap in range(9):
        gtwo[32 * tap : 32 * tap + 32] = by_channel[0:32, tap : tap + 1] * read
    gread[...] = red[233:234, 0:32]


def shards(n, features, row_proj, col_proj, first_filter, second_filter, readout, target):
    side = n // SIDE
    vmem = pl.BlockSpec(memory_space=pltpu.VMEM)

    def shape(*dims):
        return jax.ShapeDtypeStruct(dims, F32)

    def real(*dims):
        return pltpu.VMEM(dims, F32)

    def half(*dims):
        return pltpu.VMEM(dims, BF16)

    k1 = first_filter.reshape(9 * PAIR, PAIR)
    k2 = second_filter.reshape(9 * PAIR, PAIR)
    ro = readout.reshape(1, PAIR)
    row_t, col_t = row_proj.T, col_proj.T
    hbm = pl.BlockSpec(memory_space=pltpu.HBM)
    scratch = dict(
        feat=half(ROWS, 256), row_t=half(PAIR, 256), col_t=half(PAIR, 256), target=real(ROWS, 256), k1=half(288, PAIR), k2=half(288, PAIR),
        proj=real(32, 128), sbuf=real(16, 128), rbuf=real(AHEAD + 2, 16, 128), tlow=real(8, 256), thigh=real(8, 256),
        roww=real(24, 128), w1=half(1152, 256), wa=half(1152, 256), w2=real(72, 128), rol=real(8, 128),
        colr=real(LENGTH, 128), mk=pltpu.VMEM((LENGTH, 128), jnp.int32), ts=real(LENGTH, 128),
        act0=real(GROUPS + 2, LENGTH, 128), d0=real(GROUPS, LENGTH, 128),
        act1=real(GROUPS, LENGTH, 128), f1=real(GROUPS, LENGTH, 128), d1=real(GROUPS, LENGTH, 128),
        mis=real(GROUPS, LENGTH, 128), g1=real(GROUPS, LENGTH, 128),
        lhs=half(WIDE, 1152), lhs2=half(2 * WIDE, 1152), k2t=half(1152, PAIR), res=real(2 * WIDE, 256), qbuf=half(WIDE, 512),
        xall=half(8 * WIDE, 1152), gall=half(8 * WIDE, 256), fg=real(256, 1152), tacc=real(80, 128),
        colacc=real(LENGTH, 128), tiles=real(288, 256), colp=real(72, 128), rowg=real(8, 128),
        cbuf=real(REACH + 1, 8, 128), vbuf=real(2, 32, 128), arbuf=real(256, 128), pairbuf=real(128, 128), halfbuf=real(128, 128), rsbuf=real(LINE, PART, 128),
        bbuf=real(side, PART, 128), mine=real(PART, 128), gbuf=real(328, 128), loads=SEM((6,)),
        ss=SEM((AHEAD + 4,)), rs=SEM((AHEAD + 4,)), s1=SEM((REACH + 1,)), r1=SEM((REACH + 1,)),
        s2=SEM((LINE,)), r2=SEM((LINE,)), s3=SEM((side,)), r3=SEM((side,)), s4=SEM((LINE,)), r4=SEM((LINE,)), s5=SEM((2,)), r5=SEM((2,)),
    )
    red = pl.pallas_call(
        functools.partial(step_kernel, n),
        out_shape=shape(328, 128),
        in_specs=[hbm] * 6 + [vmem],
        out_specs=vmem,
        scratch_shapes=list(scratch.values()),
        compiler_params=pltpu.CompilerParams(
            collective_id=0, has_side_effects=True, vmem_limit_bytes=44 * 1024 * 1024
        ),
        name="step",
    )(features, row_t, col_t, target, k1, k2, ro)

    gfeat, grow, gcol, gone, gtwo, gread = pl.pallas_call(
        finish_kernel,
        out_shape=(shape(ROWS, 256), shape(32, 256), shape(32, 256), shape(288, 32), shape(288, 32), shape(1, 32)),
        in_specs=[vmem],
        out_specs=(vmem,) * 6,
        compiler_params=pltpu.CompilerParams(vmem_limit_bytes=4 * 1024 * 1024),
        name="finish",
    )(red)
    return gfeat, grow.T, gcol.T, gone.reshape(3, 3, PAIR, PAIR), gtwo.reshape(3, 3, PAIR, PAIR), gread.reshape(PAIR)


def solution(mesh):
    n = mesh.shape["diag"]
    in_specs = (P("diag", None), P(), P(), P(), P(), P(), P("diag", None))
    out_specs = (P("diag", None), P(), P(), P(), P(), P())
    return jax.shard_map(
        functools.partial(shards, n), mesh=mesh, in_specs=in_specs, out_specs=out_specs, check_vma=False
    )
```

```python
import functools
import math

import jax
import jax.numpy as jnp
from jax import lax
from jax.experimental import pallas as pl
from jax.experimental.pallas import tpu as pltpu
from jax.sharding import PartitionSpec as P

MESH = pl.DeviceIdType.MESH
F32, BF16 = jnp.float32, jnp.bfloat16

ROWS = 32
BAND = 256
PAIR = 32
HALO = 12
GROUPS = (ROWS + 2 * HALO) // 4
FIRST_OWN, LAST_OWN = 3, 10
PAD = 16
LENGTH = 352
WIDE, SPAN, CHUNK = 272, 264, 88
AHEAD = 9
REACH = 8
C0 = math.sqrt(2.0 / math.pi)
C1 = C0 * 0.044715
SIDE = 16
LINE = 8
PART = 16
SEM = pltpu.SemaphoreType.DMA


def iota(shape, dim):
    return lax.broadcasted_iota(jnp.int32, shape, dim)


def lane_block(rows):
    return lax.shift_right_logical(iota((rows, 128), 1), 5)


def gelu(x, with_slope):
    cubic = C1 * (x * x)
    s = 0.5 * jnp.tanh(x * (cubic + C0)) + 0.5
    value = x * s
    slope = s + value * (1.0 - s) * (6.0 * cubic + 2.0 * C0) if with_slope else None
    return value.astype(BF16).astype(F32), slope


def split(x):
    high = x.astype(BF16)
    return high, (x - high.astype(F32)).astype(BF16)


def fold(x):
    total = x[0:8]
    for i in range(1, x.shape[0] // 8):
        total = total + x[8 * i : 8 * i + 8]
    return total


def dot(a, b):
    return jnp.dot(a, b, preferred_element_type=F32)


def dot_t(a, b):
    return lax.dot_general(a, b, (((0,), (0,)), ((), ())), preferred_element_type=F32)


def dot_nt(a, b):
    return lax.dot_general(a, b, (((1,), (1,)), ((), ())), preferred_element_type=F32)


def repeater(lanes):
    return (jnp.bitwise_and(iota((PAIR, lanes), 1), 31) == iota((PAIR, lanes), 0)).astype(F32).astype(BF16)


def spread(block):
    turned = [block] + [pltpu.roll(block, 32 * s, 1) for s in (1, 2, 3)]
    where_block = lane_block(8)
    outs = []
    for b in range(4):
        value = turned[(3 - b) % 4]
        for other in range(3):
            value = jnp.where(where_block == other, turned[(other - b) % 4], value)
        outs.append(value)
    return outs


def step_kernel(
    n, feat_in, row_in, col_in, target_in, k1_in, k2_in, ro, arbuf, extra,
    feat, row_t, col_t, target, k1, k2,
    proj, sbuf, rbuf, tlow, thigh, roww, w1, wa, w2, rol, colr, mk, ts, act0, d0, act1, f1, d1, mis, g1,
    lhs, lhs2, k2t, res, qbuf, xall, gall, fg, tacc, colacc, tiles, colp, rowg, cbuf, vbuf,
    loads, ss, rs, s1, r1,
):
    me = lax.axis_index("diag")
    start = me * ROWS

    def dev(step):
        return lax.rem(me + step + n, n)

    fetches = [
        pltpu.make_async_copy(source, place, loads.at[i])
        for i, (source, place) in enumerate(
            ((feat_in, feat), (row_in, row_t), (col_in, col_t), (k1_in, k1), (k2_in, k2), (target_in, target))
        )
    ]
    for fetch in fetches:
        fetch.start()

    barrier = pltpu.get_barrier_semaphore()
    for step in (-1,) + tuple(range(1, AHEAD + 1)) + tuple(range(-REACH, 0)):
        pl.semaphore_signal(barrier, inc=1, device_id=(dev(step),), device_id_type=MESH)

    for fetch in fetches[0:3]:
        fetch.wait()
    proj[...] = dot_nt(feat[...], jnp.concatenate([row_t[...]] * 4, axis=0))
    cc = dot_nt(feat[...], jnp.concatenate([col_t[...]] * 4, axis=0))
    where_block = lane_block(8)
    row_c = jnp.zeros((8, 128), F32)
    col_c = jnp.zeros((8, 128), F32)
    for b in range(4):
        row_c = jnp.where(where_block == b, proj[pl.ds(b, 8, stride=4), :], row_c)
        col_c = jnp.where(where_block == b, cc[8 * b : 8 * b + 8], col_c)
    sbuf[0:8] = col_c
    sbuf[8:16] = row_c
    pl.semaphore_wait(barrier, AHEAD + 1 + REACH)
    gathers = []
    for slot, step in ((0, 1), (2, -1)):
        gathers.append(
            pltpu.make_async_remote_copy(sbuf, rbuf.at[slot], ss.at[slot], rs.at[slot], device_id=(dev(step),), device_id_type=MESH)
        )
    for m in range(3, AHEAD + 2):
        gathers.append(
            pltpu.make_async_remote_copy(
                sbuf.at[pl.ds(0, 8)], rbuf.at[m, pl.ds(0, 8)], ss.at[m], rs.at[m], device_id=(dev(1 - m),), device_id_type=MESH
            )
        )
    gathers.append(
        pltpu.make_async_remote_copy(
            target_in.at[pl.ds(24, 8)], tlow, ss.at[AHEAD + 2], rs.at[AHEAD + 2], device_id=(dev(1),), device_id_type=MESH
        )
    )
    gathers.append(
        pltpu.make_async_remote_copy(
            target_in.at[pl.ds(0, 8)], thigh, ss.at[AHEAD + 3], rs.at[AHEAD + 3], device_id=(dev(-1),), device_id_type=MESH
        )
    )
    for copy in gathers:
        copy.start()

    for fetch in fetches[3:6]:
        fetch.wait()
    rep8 = repeater(256)
    where_out = lax.shift_right_logical(iota((PAIR, 256), 1), 5)

    def build(weights, sign):
        for q in range(3):
            for place, ri in enumerate((8, 9, -2, -1, 0, 1, 2, 3, 4, 5, 6, 7)):
                value = jnp.zeros((PAIR, 256), F32)
                for p in range(3):
                    tap = 3 * p + q
                    ro_here = ri - sign * 2 * (p - 1)
                    if 0 <= ro_here < 8:
                        value = jnp.where(where_out == ro_here, tiles[32 * tap : 32 * tap + 32], value)
                row = (q * 12 + place) * 32
                weights[row : row + 32] = value.astype(BF16)

    tiles[...] = dot(k1[...], rep8)
    build(w1, 1)
    for tap in range(9):
        tiles[32 * tap : 32 * tap + 32] = dot_t(k1[32 * tap : 32 * tap + 32], rep8)
    build(wa, -1)
    ro8 = jnp.broadcast_to(ro[...].astype(F32), (8, PAIR)).astype(BF16)
    rol[...] = dot(ro8, repeater(128))
    for tap in range(9):
        for b in range(4):
            row = 128 * tap + 32 * b
            k2t[row : row + 32] = k2[32 * tap : 32 * tap + 32]
        w2[8 * tap : 8 * tap + 8] = dot_nt(ro8, k2t[128 * tap : 128 * tap + 128])
    extra[64:72] = rol[...]

    act0[0] = jnp.zeros((LENGTH, 128), F32)
    act0[GROUPS + 1] = jnp.zeros((LENGTH, 128), F32)
    colacc[...] = jnp.zeros((LENGTH, 128), F32)
    tacc[...] = jnp.zeros((80, 128), F32)
    ts[...] = jnp.zeros((LENGTH, 128), F32)
    arbuf[224:256] = jnp.zeros((32, 128), F32)
    column = iota((LENGTH, 128), 0) - PAD
    mk[...] = jnp.where(column + (start - HALO) < n * ROWS, column - lane_block(LENGTH), 1 << 20)

    for copy in gathers:
        copy.wait_recv()
    for m in range(AHEAD + 2):
        for b, value in enumerate(spread(col_c if m == 1 else rbuf[m, 0:8])):
            row = 32 * (m - 1) + 8 * b + HALO + PAD
            if row >= 0 and row + 8 <= LENGTH:
                colr[row : row + 8] = value
    roww[0:8] = rbuf[0, 8:16]
    roww[8:16] = row_c
    roww[16:24] = rbuf[2, 8:16]
    wide = jnp.concatenate([tlow[...], target[...], thigh[...]], axis=0)
    wide = jnp.concatenate([wide, jnp.zeros((48, 128), F32)], axis=1)
    wide = jnp.concatenate([wide, jnp.zeros((80, 384), F32)], axis=0)
    sheared = pltpu.roll(wide, 0, 1, stride=1, stride_axis=0)
    ts[4 + PAD : 4 + PAD + 312] = sheared.T[0:312]

    def first_column(u):
        return pl.multiple_of(8 * lax.shift_right_logical(u, 1), 8)

    def mask_at(u, row, count):
        shift = 4 * u - jnp.where(start + 4 * u - HALO >= 0, 0, 1 << 20)
        return jnp.bitwise_and(mk[pl.ds(row, count), :] - shift, -BAND) == 0

    def clear_sides(buffer, index, base):
        buffer[index, pl.ds(base, 16), :] = jnp.zeros((16, 128), F32)
        buffer[index, pl.ds(base + PAD + SPAN, 24), :] = jnp.zeros((24, 128), F32)

    left = lane_block(WIDE) < 2

    def pieces(buffer, index, row):
        ends = jnp.where(left, buffer[index + 3, pl.ds(row, WIDE), :], buffer[index, pl.ds(row, WIDE), :])
        return ends, buffer[index + 1, pl.ds(row, WIDE), :], buffer[index + 2, pl.ds(row, WIDE), :]

    def make_field(with_slope, u, carry):
        base = first_column(u)
        clear_sides(act0, u + 1, base)
        row_here = roww[pl.ds(u + 5, 1), :]
        for ch in range(3):
            row = base + PAD + CHUNK * ch
            mask = mask_at(u, row, CHUNK)
            x = jnp.where(mask, row_here + colr[pl.ds(row, CHUNK), :], 0.0)
            act, slope = gelu(x, with_slope)
            act0[u + 1, pl.ds(row, CHUNK), :] = act
            if with_slope:
                d0[u, pl.ds(row, CHUNK), :] = jnp.where(mask, slope, 0.0)
        return carry

    for begin, end, with_slope in ((0, 3, False), (3, 11, True), (11, 14, False)):
        lax.fori_loop(begin, end, functools.partial(make_field, with_slope), 0)

    def first_conv(with_slope, v, carry):
        base = pl.multiple_of(8 * v, 8)
        for q in range(3):
            for d, piece in enumerate(pieces(act0, 2 * v, base + PAD + 2 * (q - 1))):
                lhs[:, 128 * (3 * q + d) : 128 * (3 * q + d + 1)] = piece.astype(BF16)
        res[0:WIDE] = dot(lhs[...], w1[...])
        for h in range(2):
            u = 2 * v + h
            clear_sides(act1, u, base)
            row_here = roww[pl.ds(u + 5, 1), :]
            for ch in range(3):
                row = base + PAD + CHUNK * ch
                conv = res[CHUNK * ch : CHUNK * ch + CHUNK, 128 * h : 128 * h + 128]
                mask = mask_at(u, row, CHUNK)
                x = jnp.where(mask, (row_here + colr[pl.ds(row, CHUNK), :]) + conv, 0.0)
                act, slope = gelu(x, with_slope)
                act1[u, pl.ds(row, CHUNK), :] = act
                f1[u, pl.ds(row, CHUNK), :] = x
                if with_slope:
                    d1[u, pl.ds(row, CHUNK), :] = jnp.where(mask, slope, 0.0)
        return carry

    for begin, end, with_slope in ((0, 1, False), (1, 6, True), (6, 7, False)):
        lax.fori_loop(begin, end, functools.partial(first_conv, with_slope), 0)

    bins = lax.shift_right_logical(iota((128, 128), 0), 5)
    ones = (bins == lane_block(128)).astype(F32).astype(BF16)

    def make_misfit(u, carry):
        base = first_column(u)
        clear_sides(mis, u, base)
        for at, count in ((0, 96), (96, 96), (192, 80)):
            row = base + PAD + at
            value = rol[0:1] * f1[u, pl.ds(row, count), :]
            for p in range(3):
                for q in range(3):
                    tap = 3 * p + q
                    value = value + w2[8 * tap : 8 * tap + 1] * act1[u + p - 1, pl.ds(row + 4 * (q - 1), count), :]
            high, low = split(value)
            qbuf[at : at + count, 0:128] = high
            qbuf[at : at + count, 128:256] = low
            high, low = split(ts[pl.ds(row, count), :])
            qbuf[at : at + count, 256:384] = high
            qbuf[at : at + count, 384:512] = low
        pick = jnp.where(iota((128, 128), 0) == 4 * u - 4 + lane_block(128), -1.0, 0.0).astype(BF16)
        value = dot(qbuf[...], jnp.concatenate([ones, ones, pick, pick], axis=0)) * (1.0 / BAND)
        for at in range(0, SPAN, CHUNK):
            row = base + PAD + at
            mis[u, pl.ds(row, CHUNK), :] = jnp.where(mask_at(u, row, CHUNK), value[at : at + CHUNK], 0.0)
        return carry

    lax.fori_loop(1, GROUPS - 1, make_misfit, 0)

    def make_cotangent(u, carry):
        base = first_column(u)
        clear_sides(g1, u, base)
        sums = [None] * 10
        for ch in range(3):
            row = base + PAD + CHUNK * ch
            act = act1[u, pl.ds(row, CHUNK), :]
            back = None
            for p in range(3):
                for q in range(3):
                    tap = 3 * p + q
                    m = mis[u - (p - 1), pl.ds(row - 4 * (q - 1), CHUNK), :]
                    term = w2[8 * tap : 8 * tap + 1] * m
                    back = term if back is None else back + term
                    part = fold(act * m)
                    sums[tap] = part if sums[tap] is None else sums[tap] + part
            m = mis[u, pl.ds(row, CHUNK), :]
            part = fold(m * f1[u, pl.ds(row, CHUNK), :])
            sums[9] = part if sums[9] is None else sums[9] + part
            g1[u, pl.ds(row, CHUNK), :] = rol[0:1] * m + d1[u, pl.ds(row, CHUNK), :] * back
        for tap in range(10):
            source = u - (tap // 3 - 1) if tap < 9 else u
            own = jnp.logical_and(source >= FIRST_OWN, source <= LAST_OWN)
            tacc[8 * tap : 8 * tap + 8] += jnp.where(own, sums[tap], 0.0)
        return carry

    lax.fori_loop(2, GROUPS - 2, make_cotangent, 0)

    def first_adjoint(w, carry):
        base = pl.multiple_of(8 * w + 8, 8)
        for q in range(3):
            for d, piece in enumerate(pieces(g1, 2 * w + 2, base + PAD - 2 * (q - 1))):
                high, low = split(piece)
                lanes = slice(128 * (3 * q + d), 128 * (3 * q + d + 1))
                lhs2[0:WIDE, lanes] = high
                lhs2[WIDE : 2 * WIDE, lanes] = low
        res[...] = dot(lhs2[...], wa[...])
        for h in range(2):
            u = 2 * w + 3 + h
            total_row = None
            for ch in range(3):
                at = CHUNK * ch + 8 * h
                row = base + PAD + at
                lanes = slice(128 * h, 128 * h + 128)
                back = res[at : at + CHUNK, lanes] + res[WIDE + at : WIDE + at + CHUNK, lanes]
                value = g1[u, pl.ds(row, CHUNK), :] + d0[u, pl.ds(row, CHUNK), :] * back
                colacc[pl.ds(row, CHUNK), :] += value
                part = fold(value)
                total_row = part if total_row is None else total_row + part
            rowg[pl.ds(u - 3, 1), :] = jnp.sum(total_row, axis=0, keepdims=True)
        return carry

    lax.fori_loop(0, 4, first_adjoint, 0)

    where_block = lane_block(8)
    for m in range(REACH + 1):
        packed = jnp.zeros((8, 128), F32)
        for b in range(4):
            row = 32 * m + 8 * b + HALO + PAD
            value = colacc[row : row + 8]
            value = value + pltpu.roll(value, 64, 1)
            value = value + pltpu.roll(value, 32, 1)
            packed = jnp.where(where_block == b, value, packed)
        colp[8 * m : 8 * m + 8] = packed
    columns = []
    for m in range(1, REACH + 1):
        columns.append(
            pltpu.make_async_remote_copy(
                colp.at[pl.ds(8 * m, 8)], cbuf.at[m], s1.at[m], r1.at[m], device_id=(dev(m),), device_id_type=MESH
            )
        )
    for copy in columns:
        copy.start()

    def collect(u, carry):
        base = first_column(u)
        at = pl.multiple_of(WIDE * (u - FIRST_OWN), 16)
        high, low = split(g1[u, pl.ds(base + PAD, WIDE), :])
        gall[pl.ds(at, WIDE), 0:128] = high
        gall[pl.ds(at, WIDE), 128:256] = low
        for q in range(3):
            for d in range(3):
                piece = act0[u + d, pl.ds(base + PAD + 2 * (q - 1), WIDE), :]
                xall[pl.ds(at, WIDE), 128 * (3 * q + d) : 128 * (3 * q + d + 1)] = piece.astype(BF16)
        return carry

    lax.fori_loop(FIRST_OWN, LAST_OWN + 1, collect, 0)
    fg[...] = dot_t(gall[...], xall[...])

    where_block = lane_block(32)
    for group in range(3):
        packed = jnp.zeros((32, 128), F32)
        for place in range(4):
            tap = 4 * group + place
            if tap > 8:
                continue
            p, q = tap // 3 - 1, tap % 3
            value = jnp.zeros((32, 128), F32)
            for b in range(4):
                source = b + 2 * p
                lanes = 128 * (3 * q + source // 4 + 1)
                both = fg[32 * b : 32 * b + 32, lanes : lanes + 128] + fg[128 + 32 * b : 160 + 32 * b, lanes : lanes + 128]
                value = value + jnp.where(where_block == source % 4, both, 0.0)
            value = value + pltpu.roll(value, 64, 1)
            value = value + pltpu.roll(value, 32, 1)
            packed = jnp.where(where_block == place, value, packed)
        arbuf[128 + 32 * group : 160 + 32 * group] = packed
    for tap in range(10):
        arbuf[224 + tap : 225 + tap] = jnp.sum(tacc[8 * tap : 8 * tap + 8], axis=0, keepdims=True)
    sums = arbuf[224:240]
    sums = sums + pltpu.roll(sums, 64, 1)
    arbuf[224:240] = sums + pltpu.roll(sums, 32, 1)
    high, low = split(jnp.concatenate([tacc[8 * tap : 8 * tap + 8] for tap in range(9)], axis=1))
    by_read = jnp.sum(dot(high, k2t[...]) + dot(low, k2t[...]), axis=0, keepdims=True)
    arbuf[233:234, 0:32] = arbuf[233:234, 0:32] + by_read

    where_block = lane_block(8)
    rows = rowg[...]
    for b in range(4):
        vbuf[1, pl.ds(b, 8, stride=4), :] = jnp.where(where_block == 1, pltpu.roll(rows, (32 - 32 * b) % 128, 1) if b != 1 else rows, 0.0)
    for copy in gathers:
        copy.wait_send()
    for copy in columns:
        copy.wait_recv()
    own = colp[0:8]
    for m in range(1, REACH + 1):
        own = own + cbuf[m]
    for b in range(4):
        vbuf[0, 8 * b : 8 * b + 8] = jnp.where(where_block == 0, pltpu.roll(own, (128 - 32 * b) % 128, 1) if b else own, 0.0)
    both = vbuf[0] + vbuf[1]
    high, low = split(both)
    by_feature = dot_t(jnp.concatenate([high, low], axis=0), jnp.concatenate([feat[...]] * 2, axis=0))
    arbuf[0:64] = by_feature[0:64, 0:128]
    arbuf[64:128] = by_feature[0:64, 128:256]

    weights = jnp.concatenate([col_t[...], row_t[...]], axis=0)
    by_bin = dot(high[:, 0:64], weights) + dot(low[:, 0:64], weights)
    extra[0:32] = by_bin[:, 0:128]
    extra[32:64] = by_bin[:, 128:256]
    for copy in columns:
        copy.wait_send()


def reduce_kernel(n, arbuf, red, pairbuf, halfbuf, rsbuf, bbuf, mine, gbuf, s2, r2, s3, r3, s4, r4, s5, r5):
    me = lax.axis_index("diag")
    side = n // SIDE
    pos = lax.rem(me, SIDE)
    core = lax.rem(me, 2)
    depth = lax.div(pos, 2)
    plane = lax.div(me, SIDE)
    partner = me + 1 - 2 * core

    def in_line(q):
        return me + 2 * (q - depth)

    def across(q):
        return q * SIDE + pos

    barrier = pltpu.get_barrier_semaphore()
    pl.semaphore_signal(barrier, inc=1, device_id=(partner,), device_id_type=MESH)
    for s in range(1, LINE):
        pl.semaphore_signal(barrier, inc=1, device_id=(in_line(lax.rem(depth + s, LINE)),), device_id_type=MESH)
    for s in range(1, side):
        pl.semaphore_signal(barrier, inc=1, device_id=(across(lax.rem(plane + s, side)),), device_id_type=MESH)
    pl.semaphore_wait(barrier, LINE + side - 1)

    def chunk(q):
        return pl.ds(pl.multiple_of(q * PART, PART), PART)

    exchange = pltpu.make_async_remote_copy(
        arbuf.at[pl.ds(pl.multiple_of(128 * (1 - core), 128), 128)], pairbuf, s5.at[0], r5.at[0],
        device_id=(partner,), device_id_type=MESH,
    )
    exchange.start()
    exchange.wait()
    own_half = pl.ds(pl.multiple_of(128 * core, 128), 128)
    halfbuf[...] = arbuf[own_half, :] + pairbuf[...]

    def scatter(s):
        q = lax.rem(depth + s, LINE)
        return pltpu.make_async_remote_copy(
            halfbuf.at[chunk(q)], rsbuf.at[s], s2.at[s], r2.at[s], device_id=(in_line(q),), device_id_type=MESH
        )

    def across_copy(s):
        q = lax.rem(plane + s, side)
        return pltpu.make_async_remote_copy(
            mine, bbuf.at[plane], s3.at[s], r3.at[s], device_id=(across(q),), device_id_type=MESH
        )

    here = chunk(LINE * core + depth)

    def spread_copy(s):
        q = lax.rem(depth + s, LINE)
        return pltpu.make_async_remote_copy(
            gbuf.at[here], gbuf.at[here], s4.at[s], r4.at[s], device_id=(in_line(q),), device_id_type=MESH
        )

    def run(count, make):
        copies = [make(s) for s in range(1, count)]
        for copy in copies:
            copy.start()
        for copy in sent:
            copy.wait_send()
        sent[:] = copies
        for copy in copies:
            copy.wait_recv()

    sent = []
    run(LINE, scatter)
    total = halfbuf[chunk(depth), :]
    for s in range(1, LINE):
        total = total + rsbuf[s]
    mine[...] = total
    bbuf[plane] = total
    run(side, across_copy)
    total = bbuf[0]
    for q in range(1, side):
        total = total + bbuf[q]
    gbuf[here, :] = total
    run(LINE, spread_copy)
    back = pltpu.make_async_remote_copy(
        gbuf.at[own_half], gbuf.at[own_half], s5.at[1], r5.at[1], device_id=(partner,), device_id_type=MESH
    )
    back.start()
    for copy in sent:
        copy.wait_send()
    back.wait()
    red[...] = gbuf[...]


def finish_kernel(red, extra, gfeat, grow, gcol, gone, gtwo, gread):
    gfeat[:, 0:128] = extra[0:32]
    gfeat[:, 128:256] = extra[32:64]
    gcol[:, 0:128] = red[0:32]
    gcol[:, 128:256] = red[64:96]
    grow[:, 0:128] = red[32:64]
    grow[:, 128:256] = red[96:128]
    for group in range(3):
        block = red[128 + 32 * group : 160 + 32 * group].T
        count = 128 if group < 2 else 32
        gone[128 * group : 128 * group + count] = block[0:count]
    by_channel = red[224:240].T
    read = extra[64:65, 0:32]
    for tap in range(9):
        gtwo[32 * tap : 32 * tap + 32] = by_channel[0:32, tap : tap + 1] * read
    gread[...] = red[233:234, 0:32]


def shards(n, features, row_proj, col_proj, first_filter, second_filter, readout, target):
    side = n // SIDE
    vmem = pl.BlockSpec(memory_space=pltpu.VMEM)

    def shape(*dims):
        return jax.ShapeDtypeStruct(dims, F32)

    def real(*dims):
        return pltpu.VMEM(dims, F32)

    def half(*dims):
        return pltpu.VMEM(dims, BF16)

    k1 = first_filter.reshape(9 * PAIR, PAIR)
    k2 = second_filter.reshape(9 * PAIR, PAIR)
    ro = readout.reshape(1, PAIR)
    row_t, col_t = row_proj.T, col_proj.T
    hbm = pl.BlockSpec(memory_space=pltpu.HBM)
    scratch = dict(
        feat=half(ROWS, 256), row_t=half(PAIR, 256), col_t=half(PAIR, 256), target=real(ROWS, 256), k1=half(288, PAIR), k2=half(288, PAIR),
        proj=real(32, 128), sbuf=real(16, 128), rbuf=real(AHEAD + 2, 16, 128), tlow=real(8, 256), thigh=real(8, 256),
        roww=real(24, 128), w1=half(1152, 256), wa=half(1152, 256), w2=real(72, 128), rol=real(8, 128),
        colr=real(LENGTH, 128), mk=pltpu.VMEM((LENGTH, 128), jnp.int32), ts=real(LENGTH, 128),
        act0=real(GROUPS + 2, LENGTH, 128), d0=real(GROUPS, LENGTH, 128),
        act1=real(GROUPS, LENGTH, 128), f1=real(GROUPS, LENGTH, 128), d1=real(GROUPS, LENGTH, 128),
        mis=real(GROUPS, LENGTH, 128), g1=real(GROUPS, LENGTH, 128),
        lhs=half(WIDE, 1152), lhs2=half(2 * WIDE, 1152), k2t=half(1152, PAIR), res=real(2 * WIDE, 256), qbuf=half(WIDE, 512),
        xall=half(8 * WIDE, 1152), gall=half(8 * WIDE, 256), fg=real(256, 1152), tacc=real(80, 128),
        colacc=real(LENGTH, 128), tiles=real(288, 256), colp=real(72, 128), rowg=real(8, 128),
        cbuf=real(REACH + 1, 8, 128), vbuf=real(2, 32, 128), loads=SEM((6,)),
        ss=SEM((AHEAD + 4,)), rs=SEM((AHEAD + 4,)), s1=SEM((REACH + 1,)), r1=SEM((REACH + 1,)),
    )
    part, extra = pl.pallas_call(
        functools.partial(step_kernel, n),
        out_shape=(shape(256, 128), shape(72, 128)),
        in_specs=[hbm] * 6 + [vmem],
        out_specs=(vmem,) * 2,
        scratch_shapes=list(scratch.values()),
        compiler_params=pltpu.CompilerParams(
            collective_id=0, has_side_effects=True, vmem_limit_bytes=60 * 1024 * 1024
        ),
        name="step",
    )(features, row_t, col_t, target, k1, k2, ro)

    red = pl.pallas_call(
        functools.partial(reduce_kernel, n),
        out_shape=shape(256, 128),
        in_specs=[vmem],
        out_specs=vmem,
        scratch_shapes=[
            real(128, 128), real(128, 128), real(LINE, PART, 128), real(side, PART, 128), real(PART, 128), real(256, 128),
            SEM((LINE,)), SEM((LINE,)), SEM((side,)), SEM((side,)), SEM((LINE,)), SEM((LINE,)), SEM((2,)), SEM((2,)),
        ],
        compiler_params=pltpu.CompilerParams(
            collective_id=1, has_side_effects=True, vmem_limit_bytes=4 * 1024 * 1024
        ),
        name="reduce",
    )(part)

    gfeat, grow, gcol, gone, gtwo, gread = pl.pallas_call(
        finish_kernel,
        out_shape=(shape(ROWS, 256), shape(32, 256), shape(32, 256), shape(288, 32), shape(288, 32), shape(1, 32)),
        in_specs=[vmem] * 2,
        out_specs=(vmem,) * 6,
        compiler_params=pltpu.CompilerParams(vmem_limit_bytes=4 * 1024 * 1024),
        name="finish",
    )(red, extra)
    return gfeat, grow.T, gcol.T, gone.reshape(3, 3, PAIR, PAIR), gtwo.reshape(3, 3, PAIR, PAIR), gread.reshape(PAIR)


def solution(mesh):
    n = mesh.shape["diag"]
    in_specs = (P("diag", None), P(), P(), P(), P(), P(), P("diag", None))
    out_specs = (P("diag", None), P(), P(), P(), P(), P())
    return jax.shard_map(
        functools.partial(shards, n), mesh=mesh, in_specs=in_specs, out_specs=out_specs, check_vma=False
    )
```

```python
import functools
import math

import jax
import jax.numpy as jnp
from jax import lax
from jax.experimental import pallas as pl
from jax.experimental.pallas import tpu as pltpu
from jax.sharding import PartitionSpec as P

MESH = pl.DeviceIdType.MESH
F32, BF16 = jnp.float32, jnp.bfloat16

ROWS = 32
BAND = 256
PAIR = 32
HALO = 12
GROUPS = (ROWS + 2 * HALO) // 4
FIRST_OWN, LAST_OWN = 3, 10
PAD = 16
LENGTH = 352
WIDE, SPAN, CHUNK = 272, 264, 88
AHEAD = 9
REACH = 8
C0 = math.sqrt(2.0 / math.pi)
C1 = C0 * 0.044715
SIDE = 16
LINE = 8
PART = 16
SEM = pltpu.SemaphoreType.DMA


def iota(shape, dim):
    return lax.broadcasted_iota(jnp.int32, shape, dim)


def lane_block(rows):
    return lax.shift_right_logical(iota((rows, 128), 1), 5)


def gelu(x, with_slope):
    cubic = C1 * (x * x)
    s = 0.5 * jnp.tanh(x * (cubic + C0)) + 0.5
    value = x * s
    slope = s + value * (1.0 - s) * (6.0 * cubic + 2.0 * C0) if with_slope else None
    return value.astype(BF16).astype(F32), slope


def split(x):
    high = x.astype(BF16)
    return high, (x - high.astype(F32)).astype(BF16)


def fold(x):
    total = x[0:8]
    for i in range(1, x.shape[0] // 8):
        total = total + x[8 * i : 8 * i + 8]
    return total


def dot(a, b):
    return jnp.dot(a, b, preferred_element_type=F32)


def dot_t(a, b):
    return lax.dot_general(a, b, (((0,), (0,)), ((), ())), preferred_element_type=F32)


def dot_nt(a, b):
    return lax.dot_general(a, b, (((1,), (1,)), ((), ())), preferred_element_type=F32)


def repeater(lanes):
    return (jnp.bitwise_and(iota((PAIR, lanes), 1), 31) == iota((PAIR, lanes), 0)).astype(F32).astype(BF16)


def spread(block):
    turned = [block] + [pltpu.roll(block, 32 * s, 1) for s in (1, 2, 3)]
    where_block = lane_block(8)
    outs = []
    for b in range(4):
        value = turned[(3 - b) % 4]
        for other in range(3):
            value = jnp.where(where_block == other, turned[(other - b) % 4], value)
        outs.append(value)
    return outs


def step_kernel(
    n, feat_in, row_in, col_in, target_in, k1_in, k2_in, ro, red,
    feat, row_t, col_t, target, k1, k2,
    proj, sbuf, rbuf, tlow, thigh, roww, w1, wa, w2, rol, colr, mk, ts, act0, d0, act1, f1, d1, mis, g1,
    lhs, lhs2, k2t, res, qbuf, wq, xall, gall, fg, tacc, colacc, tiles, colp, rowg, cbuf, vbuf, arbuf, pairbuf, halfbuf, rsbuf, bbuf, mine, gbuf,
    loads, ss, rs, s1, r1, s2, r2, s3, r3, s4, r4, s5, r5,
):
    me = lax.axis_index("diag")
    start = me * ROWS
    side = n // SIDE
    pos = lax.rem(me, SIDE)
    core = lax.rem(me, 2)
    depth = lax.div(pos, 2)
    plane = lax.div(me, SIDE)
    partner = me + 1 - 2 * core

    def dev(step):
        return lax.rem(me + step + n, n)

    def in_line(q):
        return me + 2 * (q - depth)

    def across(q):
        return q * SIDE + pos

    fetches = [
        pltpu.make_async_copy(source, place, loads.at[i])
        for i, (source, place) in enumerate(
            ((feat_in, feat), (row_in, row_t), (col_in, col_t), (k1_in, k1), (k2_in, k2), (target_in, target))
        )
    ]
    for fetch in fetches:
        fetch.start()

    barrier = pltpu.get_barrier_semaphore()
    for step in (-1,) + tuple(range(1, AHEAD + 1)) + tuple(range(-REACH, 0)):
        pl.semaphore_signal(barrier, inc=1, device_id=(dev(step),), device_id_type=MESH)

    def greet(s, carry):
        pl.semaphore_signal(barrier, inc=1, device_id=(in_line(lax.rem(depth + s, LINE)),), device_id_type=MESH)
        return carry

    lax.fori_loop(1, LINE, greet, 0)
    pl.semaphore_signal(barrier, inc=1, device_id=(partner,), device_id_type=MESH)

    def greet_across(s, carry):
        pl.semaphore_signal(barrier, inc=1, device_id=(across(lax.rem(plane + s, side)),), device_id_type=MESH)
        return carry

    lax.fori_loop(1, side, greet_across, 0)

    for fetch in fetches[0:3]:
        fetch.wait()
    proj[...] = dot_nt(feat[...], jnp.concatenate([row_t[...]] * 4, axis=0))
    cc = dot_nt(feat[...], jnp.concatenate([col_t[...]] * 4, axis=0))
    where_block = lane_block(8)
    row_c = jnp.zeros((8, 128), F32)
    col_c = jnp.zeros((8, 128), F32)
    for b in range(4):
        row_c = jnp.where(where_block == b, proj[pl.ds(b, 8, stride=4), :], row_c)
        col_c = jnp.where(where_block == b, cc[8 * b : 8 * b + 8], col_c)
    sbuf[0:8] = col_c
    sbuf[8:16] = row_c
    pl.semaphore_wait(barrier, AHEAD + 1 + REACH + LINE + side - 1)
    gathers = []
    for slot, step in ((0, 1), (2, -1)):
        gathers.append(
            pltpu.make_async_remote_copy(sbuf, rbuf.at[slot], ss.at[slot], rs.at[slot], device_id=(dev(step),), device_id_type=MESH)
        )
    for m in range(3, AHEAD + 2):
        gathers.append(
            pltpu.make_async_remote_copy(
                sbuf.at[pl.ds(0, 8)], rbuf.at[m, pl.ds(0, 8)], ss.at[m], rs.at[m], device_id=(dev(1 - m),), device_id_type=MESH
            )
        )
    gathers.append(
        pltpu.make_async_remote_copy(
            target_in.at[pl.ds(24, 8)], tlow, ss.at[AHEAD + 2], rs.at[AHEAD + 2], device_id=(dev(1),), device_id_type=MESH
        )
    )
    gathers.append(
        pltpu.make_async_remote_copy(
            target_in.at[pl.ds(0, 8)], thigh, ss.at[AHEAD + 3], rs.at[AHEAD + 3], device_id=(dev(-1),), device_id_type=MESH
        )
    )
    for copy in gathers:
        copy.start()

    for fetch in fetches[3:6]:
        fetch.wait()
    rep8 = repeater(256)
    where_out = lax.shift_right_logical(iota((PAIR, 256), 1), 5)

    def build(weights, sign):
        for q in range(3):
            for place, ri in enumerate((8, 9, -2, -1, 0, 1, 2, 3, 4, 5, 6, 7)):
                value = jnp.zeros((PAIR, 256), F32)
                for p in range(3):
                    tap = 3 * p + q
                    ro_here = ri - sign * 2 * (p - 1)
                    if 0 <= ro_here < 8:
                        value = jnp.where(where_out == ro_here, tiles[32 * tap : 32 * tap + 32], value)
                row = (q * 12 + place) * 32
                weights[row : row + 32] = value.astype(BF16)

    tiles[...] = dot(k1[...], rep8)
    build(w1, 1)
    for tap in range(9):
        tiles[32 * tap : 32 * tap + 32] = dot_t(k1[32 * tap : 32 * tap + 32], rep8)
    build(wa, -1)
    ro8 = jnp.broadcast_to(ro[...].astype(F32), (8, PAIR)).astype(BF16)
    rol[...] = dot(ro8, repeater(128))
    for tap in range(9):
        for b in range(4):
            row = 128 * tap + 32 * b
            k2t[row : row + 32] = k2[32 * tap : 32 * tap + 32]
        w2[8 * tap : 8 * tap + 8] = dot_nt(ro8, k2t[128 * tap : 128 * tap + 128])
    gbuf[320:328] = rol[...]

    same = lax.shift_right_logical(iota((256, 256), 0), 5) == lax.shift_right_logical(iota((256, 256), 1), 5)
    ones = same.astype(F32).astype(BF16)
    wq[0:256] = ones
    wq[256:512] = ones
    act0[0] = jnp.zeros((LENGTH, 128), F32)
    act0[GROUPS + 1] = jnp.zeros((LENGTH, 128), F32)
    colacc[...] = jnp.zeros((LENGTH, 128), F32)
    tacc[...] = jnp.zeros((80, 128), F32)
    ts[...] = jnp.zeros((LENGTH, 128), F32)
    arbuf[224:256] = jnp.zeros((32, 128), F32)
    column = iota((LENGTH, 128), 0) - PAD
    mk[...] = jnp.where(column + (start - HALO) < n * ROWS, column - lane_block(LENGTH), 1 << 20)

    for copy in gathers:
        copy.wait_recv()
    for m in range(AHEAD + 2):
        for b, value in enumerate(spread(col_c if m == 1 else rbuf[m, 0:8])):
            row = 32 * (m - 1) + 8 * b + HALO + PAD
            if row >= 0 and row + 8 <= LENGTH:
                colr[row : row + 8] = value
    roww[0:8] = rbuf[0, 8:16]
    roww[8:16] = row_c
    roww[16:24] = rbuf[2, 8:16]
    wide = jnp.concatenate([tlow[...], target[...], thigh[...]], axis=0)
    wide = jnp.concatenate([wide, jnp.zeros((48, 128), F32)], axis=1)
    wide = jnp.concatenate([wide, jnp.zeros((80, 384), F32)], axis=0)
    sheared = pltpu.roll(wide, 0, 1, stride=1, stride_axis=0)
    ts[4 + PAD : 4 + PAD + 312] = sheared.T[0:312]

    def first_column(u):
        return pl.multiple_of(8 * lax.shift_right_logical(u, 1), 8)

    def mask_at(u, row, count):
        shift = 4 * u - jnp.where(start + 4 * u - HALO >= 0, 0, 1 << 20)
        return jnp.bitwise_and(mk[pl.ds(row, count), :] - shift, -BAND) == 0

    def clear_sides(buffer, index, base):
        buffer[index, pl.ds(base, 16), :] = jnp.zeros((16, 128), F32)
        buffer[index, pl.ds(base + PAD + SPAN, 24), :] = jnp.zeros((24, 128), F32)

    left = lane_block(WIDE) < 2

    def pieces(buffer, index, row):
        ends = jnp.where(left, buffer[index + 3, pl.ds(row, WIDE), :], buffer[index, pl.ds(row, WIDE), :])
        return ends, buffer[index + 1, pl.ds(row, WIDE), :], buffer[index + 2, pl.ds(row, WIDE), :]

    def make_field(with_slope, v):
        base = pl.multiple_of(8 * v, 8)
        for h in range(2):
            u = 2 * v + h
            clear_sides(act0, u + 1, base)
            row_here = roww[pl.ds(u + 5, 1), :]
            for ch in range(3):
                row = base + PAD + CHUNK * ch
                mask = mask_at(u, row, CHUNK)
                x = jnp.where(mask, row_here + colr[pl.ds(row, CHUNK), :], 0.0)
                act, slope = gelu(x, with_slope)
                act0[u + 1, pl.ds(row, CHUNK), :] = act
                if with_slope:
                    d0[u, pl.ds(row, CHUNK), :] = jnp.where(mask, slope, 0.0)

    def conv_operand(v):
        base = pl.multiple_of(8 * v, 8)
        for q in range(3):
            for d, piece in enumerate(pieces(act0, 2 * v, base + PAD + 2 * (q - 1))):
                lhs[:, 128 * (3 * q + d) : 128 * (3 * q + d + 1)] = piece.astype(BF16)

    def conv():
        res[0:WIDE] = dot(lhs[...], w1[...])

    def conv_result(with_slope, v):
        base = pl.multiple_of(8 * v, 8)
        for h in range(2):
            u = 2 * v + h
            clear_sides(act1, u, base)
            clear_sides(f1, u, base)
            row_here = roww[pl.ds(u + 5, 1), :]
            for ch in range(3):
                row = base + PAD + CHUNK * ch
                added = res[CHUNK * ch : CHUNK * ch + CHUNK, 128 * h : 128 * h + 128]
                mask = mask_at(u, row, CHUNK)
                x = jnp.where(mask, (row_here + colr[pl.ds(row, CHUNK), :]) + added, 0.0)
                act, slope = gelu(x, with_slope)
                act1[u, pl.ds(row, CHUNK), :] = act
                f1[u, pl.ds(row, CHUNK), :] = x
                if with_slope:
                    d1[u, pl.ds(row, CHUNK), :] = jnp.where(mask, slope, 0.0)

    make_field(False, 0)
    make_field(True, 1)
    conv_operand(0)
    make_field(True, 2)
    conv()

    def first_conv(with_field, v, carry):
        conv_operand(v)
        conv_result(True, v - 1)
        if with_field:
            make_field(True, v + 2)
        conv()
        return carry

    lax.fori_loop(1, 5, functools.partial(first_conv, True), 0)
    lax.fori_loop(5, 7, functools.partial(first_conv, False), 0)
    conv_result(False, 6)

    def make_misfit(w, carry):
        base = pl.multiple_of(8 * w, 8)
        for at, count in ((0, 96), (96, 96), (192, 80)):
            row = base + PAD + at
            for h in range(2):
                u = 2 * w + 1 + h
                value = rol[0:1] * f1[u, pl.ds(row, count), :]
                for p in range(3):
                    for q in range(3):
                        tap = 3 * p + q
                        value = value + w2[8 * tap : 8 * tap + 1] * act1[u + p - 1, pl.ds(row + 4 * (q - 1), count), :]
                high, low = split(value)
                qbuf[at : at + count, 128 * h : 128 * h + 128] = high
                qbuf[at : at + count, 256 + 128 * h : 384 + 128 * h] = low
            high, low = split(ts[pl.ds(row, count), :])
            qbuf[at : at + count, 512:640] = high
            qbuf[at : at + count, 640:768] = low
        pick = jnp.where(iota((128, 256), 0) == 8 * w + lax.shift_right_logical(iota((128, 256), 1), 5), -1.0, 0.0).astype(BF16)
        wq[512:640] = pick
        wq[640:768] = pick
        value = dot(qbuf[...], wq[...]) * (1.0 / BAND)
        for h in range(2):
            u = 2 * w + 1 + h
            clear_sides(mis, u, base)
            for at, count in ((0, 96), (96, 96), (192, 80)):
                row = base + PAD + at
                mis[u, pl.ds(row, count), :] = jnp.where(
                    mask_at(u, row, count), value[at : at + count, 128 * h : 128 * h + 128], 0.0
                )
        return carry

    lax.fori_loop(0, 6, make_misfit, 0)

    def make_cotangent(u, carry):
        base = first_column(u)
        clear_sides(g1, u, base)
        sums = [None] * 10
        for ch in range(3):
            row = base + PAD + CHUNK * ch
            act = act1[u, pl.ds(row, CHUNK), :]
            back = None
            for p in range(3):
                for q in range(3):
                    tap = 3 * p + q
                    m = mis[u - (p - 1), pl.ds(row - 4 * (q - 1), CHUNK), :]
                    term = w2[8 * tap : 8 * tap + 1] * m
                    back = term if back is None else back + term
                    part = fold(act * m)
                    sums[tap] = part if sums[tap] is None else sums[tap] + part
            m = mis[u, pl.ds(row, CHUNK), :]
            part = fold(m * f1[u, pl.ds(row, CHUNK), :])
            sums[9] = part if sums[9] is None else sums[9] + part
            g1[u, pl.ds(row, CHUNK), :] = rol[0:1] * m + d1[u, pl.ds(row, CHUNK), :] * back
        for tap in range(10):
            source = u - (tap // 3 - 1) if tap < 9 else u
            own = jnp.logical_and(source >= FIRST_OWN, source <= LAST_OWN)
            tacc[8 * tap : 8 * tap + 8] += jnp.where(own, sums[tap], 0.0)
        return carry

    lax.fori_loop(2, GROUPS - 2, make_cotangent, 0)

    def adjoint_operand(w):
        base = pl.multiple_of(8 * w + 8, 8)
        for q in range(3):
            for d, piece in enumerate(pieces(g1, 2 * w + 2, base + PAD - 2 * (q - 1))):
                high, low = split(piece)
                lanes = slice(128 * (3 * q + d), 128 * (3 * q + d + 1))
                lhs2[0:WIDE, lanes] = high
                lhs2[WIDE : 2 * WIDE, lanes] = low

    def adjoint():
        res[...] = dot(lhs2[...], wa[...])

    def adjoint_result(w):
        base = pl.multiple_of(8 * w + 8, 8)
        for h in range(2):
            u = 2 * w + 3 + h
            total_row = None
            for ch in range(3):
                at = CHUNK * ch + 8 * h
                row = base + PAD + at
                lanes = slice(128 * h, 128 * h + 128)
                back = res[at : at + CHUNK, lanes] + res[WIDE + at : WIDE + at + CHUNK, lanes]
                value = g1[u, pl.ds(row, CHUNK), :] + d0[u, pl.ds(row, CHUNK), :] * back
                colacc[pl.ds(row, CHUNK), :] += value
                part = fold(value)
                total_row = part if total_row is None else total_row + part
            rowg[pl.ds(u - 3, 1), :] = jnp.sum(total_row, axis=0, keepdims=True)

    def collect(w):
        for h in range(2):
            u = 2 * w + 3 + h
            base = pl.multiple_of(8 * w + 8 + 8 * h, 8)
            at = pl.multiple_of(WIDE * (2 * w + h), 16)
            high, low = split(g1[u, pl.ds(base + PAD, WIDE), :])
            gall[pl.ds(at, WIDE), 0:128] = high
            gall[pl.ds(at, WIDE), 128:256] = low
            for q in range(3):
                for d in range(3):
                    piece = act0[u + d, pl.ds(base + PAD + 2 * (q - 1), WIDE), :]
                    xall[pl.ds(at, WIDE), 128 * (3 * q + d) : 128 * (3 * q + d + 1)] = piece.astype(BF16)

    adjoint_operand(0)
    collect(0)
    adjoint()

    def first_adjoint(w, carry):
        adjoint_operand(w)
        adjoint_result(w - 1)
        collect(w)
        adjoint()
        return carry

    lax.fori_loop(1, 4, first_adjoint, 0)
    adjoint_result(3)

    where_block = lane_block(8)
    for m in range(REACH + 1):
        packed = jnp.zeros((8, 128), F32)
        for b in range(4):
            row = 32 * m + 8 * b + HALO + PAD
            value = colacc[row : row + 8]
            value = value + pltpu.roll(value, 64, 1)
            value = value + pltpu.roll(value, 32, 1)
            packed = jnp.where(where_block == b, value, packed)
        colp[8 * m : 8 * m + 8] = packed
    columns = []
    for m in range(1, REACH + 1):
        columns.append(
            pltpu.make_async_remote_copy(
                colp.at[pl.ds(8 * m, 8)], cbuf.at[m], s1.at[m], r1.at[m], device_id=(dev(m),), device_id_type=MESH
            )
        )
    for copy in columns:
        copy.start()

    fg[...] = dot_t(gall[...], xall[...])

    where_block = lane_block(32)
    for group in range(3):
        packed = jnp.zeros((32, 128), F32)
        for place in range(4):
            tap = 4 * group + place
            if tap > 8:
                continue
            p, q = tap // 3 - 1, tap % 3
            value = jnp.zeros((32, 128), F32)
            for b in range(4):
                source = b + 2 * p
                lanes = 128 * (3 * q + source // 4 + 1)
                both = fg[32 * b : 32 * b + 32, lanes : lanes + 128] + fg[128 + 32 * b : 160 + 32 * b, lanes : lanes + 128]
                value = value + jnp.where(where_block == source % 4, both, 0.0)
            value = value + pltpu.roll(value, 64, 1)
            value = value + pltpu.roll(value, 32, 1)
            packed = jnp.where(where_block == place, value, packed)
        arbuf[128 + 32 * group : 160 + 32 * group] = packed
    for tap in range(10):
        arbuf[224 + tap : 225 + tap] = jnp.sum(tacc[8 * tap : 8 * tap + 8], axis=0, keepdims=True)
    sums = arbuf[224:240]
    sums = sums + pltpu.roll(sums, 64, 1)
    arbuf[224:240] = sums + pltpu.roll(sums, 32, 1)
    high, low = split(jnp.concatenate([tacc[8 * tap : 8 * tap + 8] for tap in range(9)], axis=1))
    by_read = jnp.sum(dot(high, k2t[...]) + dot(low, k2t[...]), axis=0, keepdims=True)
    arbuf[233:234, 0:32] = arbuf[233:234, 0:32] + by_read

    where_block = lane_block(8)
    rows = rowg[...]
    for b in range(4):
        vbuf[1, pl.ds(b, 8, stride=4), :] = jnp.where(where_block == 1, pltpu.roll(rows, (32 - 32 * b) % 128, 1) if b != 1 else rows, 0.0)
    for copy in gathers:
        copy.wait_send()
    for copy in columns:
        copy.wait_recv()
    own = colp[0:8]
    for m in range(1, REACH + 1):
        own = own + cbuf[m]
    for b in range(4):
        vbuf[0, 8 * b : 8 * b + 8] = jnp.where(where_block == 0, pltpu.roll(own, (128 - 32 * b) % 128, 1) if b else own, 0.0)
    both = vbuf[0] + vbuf[1]
    high, low = split(both)
    by_feature = dot_t(jnp.concatenate([high, low], axis=0), jnp.concatenate([feat[...]] * 2, axis=0))
    arbuf[0:64] = by_feature[0:64, 0:128]
    arbuf[64:128] = by_feature[0:64, 128:256]

    def chunk(q):
        return pl.ds(pl.multiple_of(q * PART, PART), PART)

    exchange = pltpu.make_async_remote_copy(
        arbuf.at[pl.ds(pl.multiple_of(128 * (1 - core), 128), 128)], pairbuf, s5.at[0], r5.at[0],
        device_id=(partner,), device_id_type=MESH,
    )
    exchange.start()
    weights = jnp.concatenate([col_t[...], row_t[...]], axis=0)
    by_bin = dot(high[:, 0:64], weights) + dot(low[:, 0:64], weights)
    gbuf[256:288] = by_bin[:, 0:128]
    gbuf[288:320] = by_bin[:, 128:256]
    exchange.wait()
    own_half = pl.ds(pl.multiple_of(128 * core, 128), 128)
    halfbuf[...] = arbuf[own_half, :] + pairbuf[...]

    def scatter(s):
        q = lax.rem(depth + s, LINE)
        return pltpu.make_async_remote_copy(
            halfbuf.at[chunk(q)], rsbuf.at[s], s2.at[s], r2.at[s], device_id=(in_line(q),), device_id_type=MESH
        )

    def across_copy(s):
        q = lax.rem(plane + s, side)
        return pltpu.make_async_remote_copy(
            mine, bbuf.at[plane], s3.at[s], r3.at[s], device_id=(across(q),), device_id_type=MESH
        )

    here = chunk(LINE * core + depth)

    def spread_copy(s):
        q = lax.rem(depth + s, LINE)
        return pltpu.make_async_remote_copy(
            gbuf.at[here], gbuf.at[here], s4.at[s], r4.at[s], device_id=(in_line(q),), device_id_type=MESH
        )

    def run(count, make):
        copies = [make(s) for s in range(1, count)]
        for copy in copies:
            copy.start()
        for copy in sent:
            copy.wait_send()
        sent[:] = copies
        for copy in copies:
            copy.wait_recv()

    sent = columns
    run(LINE, scatter)
    total = halfbuf[chunk(depth), :]
    for s in range(1, LINE):
        total = total + rsbuf[s]
    mine[...] = total
    bbuf[plane] = total
    run(side, across_copy)
    total = bbuf[0]
    for q in range(1, side):
        total = total + bbuf[q]
    gbuf[here, :] = total
    run(LINE, spread_copy)
    back = pltpu.make_async_remote_copy(
        gbuf.at[own_half], gbuf.at[own_half], s5.at[1], r5.at[1], device_id=(partner,), device_id_type=MESH
    )
    back.start()
    for copy in sent:
        copy.wait_send()
    back.wait()
    red[...] = gbuf[...]


def finish_kernel(red, gfeat, grow, gcol, gone, gtwo, gread):
    gfeat[:, 0:128] = red[256:288]
    gfeat[:, 128:256] = red[288:320]
    gcol[:, 0:128] = red[0:32]
    gcol[:, 128:256] = red[64:96]
    grow[:, 0:128] = red[32:64]
    grow[:, 128:256] = red[96:128]
    for group in range(3):
        block = red[128 + 32 * group : 160 + 32 * group].T
        count = 128 if group < 2 else 32
        gone[128 * group : 128 * group + count] = block[0:count]
    by_channel = red[224:240].T
    read = red[320:321, 0:32]
    for tap in range(9):
        gtwo[32 * tap : 32 * tap + 32] = by_channel[0:32, tap : tap + 1] * read
    gread[...] = red[233:234, 0:32]


def shards(n, features, row_proj, col_proj, first_filter, second_filter, readout, target):
    side = n // SIDE
    vmem = pl.BlockSpec(memory_space=pltpu.VMEM)

    def shape(*dims):
        return jax.ShapeDtypeStruct(dims, F32)

    def real(*dims):
        return pltpu.VMEM(dims, F32)

    def half(*dims):
        return pltpu.VMEM(dims, BF16)

    k1 = first_filter.reshape(9 * PAIR, PAIR)
    k2 = second_filter.reshape(9 * PAIR, PAIR)
    ro = readout.reshape(1, PAIR)
    row_t, col_t = row_proj.T, col_proj.T
    hbm = pl.BlockSpec(memory_space=pltpu.HBM)
    scratch = dict(
        feat=half(ROWS, 256), row_t=half(PAIR, 256), col_t=half(PAIR, 256), target=real(ROWS, 256), k1=half(288, PAIR), k2=half(288, PAIR),
        proj=real(32, 128), sbuf=real(16, 128), rbuf=real(AHEAD + 2, 16, 128), tlow=real(8, 256), thigh=real(8, 256),
        roww=real(24, 128), w1=half(1152, 256), wa=half(1152, 256), w2=real(72, 128), rol=real(8, 128),
        colr=real(LENGTH, 128), mk=pltpu.VMEM((LENGTH, 128), jnp.int32), ts=real(LENGTH, 128),
        act0=real(GROUPS + 2, LENGTH, 128), d0=real(GROUPS, LENGTH, 128),
        act1=real(GROUPS, LENGTH, 128), f1=real(GROUPS, LENGTH, 128), d1=real(GROUPS, LENGTH, 128),
        mis=real(GROUPS, LENGTH, 128), g1=real(GROUPS, LENGTH, 128),
        lhs=half(WIDE, 1152), lhs2=half(2 * WIDE, 1152), k2t=half(1152, PAIR), res=real(2 * WIDE, 256), qbuf=half(WIDE, 768), wq=half(768, 256),
        xall=half(8 * WIDE, 1152), gall=half(8 * WIDE, 256), fg=real(256, 1152), tacc=real(80, 128),
        colacc=real(LENGTH, 128), tiles=real(288, 256), colp=real(72, 128), rowg=real(8, 128),
        cbuf=real(REACH + 1, 8, 128), vbuf=real(2, 32, 128), arbuf=real(256, 128), pairbuf=real(128, 128), halfbuf=real(128, 128), rsbuf=real(LINE, PART, 128),
        bbuf=real(side, PART, 128), mine=real(PART, 128), gbuf=real(328, 128), loads=SEM((6,)),
        ss=SEM((AHEAD + 4,)), rs=SEM((AHEAD + 4,)), s1=SEM((REACH + 1,)), r1=SEM((REACH + 1,)),
        s2=SEM((LINE,)), r2=SEM((LINE,)), s3=SEM((side,)), r3=SEM((side,)), s4=SEM((LINE,)), r4=SEM((LINE,)), s5=SEM((2,)), r5=SEM((2,)),
    )
    red = pl.pallas_call(
        functools.partial(step_kernel, n),
        out_shape=shape(328, 128),
        in_specs=[hbm] * 6 + [vmem],
        out_specs=vmem,
        scratch_shapes=list(scratch.values()),
        compiler_params=pltpu.CompilerParams(
            collective_id=0, has_side_effects=True, vmem_limit_bytes=60 * 1024 * 1024
        ),
        name="step",
    )(features, row_t, col_t, target, k1, k2, ro)

    gfeat, grow, gcol, gone, gtwo, gread = pl.pallas_call(
        finish_kernel,
        out_shape=(shape(ROWS, 256), shape(32, 256), shape(32, 256), shape(288, 32), shape(288, 32), shape(1, 32)),
        in_specs=[vmem],
        out_specs=(vmem,) * 6,
        compiler_params=pltpu.CompilerParams(vmem_limit_bytes=4 * 1024 * 1024),
        name="finish",
    )(red)
    return gfeat, grow.T, gcol.T, gone.reshape(3, 3, PAIR, PAIR), gtwo.reshape(3, 3, PAIR, PAIR), gread.reshape(PAIR)


def solution(mesh):
    n = mesh.shape["diag"]
    in_specs = (P("diag", None), P(), P(), P(), P(), P(), P("diag", None))
    out_specs = (P("diag", None), P(), P(), P(), P(), P())
    return jax.shard_map(
        functools.partial(shards, n), mesh=mesh, in_specs=in_specs, out_specs=out_specs, check_vma=False
    )
```

```python
import functools
import math

import jax
import jax.numpy as jnp
from jax import lax
from jax.experimental import pallas as pl
from jax.experimental.pallas import tpu as pltpu
from jax.sharding import PartitionSpec as P

MESH = pl.DeviceIdType.MESH
F32, BF16 = jnp.float32, jnp.bfloat16

ROWS = 32
BAND = 256
PAIR = 32
HALO = 12
GROUPS = (ROWS + 2 * HALO) // 4
FIRST_OWN, LAST_OWN = 3, 10
PAD = 16
LENGTH = 352
WIDE, SPAN, CHUNK = 272, 264, 88
AHEAD = 9
REACH = 8
C0 = math.sqrt(2.0 / math.pi)
C1 = C0 * 0.044715
SIDE = 16
TOTAL = 256
SEM = pltpu.SemaphoreType.DMA


def iota(shape, dim):
    return lax.broadcasted_iota(jnp.int32, shape, dim)


def lane_block(rows):
    return lax.shift_right_logical(iota((rows, 128), 1), 5)


def gelu(x, with_slope):
    cubic = C1 * (x * x)
    s = 0.5 * jnp.tanh(x * (cubic + C0)) + 0.5
    value = x * s
    slope = s + value * (1.0 - s) * (6.0 * cubic + 2.0 * C0) if with_slope else None
    return value.astype(BF16).astype(F32), slope


def split(x):
    high = x.astype(BF16)
    return high, (x - high.astype(F32)).astype(BF16)


def fold(x):
    total = x[0:8]
    for i in range(1, x.shape[0] // 8):
        total = total + x[8 * i : 8 * i + 8]
    return total


def dot(a, b):
    return jnp.dot(a, b, preferred_element_type=F32)


def dot_t(a, b):
    return lax.dot_general(a, b, (((0,), (0,)), ((), ())), preferred_element_type=F32)


def dot_nt(a, b):
    return lax.dot_general(a, b, (((1,), (1,)), ((), ())), preferred_element_type=F32)


def repeater(lanes):
    return (jnp.bitwise_and(iota((PAIR, lanes), 1), 31) == iota((PAIR, lanes), 0)).astype(F32).astype(BF16)


def spread(block):
    turned = [block] + [pltpu.roll(block, 32 * s, 1) for s in (1, 2, 3)]
    where_block = lane_block(8)
    outs = []
    for b in range(4):
        value = turned[(3 - b) % 4]
        for other in range(3):
            value = jnp.where(where_block == other, turned[(other - b) % 4], value)
        outs.append(value)
    return outs


def step_kernel(
    n, feat_in, row_in, col_in, target_in, k1_in, k2_in, ro, red,
    feat, row_t, col_t, target, k1, k2,
    proj, sbuf, rbuf, tlow, thigh, roww, w1, wa, w2, rol, colr, mk, ts, act0, d0, act1, f1, d1, mis, g1,
    lhs, lhs2, k2t, res, qbuf, wq, xall, gall, fg, tacc, colacc, tiles, colp, rowg, cbuf, vbuf, arbuf, rsbuf, bbuf, mine, gbuf,
    loads, sems,
):
    me = lax.axis_index("diag")
    start = me * ROWS
    side = n // SIDE
    part = TOTAL // side
    pos = lax.rem(me, SIDE)
    plane = lax.div(me, SIDE)

    def dev(step):
        return lax.rem(me + step + n, n)

    def in_line(s):
        return me - pos + lax.rem(pos + s, SIDE)

    def across(s):
        return lax.rem(plane + s, side) * SIDE + pos

    fetches = [
        pltpu.make_async_copy(source, place, loads.at[i])
        for i, (source, place) in enumerate(
            ((feat_in, feat), (row_in, row_t), (col_in, col_t), (k1_in, k1), (k2_in, k2), (target_in, target))
        )
    ]
    for fetch in fetches:
        fetch.start()

    barrier = pltpu.get_barrier_semaphore()
    for step in range(1, AHEAD + 1):
        for target_device in (dev(step), dev(-step)):
            pl.semaphore_signal(barrier, inc=1, device_id=(target_device,), device_id_type=MESH)

    def greet(sign, s, carry):
        pl.semaphore_signal(barrier, inc=1, device_id=(me + sign * s,), device_id_type=MESH)
        return carry

    lax.fori_loop(AHEAD + 1, SIDE - pos, functools.partial(greet, 1), 0)
    lax.fori_loop(AHEAD + 1, pos + 1, functools.partial(greet, -1), 0)

    def greet_across(s, carry):
        pl.semaphore_signal(barrier, inc=1, device_id=(across(s),), device_id_type=MESH)
        return carry

    lax.fori_loop(1, side, greet_across, 0)

    for fetch in fetches[0:3]:
        fetch.wait()
    proj[...] = dot_nt(feat[...], jnp.concatenate([row_t[...]] * 4, axis=0))
    cc = dot_nt(feat[...], jnp.concatenate([col_t[...]] * 4, axis=0))
    where_block = lane_block(8)
    row_c = jnp.zeros((8, 128), F32)
    col_c = jnp.zeros((8, 128), F32)
    for b in range(4):
        row_c = jnp.where(where_block == b, proj[pl.ds(b, 8, stride=4), :], row_c)
        col_c = jnp.where(where_block == b, cc[8 * b : 8 * b + 8], col_c)
    sbuf[0:8] = col_c
    sbuf[8:16] = row_c
    greeted = jnp.maximum(SIDE - AHEAD - 1 - pos, 0) + jnp.maximum(pos - AHEAD, 0)
    pl.semaphore_wait(barrier, 2 * AHEAD + greeted + side - 1)
    gathers = []
    for slot, step in ((0, 1), (2, -1)):
        gathers.append(
            pltpu.make_async_remote_copy(sbuf, rbuf.at[slot], sems.at[0], sems.at[1], device_id=(dev(step),), device_id_type=MESH)
        )
    for m in range(3, AHEAD + 2):
        gathers.append(
            pltpu.make_async_remote_copy(
                sbuf.at[pl.ds(0, 8)], rbuf.at[m, pl.ds(0, 8)], sems.at[0], sems.at[1], device_id=(dev(1 - m),), device_id_type=MESH
            )
        )
    gathers.append(
        pltpu.make_async_remote_copy(
            target_in.at[pl.ds(24, 8)], tlow, sems.at[0], sems.at[1], device_id=(dev(1),), device_id_type=MESH
        )
    )
    gathers.append(
        pltpu.make_async_remote_copy(
            target_in.at[pl.ds(0, 8)], thigh, sems.at[0], sems.at[1], device_id=(dev(-1),), device_id_type=MESH
        )
    )
    for copy in gathers:
        copy.start()

    for fetch in fetches[3:6]:
        fetch.wait()
    rep8 = repeater(256)
    where_out = lax.shift_right_logical(iota((PAIR, 256), 1), 5)

    def build(weights, sign):
        for q in range(3):
            for place, ri in enumerate((8, 9, -2, -1, 0, 1, 2, 3, 4, 5, 6, 7)):
                value = jnp.zeros((PAIR, 256), F32)
                for p in range(3):
                    tap = 3 * p + q
                    ro_here = ri - sign * 2 * (p - 1)
                    if 0 <= ro_here < 8:
                        value = jnp.where(where_out == ro_here, tiles[32 * tap : 32 * tap + 32], value)
                row = (q * 12 + place) * 32
                weights[row : row + 32] = value.astype(BF16)

    tiles[...] = dot(k1[...], rep8)
    build(w1, 1)
    for tap in range(9):
        tiles[32 * tap : 32 * tap + 32] = dot_t(k1[32 * tap : 32 * tap + 32], rep8)
    build(wa, -1)
    ro8 = jnp.broadcast_to(ro[...].astype(F32), (8, PAIR)).astype(BF16)
    rol[...] = dot(ro8, repeater(128))
    for tap in range(9):
        for b in range(4):
            row = 128 * tap + 32 * b
            k2t[row : row + 32] = k2[32 * tap : 32 * tap + 32]
        w2[8 * tap : 8 * tap + 8] = dot_nt(ro8, k2t[128 * tap : 128 * tap + 128])
    gbuf[320:328] = rol[...]

    same = lax.shift_right_logical(iota((256, 256), 0), 5) == lax.shift_right_logical(iota((256, 256), 1), 5)
    ones = same.astype(F32).astype(BF16)
    wq[0:256] = ones
    wq[256:512] = ones
    act0[0] = jnp.zeros((LENGTH, 128), F32)
    act0[GROUPS + 1] = jnp.zeros((LENGTH, 128), F32)
    colacc[...] = jnp.zeros((LENGTH, 128), F32)
    tacc[...] = jnp.zeros((80, 128), F32)
    ts[...] = jnp.zeros((LENGTH, 128), F32)
    arbuf[224:256] = jnp.zeros((32, 128), F32)
    column = iota((LENGTH, 128), 0) - PAD
    mk[...] = jnp.where(column + (start - HALO) < n * ROWS, column - lane_block(LENGTH), 1 << 20)

    def all_of(place, sem):
        pltpu.make_async_copy(place, place, sem).wait()

    all_of(arbuf.at[pl.ds(0, 128)], sems.at[1])
    for m in range(AHEAD + 2):
        for b, value in enumerate(spread(col_c if m == 1 else rbuf[m, 0:8])):
            row = 32 * (m - 1) + 8 * b + HALO + PAD
            if row >= 0 and row + 8 <= LENGTH:
                colr[row : row + 8] = value
    roww[0:8] = rbuf[0, 8:16]
    roww[8:16] = row_c
    roww[16:24] = rbuf[2, 8:16]
    wide = jnp.concatenate([tlow[...], target[...], thigh[...]], axis=0)
    wide = jnp.concatenate([wide, jnp.zeros((48, 128), F32)], axis=1)
    wide = jnp.concatenate([wide, jnp.zeros((80, 384), F32)], axis=0)
    sheared = pltpu.roll(wide, 0, 1, stride=1, stride_axis=0)
    ts[4 + PAD : 4 + PAD + 312] = sheared.T[0:312]

    def first_column(u):
        return pl.multiple_of(8 * lax.shift_right_logical(u, 1), 8)

    def mask_at(u, row, count):
        shift = 4 * u - jnp.where(start + 4 * u - HALO >= 0, 0, 1 << 20)
        return jnp.bitwise_and(mk[pl.ds(row, count), :] - shift, -BAND) == 0

    def clear_sides(buffer, index, base):
        buffer[index, pl.ds(base, 16), :] = jnp.zeros((16, 128), F32)
        buffer[index, pl.ds(base + PAD + SPAN, 24), :] = jnp.zeros((24, 128), F32)

    left = lane_block(WIDE) < 2

    def pieces(buffer, index, row):
        ends = jnp.where(left, buffer[index + 3, pl.ds(row, WIDE), :], buffer[index, pl.ds(row, WIDE), :])
        return ends, buffer[index + 1, pl.ds(row, WIDE), :], buffer[index + 2, pl.ds(row, WIDE), :]

    def make_field(with_slope, v):
        base = pl.multiple_of(8 * v, 8)
        for h in range(2):
            u = 2 * v + h
            clear_sides(act0, u + 1, base)
            row_here = roww[pl.ds(u + 5, 1), :]
            for ch in range(3):
                row = base + PAD + CHUNK * ch
                mask = mask_at(u, row, CHUNK)
                x = jnp.where(mask, row_here + colr[pl.ds(row, CHUNK), :], 0.0)
                act, slope = gelu(x, with_slope)
                act0[u + 1, pl.ds(row, CHUNK), :] = act
                if with_slope:
                    d0[u, pl.ds(row, CHUNK), :] = jnp.where(mask, slope, 0.0)

    def conv_operand(v):
        base = pl.multiple_of(8 * v, 8)
        for q in range(3):
            for d, piece in enumerate(pieces(act0, 2 * v, base + PAD + 2 * (q - 1))):
                lhs[:, 128 * (3 * q + d) : 128 * (3 * q + d + 1)] = piece.astype(BF16)

    def conv():
        res[0:WIDE] = dot(lhs[...], w1[...])

    def conv_result(with_slope, v):
        base = pl.multiple_of(8 * v, 8)
        for h in range(2):
            u = 2 * v + h
            clear_sides(act1, u, base)
            clear_sides(f1, u, base)
            row_here = roww[pl.ds(u + 5, 1), :]
            for ch in range(3):
                row = base + PAD + CHUNK * ch
                added = res[CHUNK * ch : CHUNK * ch + CHUNK, 128 * h : 128 * h + 128]
                mask = mask_at(u, row, CHUNK)
                x = jnp.where(mask, (row_here + colr[pl.ds(row, CHUNK), :]) + added, 0.0)
                act, slope = gelu(x, with_slope)
                act1[u, pl.ds(row, CHUNK), :] = act
                f1[u, pl.ds(row, CHUNK), :] = x
                if with_slope:
                    d1[u, pl.ds(row, CHUNK), :] = jnp.where(mask, slope, 0.0)

    make_field(False, 0)
    make_field(True, 1)
    conv_operand(0)
    make_field(True, 2)
    conv()

    def first_conv(with_field, v, carry):
        conv_operand(v)
        conv_result(True, v - 1)
        if with_field:
            make_field(True, v + 2)
        conv()
        return carry

    lax.fori_loop(1, 5, functools.partial(first_conv, True), 0)
    lax.fori_loop(5, 7, functools.partial(first_conv, False), 0)
    conv_result(False, 6)

    def make_misfit(w, carry):
        base = pl.multiple_of(8 * w, 8)
        for at, count in ((0, 96), (96, 96), (192, 80)):
            row = base + PAD + at
            for h in range(2):
                u = 2 * w + 1 + h
                value = rol[0:1] * f1[u, pl.ds(row, count), :]
                for p in range(3):
                    for q in range(3):
                        tap = 3 * p + q
                        value = value + w2[8 * tap : 8 * tap + 1] * act1[u + p - 1, pl.ds(row + 4 * (q - 1), count), :]
                high, low = split(value)
                qbuf[at : at + count, 128 * h : 128 * h + 128] = high
                qbuf[at : at + count, 256 + 128 * h : 384 + 128 * h] = low
            high, low = split(ts[pl.ds(row, count), :])
            qbuf[at : at + count, 512:640] = high
            qbuf[at : at + count, 640:768] = low
        pick = jnp.where(iota((128, 256), 0) == 8 * w + lax.shift_right_logical(iota((128, 256), 1), 5), -1.0, 0.0).astype(BF16)
        wq[512:640] = pick
        wq[640:768] = pick
        value = dot(qbuf[...], wq[...]) * (1.0 / BAND)
        for h in range(2):
            u = 2 * w + 1 + h
            clear_sides(mis, u, base)
            for at, count in ((0, 96), (96, 96), (192, 80)):
                row = base + PAD + at
                mis[u, pl.ds(row, count), :] = jnp.where(
                    mask_at(u, row, count), value[at : at + count, 128 * h : 128 * h + 128], 0.0
                )
        return carry

    lax.fori_loop(0, 6, make_misfit, 0)

    def make_cotangent(u, carry):
        base = first_column(u)
        clear_sides(g1, u, base)
        sums = [None] * 10
        for ch in range(3):
            row = base + PAD + CHUNK * ch
            act = act1[u, pl.ds(row, CHUNK), :]
            back = None
            for p in range(3):
                for q in range(3):
                    tap = 3 * p + q
                    m = mis[u - (p - 1), pl.ds(row - 4 * (q - 1), CHUNK), :]
                    term = w2[8 * tap : 8 * tap + 1] * m
                    back = term if back is None else back + term
                    part = fold(act * m)
                    sums[tap] = part if sums[tap] is None else sums[tap] + part
            m = mis[u, pl.ds(row, CHUNK), :]
            part = fold(m * f1[u, pl.ds(row, CHUNK), :])
            sums[9] = part if sums[9] is None else sums[9] + part
            g1[u, pl.ds(row, CHUNK), :] = rol[0:1] * m + d1[u, pl.ds(row, CHUNK), :] * back
        for tap in range(10):
            source = u - (tap // 3 - 1) if tap < 9 else u
            own = jnp.logical_and(source >= FIRST_OWN, source <= LAST_OWN)
            tacc[8 * tap : 8 * tap + 8] += jnp.where(own, sums[tap], 0.0)
        return carry

    lax.fori_loop(2, GROUPS - 2, make_cotangent, 0)

    def adjoint_operand(w):
        base = pl.multiple_of(8 * w + 8, 8)
        for q in range(3):
            for d, piece in enumerate(pieces(g1, 2 * w + 2, base + PAD - 2 * (q - 1))):
                high, low = split(piece)
                lanes = slice(128 * (3 * q + d), 128 * (3 * q + d + 1))
                lhs2[0:WIDE, lanes] = high
                lhs2[WIDE : 2 * WIDE, lanes] = low

    def adjoint():
        res[...] = dot(lhs2[...], wa[...])

    def adjoint_result(w):
        base = pl.multiple_of(8 * w + 8, 8)
        for h in range(2):
            u = 2 * w + 3 + h
            total_row = None
            for ch in range(3):
                at = CHUNK * ch + 8 * h
                row = base + PAD + at
                lanes = slice(128 * h, 128 * h + 128)
                back = res[at : at + CHUNK, lanes] + res[WIDE + at : WIDE + at + CHUNK, lanes]
                value = g1[u, pl.ds(row, CHUNK), :] + d0[u, pl.ds(row, CHUNK), :] * back
                colacc[pl.ds(row, CHUNK), :] += value
                part = fold(value)
                total_row = part if total_row is None else total_row + part
            rowg[pl.ds(u - 3, 1), :] = jnp.sum(total_row, axis=0, keepdims=True)

    def collect(w):
        for h in range(2):
            u = 2 * w + 3 + h
            base = pl.multiple_of(8 * w + 8 + 8 * h, 8)
            at = pl.multiple_of(WIDE * (2 * w + h), 16)
            high, low = split(g1[u, pl.ds(base + PAD, WIDE), :])
            gall[pl.ds(at, WIDE), 0:128] = high
            gall[pl.ds(at, WIDE), 128:256] = low
            for q in range(3):
                row = base + PAD + 2 * (q - 1)
                ends = jnp.where(left, act0[u + 2, pl.ds(row, WIDE), :], act0[u, pl.ds(row, WIDE), :])
                xall[pl.ds(at, WIDE), 256 * q : 256 * q + 128] = ends.astype(BF16)
                xall[pl.ds(at, WIDE), 256 * q + 128 : 256 * q + 256] = act0[u + 1, pl.ds(row, WIDE), :].astype(BF16)

    adjoint_operand(0)
    collect(0)
    adjoint()

    def first_adjoint(w, carry):
        adjoint_operand(w)
        adjoint_result(w - 1)
        collect(w)
        adjoint()
        return carry

    lax.fori_loop(1, 4, first_adjoint, 0)
    adjoint_result(3)

    where_block = lane_block(8)
    for m in range(REACH + 1):
        packed = jnp.zeros((8, 128), F32)
        for b in range(4):
            row = 32 * m + 8 * b + HALO + PAD
            value = colacc[row : row + 8]
            value = value + pltpu.roll(value, 64, 1)
            value = value + pltpu.roll(value, 32, 1)
            packed = jnp.where(where_block == b, value, packed)
        colp[8 * m : 8 * m + 8] = packed
    columns = []
    for m in range(1, REACH + 1):
        columns.append(
            pltpu.make_async_remote_copy(
                colp.at[pl.ds(8 * m, 8)], cbuf.at[m - 1], sems.at[2], sems.at[3], device_id=(dev(m),), device_id_type=MESH
            )
        )
    for copy in columns:
        copy.start()

    fg[...] = dot_t(gall[...], xall[...])

    where_block = lane_block(32)
    for group in range(3):
        packed = jnp.zeros((32, 128), F32)
        for place in range(4):
            tap = 4 * group + place
            if tap > 8:
                continue
            p, q = tap // 3 - 1, tap % 3
            value = jnp.zeros((32, 128), F32)
            for b in range(4):
                source = b + 2 * p
                lanes = 256 * q + (128 if 0 <= source < 4 else 0)
                both = fg[32 * b : 32 * b + 32, lanes : lanes + 128] + fg[128 + 32 * b : 160 + 32 * b, lanes : lanes + 128]
                value = value + jnp.where(where_block == source % 4, both, 0.0)
            value = value + pltpu.roll(value, 64, 1)
            value = value + pltpu.roll(value, 32, 1)
            packed = jnp.where(where_block == place, value, packed)
        arbuf[128 + 32 * group : 160 + 32 * group] = packed
    for tap in range(10):
        arbuf[224 + tap : 225 + tap] = jnp.sum(tacc[8 * tap : 8 * tap + 8], axis=0, keepdims=True)
    sums = arbuf[224:240]
    sums = sums + pltpu.roll(sums, 64, 1)
    arbuf[224:240] = sums + pltpu.roll(sums, 32, 1)
    high, low = split(jnp.concatenate([tacc[8 * tap : 8 * tap + 8] for tap in range(9)], axis=1))
    by_read = jnp.sum(dot(high, k2t[...]) + dot(low, k2t[...]), axis=0, keepdims=True)
    arbuf[233:234, 0:32] = arbuf[233:234, 0:32] + by_read

    where_block = lane_block(8)
    rows = rowg[...]
    for b in range(4):
        vbuf[1, pl.ds(b, 8, stride=4), :] = jnp.where(where_block == 1, pltpu.roll(rows, (32 - 32 * b) % 128, 1) if b != 1 else rows, 0.0)
    all_of(arbuf.at[pl.ds(0, 128)], sems.at[0])
    all_of(cbuf, sems.at[3])
    all_of(cbuf, sems.at[2])
    own = colp[0:8]
    for m in range(1, REACH + 1):
        own = own + cbuf[m - 1]
    for b in range(4):
        vbuf[0, 8 * b : 8 * b + 8] = jnp.where(where_block == 0, pltpu.roll(own, (128 - 32 * b) % 128, 1) if b else own, 0.0)
    both = vbuf[0] + vbuf[1]
    high, low = split(both)
    by_feature = dot_t(jnp.concatenate([high, low], axis=0), jnp.concatenate([feat[...]] * 2, axis=0))
    arbuf[0:64] = by_feature[0:64, 0:128]
    arbuf[64:128] = by_feature[0:64, 128:256]

    def chunk(q):
        return pl.ds(pl.multiple_of(q * part, part), part)

    def send(source, place, at, device):
        pltpu.make_async_remote_copy(
            source, place, sems.at[at], sems.at[at + 1], device_id=(device,), device_id_type=MESH
        ).start()

    for s in range(1, side):
        send(arbuf.at[chunk(lax.rem(plane + s, side))], rsbuf.at[s - 1], 4, across(s))
    weights = jnp.concatenate([col_t[...], row_t[...]], axis=0)
    by_bin = dot(high[:, 0:64], weights) + dot(low[:, 0:64], weights)
    gbuf[256:288] = by_bin[:, 0:128]
    gbuf[288:320] = by_bin[:, 128:256]
    all_of(rsbuf, sems.at[5])
    total = arbuf[chunk(plane), :]
    for s in range(1, side):
        total = total + rsbuf[s - 1]
    mine[...] = total
    bbuf[pos] = total
    for s in range(1, SIDE):
        send(mine, bbuf.at[pos], 6, in_line(s))
    all_of(rsbuf, sems.at[4])
    all_of(bbuf.at[pl.ds(0, SIDE - 1)], sems.at[7])
    total = bbuf[0]
    for q in range(1, SIDE):
        total = total + bbuf[q]
    gbuf[chunk(plane), :] = total
    for s in range(1, side):
        send(gbuf.at[chunk(plane)], gbuf.at[chunk(plane)], 8, across(s))
    all_of(bbuf.at[pl.ds(0, SIDE - 1)], sems.at[6])
    all_of(rsbuf, sems.at[9])
    all_of(rsbuf, sems.at[8])
    red[...] = gbuf[...]


def finish_kernel(red, gfeat, grow, gcol, gone, gtwo, gread):
    gfeat[:, 0:128] = red[256:288]
    gfeat[:, 128:256] = red[288:320]
    gcol[:, 0:128] = red[0:32]
    gcol[:, 128:256] = red[64:96]
    grow[:, 0:128] = red[32:64]
    grow[:, 128:256] = red[96:128]
    for group in range(3):
        block = red[128 + 32 * group : 160 + 32 * group].T
        count = 128 if group < 2 else 32
        gone[128 * group : 128 * group + count] = block[0:count]
    by_channel = red[224:240].T
    read = red[320:321, 0:32]
    for tap in range(9):
        gtwo[32 * tap : 32 * tap + 32] = by_channel[0:32, tap : tap + 1] * read
    gread[...] = red[233:234, 0:32]


def shards(n, features, row_proj, col_proj, first_filter, second_filter, readout, target):
    side = n // SIDE
    part = TOTAL // side
    vmem = pl.BlockSpec(memory_space=pltpu.VMEM)

    def shape(*dims):
        return jax.ShapeDtypeStruct(dims, F32)

    def real(*dims):
        return pltpu.VMEM(dims, F32)

    def half(*dims):
        return pltpu.VMEM(dims, BF16)

    k1 = first_filter.reshape(9 * PAIR, PAIR)
    k2 = second_filter.reshape(9 * PAIR, PAIR)
    ro = readout.reshape(1, PAIR)
    row_t, col_t = row_proj.T, col_proj.T
    hbm = pl.BlockSpec(memory_space=pltpu.HBM)
    scratch = dict(
        feat=half(ROWS, 256), row_t=half(PAIR, 256), col_t=half(PAIR, 256), target=real(ROWS, 256), k1=half(288, PAIR), k2=half(288, PAIR),
        proj=real(32, 128), sbuf=real(16, 128), rbuf=real(AHEAD + 2, 16, 128), tlow=real(8, 256), thigh=real(8, 256),
        roww=real(24, 128), w1=half(1152, 256), wa=half(1152, 256), w2=real(72, 128), rol=real(8, 128),
        colr=real(LENGTH, 128), mk=pltpu.VMEM((LENGTH, 128), jnp.int32), ts=real(LENGTH, 128),
        act0=real(GROUPS + 2, LENGTH, 128), d0=real(GROUPS, LENGTH, 128),
        act1=real(GROUPS, LENGTH, 128), f1=real(GROUPS, LENGTH, 128), d1=real(GROUPS, LENGTH, 128),
        mis=real(GROUPS, LENGTH, 128), g1=real(GROUPS, LENGTH, 128),
        lhs=half(WIDE, 1152), lhs2=half(2 * WIDE, 1152), k2t=half(1152, PAIR), res=real(2 * WIDE, 256), qbuf=half(WIDE, 768), wq=half(768, 256),
        xall=half(8 * WIDE, 768), gall=half(8 * WIDE, 256), fg=real(256, 768), tacc=real(80, 128),
        colacc=real(LENGTH, 128), tiles=real(288, 256), colp=real(72, 128), rowg=real(8, 128),
        cbuf=real(REACH, 8, 128), vbuf=real(2, 32, 128), arbuf=real(256, 128), rsbuf=real(side - 1, part, 128),
        bbuf=real(SIDE, part, 128), mine=real(part, 128), gbuf=real(328, 128), loads=SEM((6,)), sems=SEM((10,)),
    )
    red = pl.pallas_call(
        functools.partial(step_kernel, n),
        out_shape=shape(328, 128),
        in_specs=[hbm] * 6 + [vmem],
        out_specs=vmem,
        scratch_shapes=list(scratch.values()),
        compiler_params=pltpu.CompilerParams(
            collective_id=0, has_side_effects=True, vmem_limit_bytes=60 * 1024 * 1024
        ),
        name="step",
    )(features, row_t, col_t, target, k1, k2, ro)

    gfeat, grow, gcol, gone, gtwo, gread = pl.pallas_call(
        finish_kernel,
        out_shape=(shape(ROWS, 256), shape(32, 256), shape(32, 256), shape(288, 32), shape(288, 32), shape(1, 32)),
        in_specs=[vmem],
        out_specs=(vmem,) * 6,
        compiler_params=pltpu.CompilerParams(vmem_limit_bytes=4 * 1024 * 1024),
        name="finish",
    )(red)
    return gfeat, grow.T, gcol.T, gone.reshape(3, 3, PAIR, PAIR), gtwo.reshape(3, 3, PAIR, PAIR), gread.reshape(PAIR)


def solution(mesh):
    n = mesh.shape["diag"]
    in_specs = (P("diag", None), P(), P(), P(), P(), P(), P("diag", None))
    out_specs = (P("diag", None), P(), P(), P(), P(), P())
    return jax.shard_map(
        functools.partial(shards, n), mesh=mesh, in_specs=in_specs, out_specs=out_specs, check_vma=False
    )
```

```python
import functools
import math

import jax
import jax.numpy as jnp
from jax import lax
from jax.experimental import pallas as pl
from jax.experimental.pallas import tpu as pltpu
from jax.sharding import PartitionSpec as P

MESH = pl.DeviceIdType.MESH
F32, BF16 = jnp.float32, jnp.bfloat16

ROWS = 32
BAND = 256
PAIR = 32
HALO = 12
GROUPS = (ROWS + 2 * HALO) // 4
FIRST_OWN, LAST_OWN = 3, 10
PAD = 16
LENGTH = 352
WIDE, SPAN, CHUNK = 272, 264, 88
AHEAD = 9
REACH = 8
C0 = math.sqrt(2.0 / math.pi)
C1 = C0 * 0.044715
SIDE = 16
TOTAL = 256
SEM = pltpu.SemaphoreType.DMA


def iota(shape, dim):
    return lax.broadcasted_iota(jnp.int32, shape, dim)


def lane_block(rows):
    return lax.shift_right_logical(iota((rows, 128), 1), 5)


def gelu(x):
    cubic = C1 * (x * x)
    s = 0.5 * jnp.tanh(x * (cubic + C0)) + 0.5
    value = x * s
    slope = s + value * (1.0 - s) * (6.0 * cubic + 2.0 * C0)
    return value.astype(BF16).astype(F32), slope


def split(x):
    high = x.astype(BF16)
    return high, (x - high.astype(F32)).astype(BF16)


def fold(x):
    total = x[0:8]
    for i in range(1, x.shape[0] // 8):
        total = total + x[8 * i : 8 * i + 8]
    return total


def dot(a, b):
    return jnp.dot(a, b, preferred_element_type=F32)


def dot_t(a, b):
    return lax.dot_general(a, b, (((0,), (0,)), ((), ())), preferred_element_type=F32)


def dot_nt(a, b):
    return lax.dot_general(a, b, (((1,), (1,)), ((), ())), preferred_element_type=F32)


def repeater(lanes):
    return (jnp.bitwise_and(iota((PAIR, lanes), 1), 31) == iota((PAIR, lanes), 0)).astype(F32).astype(BF16)


def spread(block):
    turned = [block] + [pltpu.roll(block, 32 * s, 1) for s in (1, 2, 3)]
    where_block = lane_block(8)
    outs = []
    for b in range(4):
        value = turned[(3 - b) % 4]
        for other in range(3):
            value = jnp.where(where_block == other, turned[(other - b) % 4], value)
        outs.append(value)
    return outs


def step_kernel(
    n, feat_in, row_in, col_in, target_in, k1_in, k2_in, ro, red,
    feat, row_t, col_t, target, k1, k2,
    proj, sbuf, rbuf, tlow, thigh, roww, w1, wa, w2, rol, colr, mk, ts, act0, d0, act1, f1, d1, mis, g1,
    lhs, lhs2, k2t, res, qbuf, wq, xall, gall, galt, fg, tacc, colacc, tiles, colp, rowg, cbuf, vbuf, arbuf, rsbuf, bbuf, mine, gbuf,
    loads, sems,
):
    me = lax.axis_index("diag")
    start = me * ROWS
    side = n // SIDE
    part = TOTAL // side
    pos = lax.rem(me, SIDE)
    plane = lax.div(me, SIDE)

    def dev(step):
        return lax.rem(me + step + n, n)

    def in_line(s):
        return me - pos + lax.rem(pos + s, SIDE)

    def across(s):
        return lax.rem(plane + s, side) * SIDE + pos

    fetches = [
        pltpu.make_async_copy(source, place, loads.at[i])
        for i, (source, place) in enumerate(
            ((feat_in, feat), (row_in, row_t), (col_in, col_t), (k1_in, k1), (k2_in, k2), (target_in, target))
        )
    ]
    for fetch in fetches:
        fetch.start()

    barrier = pltpu.get_barrier_semaphore()
    for step in range(1, AHEAD + 1):
        for target_device in (dev(step), dev(-step)):
            pl.semaphore_signal(barrier, inc=1, device_id=(target_device,), device_id_type=MESH)

    def greet(sign, s, carry):
        pl.semaphore_signal(barrier, inc=1, device_id=(me + sign * s,), device_id_type=MESH)
        return carry

    lax.fori_loop(AHEAD + 1, SIDE - pos, functools.partial(greet, 1), 0)
    lax.fori_loop(AHEAD + 1, pos + 1, functools.partial(greet, -1), 0)

    def greet_across(s, carry):
        pl.semaphore_signal(barrier, inc=1, device_id=(across(s),), device_id_type=MESH)
        return carry

    lax.fori_loop(1, side, greet_across, 0)

    for fetch in fetches[0:3]:
        fetch.wait()
    proj[...] = dot_nt(feat[...], jnp.concatenate([row_t[...]] * 4, axis=0))
    cc = dot_nt(feat[...], jnp.concatenate([col_t[...]] * 4, axis=0))
    where_block = lane_block(8)
    row_c = jnp.zeros((8, 128), F32)
    col_c = jnp.zeros((8, 128), F32)
    for b in range(4):
        row_c = jnp.where(where_block == b, proj[pl.ds(b, 8, stride=4), :], row_c)
        col_c = jnp.where(where_block == b, cc[8 * b : 8 * b + 8], col_c)
    sbuf[0:8] = col_c
    sbuf[8:16] = row_c
    greeted = jnp.maximum(SIDE - AHEAD - 1 - pos, 0) + jnp.maximum(pos - AHEAD, 0)
    pl.semaphore_wait(barrier, 2 * AHEAD + greeted + side - 1)
    gathers = []
    for slot, step in ((0, 1), (2, -1)):
        gathers.append(
            pltpu.make_async_remote_copy(sbuf, rbuf.at[slot], sems.at[0], sems.at[1], device_id=(dev(step),), device_id_type=MESH)
        )
    for m in range(3, AHEAD + 2):
        gathers.append(
            pltpu.make_async_remote_copy(
                sbuf.at[pl.ds(0, 8)], rbuf.at[m, pl.ds(0, 8)], sems.at[0], sems.at[1], device_id=(dev(1 - m),), device_id_type=MESH
            )
        )
    gathers.append(
        pltpu.make_async_remote_copy(
            target_in.at[pl.ds(24, 8)], tlow, sems.at[0], sems.at[1], device_id=(dev(1),), device_id_type=MESH
        )
    )
    gathers.append(
        pltpu.make_async_remote_copy(
            target_in.at[pl.ds(0, 8)], thigh, sems.at[0], sems.at[1], device_id=(dev(-1),), device_id_type=MESH
        )
    )
    for copy in gathers:
        copy.start()

    for fetch in fetches[3:6]:
        fetch.wait()
    rep8 = repeater(256)
    where_out = lax.shift_right_logical(iota((PAIR, 256), 1), 5)

    def build(weights, sign):
        for q in range(3):
            for place, ri in enumerate((8, 9, -2, -1, 0, 1, 2, 3, 4, 5, 6, 7)):
                value = jnp.zeros((PAIR, 256), F32)
                for p in range(3):
                    tap = 3 * p + q
                    ro_here = ri - sign * 2 * (p - 1)
                    if 0 <= ro_here < 8:
                        value = jnp.where(where_out == ro_here, tiles[32 * tap : 32 * tap + 32], value)
                row = (q * 12 + place) * 32
                weights[row : row + 32] = value.astype(BF16)

    tiles[...] = dot(k1[...], rep8)
    build(w1, 1)
    tiles[...] = dot_t(jnp.concatenate([k1[32 * tap : 32 * tap + 32] for tap in range(9)], axis=1), rep8)
    build(wa, -1)
    ro8 = jnp.broadcast_to(ro[...].astype(F32), (8, PAIR)).astype(BF16)
    rol[...] = dot(ro8, repeater(128))
    for tap in range(9):
        for b in range(4):
            row = 128 * tap + 32 * b
            k2t[row : row + 32] = k2[32 * tap : 32 * tap + 32]
        w2[8 * tap : 8 * tap + 8] = dot_nt(ro8, k2t[128 * tap : 128 * tap + 128])
    gbuf[320:328] = rol[...]

    same = lax.shift_right_logical(iota((256, 256), 0), 5) == lax.shift_right_logical(iota((256, 256), 1), 5)
    ones = same.astype(F32).astype(BF16)
    wq[0:256] = ones
    wq[256:512] = ones
    act0[0] = jnp.zeros((LENGTH, 128), F32)
    act0[GROUPS + 1] = jnp.zeros((LENGTH, 128), F32)
    colacc[...] = jnp.zeros((LENGTH, 128), F32)
    tacc[...] = jnp.zeros((80, 128), F32)
    ts[...] = jnp.zeros((LENGTH, 128), F32)
    arbuf[224:256] = jnp.zeros((32, 128), F32)
    column = iota((LENGTH, 128), 0) - PAD
    mk[...] = jnp.where(column + (start - HALO) < n * ROWS, column - lane_block(LENGTH), 1 << 20)

    def all_of(place, sem):
        pltpu.make_async_copy(place, place, sem).wait()

    all_of(arbuf.at[pl.ds(0, 128)], sems.at[1])
    for m in range(AHEAD + 2):
        for b, value in enumerate(spread(col_c if m == 1 else rbuf[m, 0:8])):
            row = 32 * (m - 1) + 8 * b + HALO + PAD
            if row >= 0 and row + 8 <= LENGTH:
                colr[row : row + 8] = value
    roww[0:8] = rbuf[0, 8:16]
    roww[8:16] = row_c
    roww[16:24] = rbuf[2, 8:16]
    wide = jnp.concatenate([tlow[...], target[...], thigh[...]], axis=0)
    wide = jnp.concatenate([wide, jnp.zeros((48, 128), F32)], axis=1)
    wide = jnp.concatenate([wide, jnp.zeros((80, 384), F32)], axis=0)
    sheared = pltpu.roll(wide, 0, 1, stride=1, stride_axis=0)
    ts[4 + PAD : 4 + PAD + 312] = sheared.T[0:312]

    def first_column(u):
        return pl.multiple_of(8 * lax.shift_right_logical(u, 1), 8)

    def mask_at(u, row, count):
        shift = 4 * u - jnp.where(start + 4 * u - HALO >= 0, 0, 1 << 20)
        return jnp.bitwise_and(mk[pl.ds(row, count), :] - shift, -BAND) == 0

    def clear_sides(buffer, index, base):
        buffer[index, pl.ds(base, 16), :] = jnp.zeros((16, 128), F32)
        buffer[index, pl.ds(base + PAD + SPAN, 24), :] = jnp.zeros((24, 128), F32)

    left = lane_block(WIDE) < 2

    def pieces(buffer, index, row):
        ends = jnp.where(left, buffer[index + 3, pl.ds(row, WIDE), :], buffer[index, pl.ds(row, WIDE), :])
        return ends, buffer[index + 1, pl.ds(row, WIDE), :], buffer[index + 2, pl.ds(row, WIDE), :]

    def make_field(v):
        base = pl.multiple_of(8 * v, 8)
        for h in range(2):
            u = 2 * v + h
            clear_sides(act0, u + 1, base)
            row_here = roww[pl.ds(u + 5, 1), :]
            for ch in range(3):
                row = base + PAD + CHUNK * ch
                mask = mask_at(u, row, CHUNK)
                x = jnp.where(mask, row_here + colr[pl.ds(row, CHUNK), :], 0.0)
                act, slope = gelu(x)
                act0[u + 1, pl.ds(row, CHUNK), :] = act
                d0[u, pl.ds(row, CHUNK), :] = jnp.where(mask, slope, 0.0)

    def conv_operand(v):
        base = pl.multiple_of(8 * v, 8)
        for q in range(3):
            for d, piece in enumerate(pieces(act0, 2 * v, base + PAD + 2 * (q - 1))):
                lhs[:, 128 * (3 * q + d) : 128 * (3 * q + d + 1)] = piece.astype(BF16)

    def conv():
        res[0:WIDE] = dot(lhs[...], w1[...])

    def conv_result(v):
        base = pl.multiple_of(8 * v, 8)
        for h in range(2):
            u = 2 * v + h
            clear_sides(act1, u, base)
            clear_sides(f1, u, base)
            row_here = roww[pl.ds(u + 5, 1), :]
            for ch in range(3):
                row = base + PAD + CHUNK * ch
                added = res[CHUNK * ch : CHUNK * ch + CHUNK, 128 * h : 128 * h + 128]
                mask = mask_at(u, row, CHUNK)
                x = jnp.where(mask, (row_here + colr[pl.ds(row, CHUNK), :]) + added, 0.0)
                act, slope = gelu(x)
                act1[u, pl.ds(row, CHUNK), :] = act
                f1[u, pl.ds(row, CHUNK), :] = x
                d1[u, pl.ds(row, CHUNK), :] = jnp.where(mask, slope, 0.0)

    def fields(v, carry):
        make_field(v)
        return carry

    lax.fori_loop(0, GROUPS // 2, fields, 0)

    def first_conv(v, carry):
        conv_operand(v)
        conv()
        conv_result(v)
        return carry

    lax.fori_loop(0, GROUPS // 2, first_conv, 0)

    def make_misfit(w, carry):
        base = pl.multiple_of(8 * w, 8)
        for at, count in ((0, 96), (96, 96), (192, 80)):
            row = base + PAD + at
            for h in range(2):
                u = 2 * w + 1 + h
                value = rol[0:1] * f1[u, pl.ds(row, count), :]
                for p in range(3):
                    for q in range(3):
                        tap = 3 * p + q
                        value = value + w2[8 * tap : 8 * tap + 1] * act1[u + p - 1, pl.ds(row + 4 * (q - 1), count), :]
                high, low = split(value)
                qbuf[at : at + count, 128 * h : 128 * h + 128] = high
                qbuf[at : at + count, 256 + 128 * h : 384 + 128 * h] = low
            high, low = split(ts[pl.ds(row, count), :])
            qbuf[at : at + count, 512:640] = high
            qbuf[at : at + count, 640:768] = low
        pick = jnp.where(iota((128, 256), 0) == 8 * w + lax.shift_right_logical(iota((128, 256), 1), 5), -1.0, 0.0).astype(BF16)
        wq[512:640] = pick
        wq[640:768] = pick
        value = dot(qbuf[...], wq[...]) * (1.0 / BAND)
        for h in range(2):
            u = 2 * w + 1 + h
            clear_sides(mis, u, base)
            for at, count in ((0, 96), (96, 96), (192, 80)):
                row = base + PAD + at
                mis[u, pl.ds(row, count), :] = jnp.where(
                    mask_at(u, row, count), value[at : at + count, 128 * h : 128 * h + 128], 0.0
                )
        return carry

    lax.fori_loop(0, 6, make_misfit, 0)

    def make_cotangent(u, carry):
        base = first_column(u)
        clear_sides(g1, u, base)
        sums = [None] * 10
        for ch in range(3):
            row = base + PAD + CHUNK * ch
            act = act1[u, pl.ds(row, CHUNK), :]
            back = None
            for p in range(3):
                for q in range(3):
                    tap = 3 * p + q
                    m = mis[u - (p - 1), pl.ds(row - 4 * (q - 1), CHUNK), :]
                    term = w2[8 * tap : 8 * tap + 1] * m
                    back = term if back is None else back + term
                    part = fold(act * m)
                    sums[tap] = part if sums[tap] is None else sums[tap] + part
            m = mis[u, pl.ds(row, CHUNK), :]
            part = fold(m * f1[u, pl.ds(row, CHUNK), :])
            sums[9] = part if sums[9] is None else sums[9] + part
            g1[u, pl.ds(row, CHUNK), :] = rol[0:1] * m + d1[u, pl.ds(row, CHUNK), :] * back
        for tap in range(10):
            source = u - (tap // 3 - 1) if tap < 9 else u
            own = jnp.logical_and(source >= FIRST_OWN, source <= LAST_OWN)
            tacc[8 * tap : 8 * tap + 8] += jnp.where(own, sums[tap], 0.0)
        return carry

    lax.fori_loop(2, GROUPS - 2, make_cotangent, 0)

    def adjoint_operand(w):
        base = pl.multiple_of(8 * w + 8, 8)
        for q in range(3):
            for d, piece in enumerate(pieces(g1, 2 * w + 2, base + PAD - 2 * (q - 1))):
                high, low = split(piece)
                lanes = slice(128 * (3 * q + d), 128 * (3 * q + d + 1))
                lhs2[0:WIDE, lanes] = high
                lhs2[WIDE : 2 * WIDE, lanes] = low

    def adjoint():
        res[...] = dot(lhs2[...], wa[...])

    def adjoint_result(w):
        base = pl.multiple_of(8 * w + 8, 8)
        for h in range(2):
            u = 2 * w + 3 + h
            total_row = None
            for ch in range(3):
                at = CHUNK * ch + 8 * h
                row = base + PAD + at
                lanes = slice(128 * h, 128 * h + 128)
                back = res[at : at + CHUNK, lanes] + res[WIDE + at : WIDE + at + CHUNK, lanes]
                value = g1[u, pl.ds(row, CHUNK), :] + d0[u, pl.ds(row, CHUNK), :] * back
                colacc[pl.ds(row, CHUNK), :] += value
                part = fold(value)
                total_row = part if total_row is None else total_row + part
            rowg[pl.ds(u - 3, 1), :] = jnp.sum(total_row, axis=0, keepdims=True)

    def collect(w):
        for h in range(2):
            u = 2 * w + 3 + h
            base = pl.multiple_of(8 * w + 8 + 8 * h, 8)
            at = pl.multiple_of(WIDE * (2 * w + h), 16)
            high, low = split(g1[u, pl.ds(base + PAD, WIDE), :])
            gall[pl.ds(at, WIDE), 0:128] = high
            gall[pl.ds(at, WIDE), 128:256] = low
            for q in range(3):
                row = base + PAD + 2 * (q - 1)
                ends = jnp.where(left, act0[u + 2, pl.ds(row, WIDE), :], act0[u, pl.ds(row, WIDE), :])
                xall[q, pl.ds(at, WIDE), 0:128] = ends.astype(BF16)
                xall[q, pl.ds(at, WIDE), 128:256] = act0[u + 1, pl.ds(row, WIDE), :].astype(BF16)

    def first_adjoint(w, carry):
        adjoint_operand(w)
        collect(w)
        adjoint()
        adjoint_result(w)
        return carry

    lax.fori_loop(0, 4, first_adjoint, 0)

    where_block = lane_block(8)
    for m in range(REACH + 1):
        packed = jnp.zeros((8, 128), F32)
        for b in range(4):
            row = 32 * m + 8 * b + HALO + PAD
            value = colacc[row : row + 8]
            value = value + pltpu.roll(value, 64, 1)
            value = value + pltpu.roll(value, 32, 1)
            packed = jnp.where(where_block == b, value, packed)
        colp[8 * m : 8 * m + 8] = packed
    columns = []
    for m in range(1, REACH + 1):
        columns.append(
            pltpu.make_async_remote_copy(
                colp.at[pl.ds(8 * m, 8)], cbuf.at[m - 1], sems.at[2], sems.at[3], device_id=(dev(m),), device_id_type=MESH
            )
        )
    for copy in columns:
        copy.start()

    galt[...] = gall[...].T

    def by_column_tap(q, carry):
        fg[q] = dot(galt[...], xall[q])
        return carry

    lax.fori_loop(0, 3, by_column_tap, 0)

    where_block = lane_block(32)
    for group in range(3):
        packed = jnp.zeros((32, 128), F32)
        for place in range(4):
            tap = 4 * group + place
            if tap > 8:
                continue
            p, q = tap // 3 - 1, tap % 3
            value = jnp.zeros((32, 128), F32)
            for b in range(4):
                source = b + 2 * p
                lanes = slice(128, 256) if 0 <= source < 4 else slice(0, 128)
                both = fg[q, 32 * b : 32 * b + 32, lanes] + fg[q, 128 + 32 * b : 160 + 32 * b, lanes]
                value = value + jnp.where(where_block == source % 4, both, 0.0)
            value = value + pltpu.roll(value, 64, 1)
            value = value + pltpu.roll(value, 32, 1)
            packed = jnp.where(where_block == place, value, packed)
        arbuf[128 + 32 * group : 160 + 32 * group] = packed
    for tap in range(10):
        arbuf[224 + tap : 225 + tap] = jnp.sum(tacc[8 * tap : 8 * tap + 8], axis=0, keepdims=True)
    sums = arbuf[224:240]
    sums = sums + pltpu.roll(sums, 64, 1)
    arbuf[224:240] = sums + pltpu.roll(sums, 32, 1)
    high, low = split(jnp.concatenate([tacc[8 * tap : 8 * tap + 8] for tap in range(9)], axis=1))
    by_read = jnp.sum(dot(high, k2t[...]) + dot(low, k2t[...]), axis=0, keepdims=True)
    arbuf[233:234, 0:32] = arbuf[233:234, 0:32] + by_read

    where_block = lane_block(8)
    rows = rowg[...]
    for b in range(4):
        vbuf[1, pl.ds(b, 8, stride=4), :] = jnp.where(where_block == 1, pltpu.roll(rows, (32 - 32 * b) % 128, 1) if b != 1 else rows, 0.0)
    all_of(arbuf.at[pl.ds(0, 128)], sems.at[0])
    all_of(cbuf, sems.at[3])
    all_of(cbuf, sems.at[2])
    own = colp[0:8]
    for m in range(1, REACH + 1):
        own = own + cbuf[m - 1]
    for b in range(4):
        vbuf[0, 8 * b : 8 * b + 8] = jnp.where(where_block == 0, pltpu.roll(own, (128 - 32 * b) % 128, 1) if b else own, 0.0)
    both = vbuf[0] + vbuf[1]
    high, low = split(both)
    by_feature = dot_t(jnp.concatenate([high, low], axis=0), jnp.concatenate([feat[...]] * 2, axis=0))
    arbuf[0:64] = by_feature[0:64, 0:128]
    arbuf[64:128] = by_feature[0:64, 128:256]

    def chunk(q):
        return pl.ds(pl.multiple_of(q * part, part), part)

    def send(source, place, at, device):
        pltpu.make_async_remote_copy(
            source, place, sems.at[at], sems.at[at + 1], device_id=(device,), device_id_type=MESH
        ).start()

    def each(count, action):
        def step(s, carry):
            action(s)
            return carry

        lax.fori_loop(1, count, step, 0)

    each(side, lambda s: send(arbuf.at[chunk(lax.rem(plane + s, side))], rsbuf.at[s - 1], 4, across(s)))
    weights = jnp.concatenate([col_t[...], row_t[...]], axis=0)
    by_bin = dot(high[:, 0:64], weights) + dot(low[:, 0:64], weights)
    gbuf[256:288] = by_bin[:, 0:128]
    gbuf[288:320] = by_bin[:, 128:256]
    all_of(rsbuf, sems.at[5])
    total = arbuf[chunk(plane), :]
    for s in range(1, side):
        total = total + rsbuf[s - 1]
    mine[...] = total
    bbuf[pos] = total
    each(SIDE, lambda s: send(mine, bbuf.at[pos], 6, in_line(s)))
    all_of(rsbuf, sems.at[4])
    all_of(bbuf.at[pl.ds(0, SIDE - 1)], sems.at[7])
    total = bbuf[0]
    for q in range(1, SIDE):
        total = total + bbuf[q]
    gbuf[chunk(plane), :] = total
    each(side, lambda s: send(gbuf.at[chunk(plane)], gbuf.at[chunk(plane)], 8, across(s)))
    all_of(bbuf.at[pl.ds(0, SIDE - 1)], sems.at[6])
    all_of(rsbuf, sems.at[9])
    all_of(rsbuf, sems.at[8])
    red[...] = gbuf[...]


def finish_kernel(red, gfeat, grow, gcol, gone, gtwo, gread):
    gfeat[:, 0:128] = red[256:288]
    gfeat[:, 128:256] = red[288:320]
    gcol[:, 0:128] = red[0:32]
    gcol[:, 128:256] = red[64:96]
    grow[:, 0:128] = red[32:64]
    grow[:, 128:256] = red[96:128]
    for group in range(3):
        block = red[128 + 32 * group : 160 + 32 * group].T
        count = 128 if group < 2 else 32
        gone[128 * group : 128 * group + count] = block[0:count]
    by_channel = red[224:240].T
    read = red[320:321, 0:32]
    for tap in range(9):
        gtwo[32 * tap : 32 * tap + 32] = by_channel[0:32, tap : tap + 1] * read
    gread[...] = red[233:234, 0:32]


def shards(n, features, row_proj, col_proj, first_filter, second_filter, readout, target):
    side = n // SIDE
    part = TOTAL // side
    vmem = pl.BlockSpec(memory_space=pltpu.VMEM)

    def shape(*dims):
        return jax.ShapeDtypeStruct(dims, F32)

    def real(*dims):
        return pltpu.VMEM(dims, F32)

    def half(*dims):
        return pltpu.VMEM(dims, BF16)

    k1 = first_filter.reshape(9 * PAIR, PAIR)
    k2 = second_filter.reshape(9 * PAIR, PAIR)
    ro = readout.reshape(1, PAIR)
    row_t, col_t = row_proj.T, col_proj.T
    hbm = pl.BlockSpec(memory_space=pltpu.HBM)
    scratch = dict(
        feat=half(ROWS, 256), row_t=half(PAIR, 256), col_t=half(PAIR, 256), target=real(ROWS, 256), k1=half(288, PAIR), k2=half(288, PAIR),
        proj=real(32, 128), sbuf=real(16, 128), rbuf=real(AHEAD + 2, 16, 128), tlow=real(8, 256), thigh=real(8, 256),
        roww=real(24, 128), w1=half(1152, 256), wa=half(1152, 256), w2=real(72, 128), rol=real(8, 128),
        colr=real(LENGTH, 128), mk=pltpu.VMEM((LENGTH, 128), jnp.int32), ts=real(LENGTH, 128),
        act0=real(GROUPS + 2, LENGTH, 128), d0=real(GROUPS, LENGTH, 128),
        act1=real(GROUPS, LENGTH, 128), f1=real(GROUPS, LENGTH, 128), d1=real(GROUPS, LENGTH, 128),
        mis=real(GROUPS, LENGTH, 128), g1=real(GROUPS, LENGTH, 128),
        lhs=half(WIDE, 1152), lhs2=half(2 * WIDE, 1152), k2t=half(1152, PAIR), res=real(2 * WIDE, 256), qbuf=half(WIDE, 768), wq=half(768, 256),
        xall=half(3, 8 * WIDE, 256), gall=half(8 * WIDE, 256), galt=half(256, 8 * WIDE), fg=real(3, 256, 256), tacc=real(80, 128),
        colacc=real(LENGTH, 128), tiles=real(288, 256), colp=real(72, 128), rowg=real(8, 128),
        cbuf=real(REACH, 8, 128), vbuf=real(2, 32, 128), arbuf=real(256, 128), rsbuf=real(side - 1, part, 128),
        bbuf=real(SIDE, part, 128), mine=real(part, 128), gbuf=real(328, 128), loads=SEM((6,)), sems=SEM((10,)),
    )
    red = pl.pallas_call(
        functools.partial(step_kernel, n),
        out_shape=shape(328, 128),
        in_specs=[hbm] * 6 + [vmem],
        out_specs=vmem,
        scratch_shapes=list(scratch.values()),
        compiler_params=pltpu.CompilerParams(
            collective_id=0, has_side_effects=True, vmem_limit_bytes=60 * 1024 * 1024
        ),
        name="step",
    )(features, row_t, col_t, target, k1, k2, ro)

    gfeat, grow, gcol, gone, gtwo, gread = pl.pallas_call(
        finish_kernel,
        out_shape=(shape(ROWS, 256), shape(32, 256), shape(32, 256), shape(288, 32), shape(288, 32), shape(1, 32)),
        in_specs=[vmem],
        out_specs=(vmem,) * 6,
        compiler_params=pltpu.CompilerParams(vmem_limit_bytes=4 * 1024 * 1024),
        name="finish",
    )(red)
    return gfeat, grow.T, gcol.T, gone.reshape(3, 3, PAIR, PAIR), gtwo.reshape(3, 3, PAIR, PAIR), gread.reshape(PAIR)


def solution(mesh):
    n = mesh.shape["diag"]
    in_specs = (P("diag", None), P(), P(), P(), P(), P(), P("diag", None))
    out_specs = (P("diag", None), P(), P(), P(), P(), P())
    return jax.shard_map(
        functools.partial(shards, n), mesh=mesh, in_specs=in_specs, out_specs=out_specs, check_vma=False
    )
```

```python
import functools
import math

import jax
import jax.numpy as jnp
from jax import lax
from jax.experimental import pallas as pl
from jax.experimental.pallas import tpu as pltpu
from jax.sharding import PartitionSpec as P

MESH = pl.DeviceIdType.MESH
F32, BF16 = jnp.float32, jnp.bfloat16

ROWS = 32
BAND = 256
PAIR = 32
HALO = 12
GROUPS = (ROWS + 2 * HALO) // 4
FIRST_OWN, LAST_OWN = 3, 10
PAD = 16
LENGTH = 352
WIDE, SPAN, CHUNK = 272, 264, 88
AHEAD = 9
REACH = 8
C0 = math.sqrt(2.0 / math.pi)
C1 = C0 * 0.044715
SIDE = 16
TOTAL = 256
SEM = pltpu.SemaphoreType.DMA


def iota(shape, dim):
    return lax.broadcasted_iota(jnp.int32, shape, dim)


def lane_block(rows):
    return lax.shift_right_logical(iota((rows, 128), 1), 5)


def gelu(x, with_slope):
    cubic = C1 * (x * x)
    s = 0.5 * jnp.tanh(x * (cubic + C0)) + 0.5
    value = x * s
    slope = s + value * (1.0 - s) * (6.0 * cubic + 2.0 * C0) if with_slope else None
    return value.astype(BF16).astype(F32), slope


def split(x):
    high = x.astype(BF16)
    return high, (x - high.astype(F32)).astype(BF16)


def fold(x):
    total = x[0:8]
    for i in range(1, x.shape[0] // 8):
        total = total + x[8 * i : 8 * i + 8]
    return total


def dot(a, b):
    return jnp.dot(a, b, preferred_element_type=F32)


def dot_t(a, b):
    return lax.dot_general(a, b, (((0,), (0,)), ((), ())), preferred_element_type=F32)


def dot_nt(a, b):
    return lax.dot_general(a, b, (((1,), (1,)), ((), ())), preferred_element_type=F32)


def repeater(lanes):
    return (jnp.bitwise_and(iota((PAIR, lanes), 1), 31) == iota((PAIR, lanes), 0)).astype(F32).astype(BF16)


def spread(block):
    turned = [block] + [pltpu.roll(block, 32 * s, 1) for s in (1, 2, 3)]
    where_block = lane_block(8)
    outs = []
    for b in range(4):
        value = turned[(3 - b) % 4]
        for other in range(3):
            value = jnp.where(where_block == other, turned[(other - b) % 4], value)
        outs.append(value)
    return outs


def step_kernel(
    n, feat_in, row_in, col_in, target_in, k1_in, k2_in, ro, red,
    feat, row_t, col_t, target, k1, k2,
    proj, sbuf, rbuf, tlow, thigh, roww, w1, wa, w2, rol, colr, mk, ts, act0, d0, act1, f1, d1, mis, g1,
    lhs, lhs2, k2t, res, qbuf, wq, xall, gall, fg, tacc, colacc, tiles, colp, rowg, cbuf, vbuf, arbuf, rsbuf, bbuf, mine, gbuf,
    loads, sems,
):
    me = lax.axis_index("diag")
    start = me * ROWS
    side = n // SIDE
    part = TOTAL // side
    pos = lax.rem(me, SIDE)
    plane = lax.div(me, SIDE)

    def dev(step):
        return lax.rem(me + step + n, n)

    def in_line(s):
        return me - pos + lax.rem(pos + s, SIDE)

    def across(s):
        return lax.rem(plane + s, side) * SIDE + pos

    fetches = [
        pltpu.make_async_copy(source, place, loads.at[i])
        for i, (source, place) in enumerate(
            ((feat_in, feat), (row_in, row_t), (col_in, col_t), (k1_in, k1), (k2_in, k2), (target_in, target))
        )
    ]
    for fetch in fetches:
        fetch.start()

    barrier = pltpu.get_barrier_semaphore()
    for step in range(1, AHEAD + 1):
        for target_device in (dev(step), dev(-step)):
            pl.semaphore_signal(barrier, inc=1, device_id=(target_device,), device_id_type=MESH)

    def greet(sign, s, carry):
        pl.semaphore_signal(barrier, inc=1, device_id=(me + sign * s,), device_id_type=MESH)
        return carry

    lax.fori_loop(AHEAD + 1, SIDE - pos, functools.partial(greet, 1), 0)
    lax.fori_loop(AHEAD + 1, pos + 1, functools.partial(greet, -1), 0)

    def greet_across(s, carry):
        pl.semaphore_signal(barrier, inc=1, device_id=(across(s),), device_id_type=MESH)
        return carry

    lax.fori_loop(1, side, greet_across, 0)

    for fetch in fetches[0:3]:
        fetch.wait()
    proj[...] = dot_nt(feat[...], jnp.concatenate([row_t[...]] * 4, axis=0))
    cc = dot_nt(feat[...], jnp.concatenate([col_t[...]] * 4, axis=0))
    where_block = lane_block(8)
    row_c = jnp.zeros((8, 128), F32)
    col_c = jnp.zeros((8, 128), F32)
    for b in range(4):
        row_c = jnp.where(where_block == b, proj[pl.ds(b, 8, stride=4), :], row_c)
        col_c = jnp.where(where_block == b, cc[8 * b : 8 * b + 8], col_c)
    sbuf[0:8] = col_c
    sbuf[8:16] = row_c
    greeted = jnp.maximum(SIDE - AHEAD - 1 - pos, 0) + jnp.maximum(pos - AHEAD, 0)
    pl.semaphore_wait(barrier, 2 * AHEAD + greeted + side - 1)
    gathers = []
    for m in range(AHEAD + 1, 2, -1):
        gathers.append(
            pltpu.make_async_remote_copy(
                sbuf.at[pl.ds(0, 8)], rbuf.at[m, pl.ds(0, 8)], sems.at[0], sems.at[1], device_id=(dev(1 - m),), device_id_type=MESH
            )
        )
    for slot, step in ((0, 1), (2, -1)):
        gathers.append(
            pltpu.make_async_remote_copy(sbuf, rbuf.at[slot], sems.at[0], sems.at[1], device_id=(dev(step),), device_id_type=MESH)
        )
    gathers.append(
        pltpu.make_async_remote_copy(
            target_in.at[pl.ds(24, 8)], tlow, sems.at[0], sems.at[1], device_id=(dev(1),), device_id_type=MESH
        )
    )
    gathers.append(
        pltpu.make_async_remote_copy(
            target_in.at[pl.ds(0, 8)], thigh, sems.at[0], sems.at[1], device_id=(dev(-1),), device_id_type=MESH
        )
    )
    for copy in gathers:
        copy.start()

    for fetch in fetches[3:6]:
        fetch.wait()
    rep8 = repeater(256)
    where_out = lax.shift_right_logical(iota((PAIR, 256), 1), 5)

    def build(weights, sign):
        for q in range(3):
            for place, ri in enumerate((8, 9, -2, -1, 0, 1, 2, 3, 4, 5, 6, 7)):
                value = jnp.zeros((PAIR, 256), F32)
                for p in range(3):
                    tap = 3 * p + q
                    ro_here = ri - sign * 2 * (p - 1)
                    if 0 <= ro_here < 8:
                        value = jnp.where(where_out == ro_here, tiles[32 * tap : 32 * tap + 32], value)
                row = (q * 12 + place) * 32
                weights[row : row + 32] = value.astype(BF16)

    tiles[...] = dot(k1[...], rep8)
    build(w1, 1)
    tiles[...] = dot_t(jnp.concatenate([k1[32 * tap : 32 * tap + 32] for tap in range(9)], axis=1), rep8)
    build(wa, -1)
    ro8 = jnp.broadcast_to(ro[...].astype(F32), (8, PAIR)).astype(BF16)
    rol[...] = dot(ro8, repeater(128))
    for tap in range(9):
        for b in range(4):
            row = 128 * tap + 32 * b
            k2t[row : row + 32] = k2[32 * tap : 32 * tap + 32]
        w2[8 * tap : 8 * tap + 8] = dot_nt(ro8, k2t[128 * tap : 128 * tap + 128])
    gbuf[320:328] = rol[...]

    same = lax.shift_right_logical(iota((256, 256), 0), 5) == lax.shift_right_logical(iota((256, 256), 1), 5)
    ones = same.astype(F32).astype(BF16)
    wq[0:256] = ones
    wq[256:512] = ones
    act0[0] = jnp.zeros((LENGTH, 128), F32)
    act0[GROUPS + 1] = jnp.zeros((LENGTH, 128), F32)
    colacc[...] = jnp.zeros((LENGTH, 128), F32)
    tacc[...] = jnp.zeros((80, 128), F32)
    ts[...] = jnp.zeros((LENGTH, 128), F32)
    arbuf[224:256] = jnp.zeros((32, 128), F32)
    column = iota((LENGTH, 128), 0) - PAD
    mk[...] = jnp.where(column + (start - HALO) < n * ROWS, column - lane_block(LENGTH), 1 << 20)

    def all_of(place, sem):
        pltpu.make_async_copy(place, place, sem).wait()

    all_of(arbuf.at[pl.ds(0, 128)], sems.at[1])
    for m in range(AHEAD + 2):
        for b, value in enumerate(spread(col_c if m == 1 else rbuf[m, 0:8])):
            row = 32 * (m - 1) + 8 * b + HALO + PAD
            if row >= 0 and row + 8 <= LENGTH:
                colr[row : row + 8] = value
    roww[0:8] = rbuf[0, 8:16]
    roww[8:16] = row_c
    roww[16:24] = rbuf[2, 8:16]
    def first_column(u):
        return pl.multiple_of(8 * lax.shift_right_logical(u, 1), 8)

    def mask_at(u, row, count):
        shift = 4 * u - jnp.where(start + 4 * u - HALO >= 0, 0, 1 << 20)
        return jnp.bitwise_and(mk[pl.ds(row, count), :] - shift, -BAND) == 0

    def clear_sides(buffer, index, base):
        buffer[index, pl.ds(base, 16), :] = jnp.zeros((16, 128), F32)
        buffer[index, pl.ds(base + PAD + SPAN, 24), :] = jnp.zeros((24, 128), F32)

    left = lane_block(WIDE) < 2

    def pieces(buffer, index, row):
        ends = jnp.where(left, buffer[index + 3, pl.ds(row, WIDE), :], buffer[index, pl.ds(row, WIDE), :])
        return ends, buffer[index + 1, pl.ds(row, WIDE), :], buffer[index + 2, pl.ds(row, WIDE), :]

    def make_field(with_slope, v):
        base = pl.multiple_of(8 * v, 8)
        for h in range(2):
            u = 2 * v + h
            clear_sides(act0, u + 1, base)
            row_here = roww[pl.ds(u + 5, 1), :]
            for ch in range(3):
                row = base + PAD + CHUNK * ch
                mask = mask_at(u, row, CHUNK)
                x = jnp.where(mask, row_here + colr[pl.ds(row, CHUNK), :], 0.0)
                act, slope = gelu(x, with_slope)
                act0[u + 1, pl.ds(row, CHUNK), :] = act
                if with_slope:
                    d0[u, pl.ds(row, CHUNK), :] = jnp.where(mask, slope, 0.0)

    def conv_operand(v):
        base = pl.multiple_of(8 * v, 8)
        for q in range(3):
            for d, piece in enumerate(pieces(act0, 2 * v, base + PAD + 2 * (q - 1))):
                lhs[:, 128 * (3 * q + d) : 128 * (3 * q + d + 1)] = piece.astype(BF16)

    def conv():
        res[0:WIDE] = dot(lhs[...], w1[...])

    def conv_result(with_slope, v):
        base = pl.multiple_of(8 * v, 8)
        for h in range(2):
            u = 2 * v + h
            clear_sides(act1, u, base)
            clear_sides(f1, u, base)
            row_here = roww[pl.ds(u + 5, 1), :]
            for ch in range(3):
                row = base + PAD + CHUNK * ch
                added = res[CHUNK * ch : CHUNK * ch + CHUNK, 128 * h : 128 * h + 128]
                mask = mask_at(u, row, CHUNK)
                x = jnp.where(mask, (row_here + colr[pl.ds(row, CHUNK), :]) + added, 0.0)
                act, slope = gelu(x, with_slope)
                act1[u, pl.ds(row, CHUNK), :] = act
                f1[u, pl.ds(row, CHUNK), :] = x
                if with_slope:
                    d1[u, pl.ds(row, CHUNK), :] = jnp.where(mask, slope, 0.0)

    make_field(False, 0)
    make_field(True, 1)
    conv_operand(0)
    wide = jnp.concatenate([tlow[...], target[...], thigh[...]], axis=0)
    wide = jnp.concatenate([wide, jnp.zeros((48, 128), F32)], axis=1)
    wide = jnp.concatenate([wide, jnp.zeros((80, 384), F32)], axis=0)
    sheared = pltpu.roll(wide, 0, 1, stride=1, stride_axis=0)
    ts[4 + PAD : 4 + PAD + 312] = sheared.T[0:312]
    make_field(True, 2)
    conv()

    def first_conv(with_field, v, carry):
        conv_operand(v)
        conv_result(True, v - 1)
        if with_field:
            make_field(True, v + 2)
        conv()
        return carry

    lax.fori_loop(1, 5, functools.partial(first_conv, True), 0)
    lax.fori_loop(5, 7, functools.partial(first_conv, False), 0)
    conv_result(False, 6)

    def make_misfit(w, carry):
        base = pl.multiple_of(8 * w, 8)
        for at, count in ((0, 96), (96, 96), (192, 80)):
            row = base + PAD + at
            for h in range(2):
                u = 2 * w + 1 + h
                value = rol[0:1] * f1[u, pl.ds(row, count), :]
                for p in range(3):
                    for q in range(3):
                        tap = 3 * p + q
                        value = value + w2[8 * tap : 8 * tap + 1] * act1[u + p - 1, pl.ds(row + 4 * (q - 1), count), :]
                high, low = split(value)
                qbuf[at : at + count, 128 * h : 128 * h + 128] = high
                qbuf[at : at + count, 256 + 128 * h : 384 + 128 * h] = low
            high, low = split(ts[pl.ds(row, count), :])
            qbuf[at : at + count, 512:640] = high
            qbuf[at : at + count, 640:768] = low
        pick = jnp.where(iota((128, 256), 0) == 8 * w + lax.shift_right_logical(iota((128, 256), 1), 5), -1.0, 0.0).astype(BF16)
        wq[512:640] = pick
        wq[640:768] = pick
        value = dot(qbuf[...], wq[...]) * (1.0 / BAND)
        for h in range(2):
            u = 2 * w + 1 + h
            clear_sides(mis, u, base)
            for at, count in ((0, 96), (96, 96), (192, 80)):
                row = base + PAD + at
                mis[u, pl.ds(row, count), :] = jnp.where(
                    mask_at(u, row, count), value[at : at + count, 128 * h : 128 * h + 128], 0.0
                )
        return carry

    lax.fori_loop(0, 6, make_misfit, 0)

    def make_cotangent(u, carry):
        base = first_column(u)
        clear_sides(g1, u, base)
        sums = [None] * 10
        for ch in range(3):
            row = base + PAD + CHUNK * ch
            act = act1[u, pl.ds(row, CHUNK), :]
            back = None
            for p in range(3):
                for q in range(3):
                    tap = 3 * p + q
                    m = mis[u - (p - 1), pl.ds(row - 4 * (q - 1), CHUNK), :]
                    term = w2[8 * tap : 8 * tap + 1] * m
                    back = term if back is None else back + term
                    part = fold(act * m)
                    sums[tap] = part if sums[tap] is None else sums[tap] + part
            m = mis[u, pl.ds(row, CHUNK), :]
            part = fold(m * f1[u, pl.ds(row, CHUNK), :])
            sums[9] = part if sums[9] is None else sums[9] + part
            g1[u, pl.ds(row, CHUNK), :] = rol[0:1] * m + d1[u, pl.ds(row, CHUNK), :] * back
        for tap in range(10):
            source = u - (tap // 3 - 1) if tap < 9 else u
            own = jnp.logical_and(source >= FIRST_OWN, source <= LAST_OWN)
            tacc[8 * tap : 8 * tap + 8] += jnp.where(own, sums[tap], 0.0)
        return carry

    lax.fori_loop(2, GROUPS - 2, make_cotangent, 0)

    def adjoint_operand(w):
        base = pl.multiple_of(8 * w + 8, 8)
        for q in range(3):
            for d, piece in enumerate(pieces(g1, 2 * w + 2, base + PAD - 2 * (q - 1))):
                high, low = split(piece)
                lanes = slice(128 * (3 * q + d), 128 * (3 * q + d + 1))
                lhs2[0:WIDE, lanes] = high
                lhs2[WIDE : 2 * WIDE, lanes] = low

    def adjoint():
        res[...] = dot(lhs2[...], wa[...])

    def adjoint_result(w):
        base = pl.multiple_of(8 * w + 8, 8)
        for h in range(2):
            u = 2 * w + 3 + h
            total_row = None
            for ch in range(3):
                at = CHUNK * ch + 8 * h
                row = base + PAD + at
                lanes = slice(128 * h, 128 * h + 128)
                back = res[at : at + CHUNK, lanes] + res[WIDE + at : WIDE + at + CHUNK, lanes]
                value = g1[u, pl.ds(row, CHUNK), :] + d0[u, pl.ds(row, CHUNK), :] * back
                colacc[pl.ds(row, CHUNK), :] += value
                part = fold(value)
                total_row = part if total_row is None else total_row + part
            rowg[pl.ds(u - 3, 1), :] = jnp.sum(total_row, axis=0, keepdims=True)

    def collect(w):
        for h in range(2):
            u = 2 * w + 3 + h
            base = pl.multiple_of(8 * w + 8 + 8 * h, 8)
            at = pl.multiple_of(WIDE * (2 * w + h), 16)
            high, low = split(g1[u, pl.ds(base + PAD, WIDE), :])
            gall[pl.ds(at, WIDE), 0:128] = high
            gall[pl.ds(at, WIDE), 128:256] = low
            for q in range(3):
                row = base + PAD + 2 * (q - 1)
                ends = jnp.where(left, act0[u + 2, pl.ds(row, WIDE), :], act0[u, pl.ds(row, WIDE), :])
                xall[pl.ds(at, WIDE), 256 * q : 256 * q + 128] = ends.astype(BF16)
                xall[pl.ds(at, WIDE), 256 * q + 128 : 256 * q + 256] = act0[u + 1, pl.ds(row, WIDE), :].astype(BF16)

    adjoint_operand(0)
    collect(0)
    adjoint()

    def first_adjoint(w, carry):
        adjoint_operand(w)
        adjoint_result(w - 1)
        collect(w)
        adjoint()
        return carry

    lax.fori_loop(1, 4, first_adjoint, 0)
    adjoint_result(3)

    where_block = lane_block(8)
    for m in range(REACH + 1):
        packed = jnp.zeros((8, 128), F32)
        for b in range(4):
            row = 32 * m + 8 * b + HALO + PAD
            value = colacc[row : row + 8]
            value = value + pltpu.roll(value, 64, 1)
            value = value + pltpu.roll(value, 32, 1)
            packed = jnp.where(where_block == b, value, packed)
        colp[8 * m : 8 * m + 8] = packed
    columns = []
    for m in range(1, REACH + 1):
        columns.append(
            pltpu.make_async_remote_copy(
                colp.at[pl.ds(8 * m, 8)], cbuf.at[m - 1], sems.at[2], sems.at[3], device_id=(dev(m),), device_id_type=MESH
            )
        )
    for copy in columns:
        copy.start()

    fg[...] = dot_t(gall[...], xall[...])

    where_block = lane_block(32)
    for group in range(3):
        packed = jnp.zeros((32, 128), F32)
        for place in range(4):
            tap = 4 * group + place
            if tap > 8:
                continue
            p, q = tap // 3 - 1, tap % 3
            value = jnp.zeros((32, 128), F32)
            for b in range(4):
                source = b + 2 * p
                lanes = 256 * q + (128 if 0 <= source < 4 else 0)
                both = fg[32 * b : 32 * b + 32, lanes : lanes + 128] + fg[128 + 32 * b : 160 + 32 * b, lanes : lanes + 128]
                value = value + jnp.where(where_block == source % 4, both, 0.0)
            value = value + pltpu.roll(value, 64, 1)
            value = value + pltpu.roll(value, 32, 1)
            packed = jnp.where(where_block == place, value, packed)
        arbuf[128 + 32 * group : 160 + 32 * group] = packed
    for tap in range(10):
        arbuf[224 + tap : 225 + tap] = jnp.sum(tacc[8 * tap : 8 * tap + 8], axis=0, keepdims=True)
    sums = arbuf[224:240]
    sums = sums + pltpu.roll(sums, 64, 1)
    arbuf[224:240] = sums + pltpu.roll(sums, 32, 1)
    high, low = split(jnp.concatenate([tacc[8 * tap : 8 * tap + 8] for tap in range(9)], axis=1))
    by_read = jnp.sum(dot(high, k2t[...]) + dot(low, k2t[...]), axis=0, keepdims=True)
    arbuf[233:234, 0:32] = arbuf[233:234, 0:32] + by_read

    def chunk(q):
        return pl.ds(pl.multiple_of(q * part, part), part)

    def send(source, place, at, device):
        pltpu.make_async_remote_copy(
            source, place, sems.at[at], sems.at[at + 1], device_id=(device,), device_id_type=MESH
        ).start()

    def scatter(begin, end):
        for q in range(begin, end):
            s = lax.rem(q - plane + side, side)

            @pl.when(s > 0)
            def _():
                send(arbuf.at[pl.ds(q * part, part)], rsbuf.at[s - 1], 4, across(s))

    scatter(side // 2, side)

    where_block = lane_block(8)
    rows = rowg[...]
    for b in range(4):
        vbuf[1, pl.ds(b, 8, stride=4), :] = jnp.where(where_block == 1, pltpu.roll(rows, (32 - 32 * b) % 128, 1) if b != 1 else rows, 0.0)
    all_of(arbuf.at[pl.ds(0, 128)], sems.at[0])
    all_of(cbuf, sems.at[3])
    all_of(cbuf, sems.at[2])
    own = colp[0:8]
    for m in range(1, REACH + 1):
        own = own + cbuf[m - 1]
    for b in range(4):
        vbuf[0, 8 * b : 8 * b + 8] = jnp.where(where_block == 0, pltpu.roll(own, (128 - 32 * b) % 128, 1) if b else own, 0.0)
    both = vbuf[0] + vbuf[1]
    high, low = split(both)
    by_feature = dot_t(jnp.concatenate([high, low], axis=0), jnp.concatenate([feat[...]] * 2, axis=0))
    arbuf[0:64] = by_feature[0:64, 0:128]
    arbuf[64:128] = by_feature[0:64, 128:256]

    scatter(0, side // 2)
    weights = jnp.concatenate([col_t[...], row_t[...]], axis=0)
    by_bin = dot(high[:, 0:64], weights) + dot(low[:, 0:64], weights)
    gbuf[256:288] = by_bin[:, 0:128]
    gbuf[288:320] = by_bin[:, 128:256]
    keep = pltpu.make_async_copy(gbuf.at[pl.ds(256, 72)], red.at[pl.ds(256, 72)], loads.at[6])
    keep.start()
    all_of(rsbuf, sems.at[5])
    total = arbuf[chunk(plane), :]
    for s in range(1, side):
        total = total + rsbuf[s - 1]
    mine[...] = total
    bbuf[pos] = total
    for s in range(1, SIDE):
        send(mine, bbuf.at[pos], 6, in_line(s))
    all_of(rsbuf, sems.at[4])
    all_of(bbuf.at[pl.ds(0, SIDE - 1)], sems.at[7])
    total = bbuf[0]
    for q in range(1, SIDE):
        total = total + bbuf[q]
    gbuf[chunk(plane), :] = total
    for s in range(1, side):
        send(gbuf.at[chunk(plane)], red.at[chunk(plane)], 8, across(s))
    place = pltpu.make_async_copy(gbuf.at[chunk(plane)], red.at[chunk(plane)], loads.at[7])
    place.start()
    all_of(bbuf.at[pl.ds(0, SIDE - 1)], sems.at[6])
    all_of(rsbuf, sems.at[9])
    all_of(rsbuf, sems.at[8])
    keep.wait()
    place.wait()


def finish_kernel(red, gfeat, grow, gcol, gone, gtwo, gread):
    gfeat[:, 0:128] = red[256:288]
    gfeat[:, 128:256] = red[288:320]
    gcol[:, 0:128] = red[0:32]
    gcol[:, 128:256] = red[64:96]
    grow[:, 0:128] = red[32:64]
    grow[:, 128:256] = red[96:128]
    for group in range(3):
        block = red[128 + 32 * group : 160 + 32 * group].T
        count = 128 if group < 2 else 32
        gone[128 * group : 128 * group + count] = block[0:count]
    by_channel = red[224:240].T
    read = red[320:321, 0:32]
    for tap in range(9):
        gtwo[32 * tap : 32 * tap + 32] = by_channel[0:32, tap : tap + 1] * read
    gread[...] = red[233:234, 0:32]


def shards(n, features, row_proj, col_proj, first_filter, second_filter, readout, target):
    side = n // SIDE
    part = TOTAL // side
    vmem = pl.BlockSpec(memory_space=pltpu.VMEM)

    def shape(*dims):
        return jax.ShapeDtypeStruct(dims, F32)

    def real(*dims):
        return pltpu.VMEM(dims, F32)

    def half(*dims):
        return pltpu.VMEM(dims, BF16)

    k1 = first_filter.reshape(9 * PAIR, PAIR)
    k2 = second_filter.reshape(9 * PAIR, PAIR)
    ro = readout.reshape(1, PAIR)
    row_t, col_t = row_proj.T, col_proj.T
    hbm = pl.BlockSpec(memory_space=pltpu.HBM)
    scratch = dict(
        feat=half(ROWS, 256), row_t=half(PAIR, 256), col_t=half(PAIR, 256), target=real(ROWS, 256), k1=half(288, PAIR), k2=half(288, PAIR),
        proj=real(32, 128), sbuf=real(16, 128), rbuf=real(AHEAD + 2, 16, 128), tlow=real(8, 256), thigh=real(8, 256),
        roww=real(24, 128), w1=half(1152, 256), wa=half(1152, 256), w2=real(72, 128), rol=real(8, 128),
        colr=real(LENGTH, 128), mk=pltpu.VMEM((LENGTH, 128), jnp.int32), ts=real(LENGTH, 128),
        act0=real(GROUPS + 2, LENGTH, 128), d0=real(GROUPS, LENGTH, 128),
        act1=real(GROUPS, LENGTH, 128), f1=real(GROUPS, LENGTH, 128), d1=real(GROUPS, LENGTH, 128),
        mis=real(GROUPS, LENGTH, 128), g1=real(GROUPS, LENGTH, 128),
        lhs=half(WIDE, 1152), lhs2=half(2 * WIDE, 1152), k2t=half(1152, PAIR), res=real(2 * WIDE, 256), qbuf=half(WIDE, 768), wq=half(768, 256),
        xall=half(8 * WIDE, 768), gall=half(8 * WIDE, 256), fg=real(256, 768), tacc=real(80, 128),
        colacc=real(LENGTH, 128), tiles=real(288, 256), colp=real(72, 128), rowg=real(8, 128),
        cbuf=real(REACH, 8, 128), vbuf=real(2, 32, 128), arbuf=real(256, 128), rsbuf=real(side - 1, part, 128),
        bbuf=real(SIDE, part, 128), mine=real(part, 128), gbuf=real(328, 128), loads=SEM((8,)), sems=SEM((10,)),
    )
    red = pl.pallas_call(
        functools.partial(step_kernel, n),
        out_shape=shape(328, 128),
        in_specs=[hbm] * 6 + [vmem],
        out_specs=hbm,
        scratch_shapes=list(scratch.values()),
        compiler_params=pltpu.CompilerParams(
            collective_id=0, has_side_effects=True, vmem_limit_bytes=60 * 1024 * 1024
        ),
        name="step",
    )(features, row_t, col_t, target, k1, k2, ro)

    gfeat, grow, gcol, gone, gtwo, gread = pl.pallas_call(
        finish_kernel,
        out_shape=(shape(ROWS, 256), shape(32, 256), shape(32, 256), shape(288, 32), shape(288, 32), shape(1, 32)),
        in_specs=[vmem],
        out_specs=(vmem,) * 6,
        compiler_params=pltpu.CompilerParams(vmem_limit_bytes=4 * 1024 * 1024),
        name="finish",
    )(red)
    return gfeat, grow.T, gcol.T, gone.reshape(3, 3, PAIR, PAIR), gtwo.reshape(3, 3, PAIR, PAIR), gread.reshape(PAIR)


def solution(mesh):
    n = mesh.shape["diag"]
    in_specs = (P("diag", None), P(), P(), P(), P(), P(), P("diag", None))
    out_specs = (P("diag", None), P(), P(), P(), P(), P())
    return jax.shard_map(
        functools.partial(shards, n), mesh=mesh, in_specs=in_specs, out_specs=out_specs, check_vma=False
    )
```

```python
import functools
import math

import jax
import jax.numpy as jnp
from jax import lax
from jax.experimental import pallas as pl
from jax.experimental.pallas import tpu as pltpu
from jax.sharding import PartitionSpec as P

MESH = pl.DeviceIdType.MESH
F32, BF16 = jnp.float32, jnp.bfloat16

ROWS = 32
BAND = 256
PAIR = 32
HALO = 12
GROUPS = (ROWS + 2 * HALO) // 4
FIRST_OWN, LAST_OWN = 3, 10
PAD = 16
LENGTH = 352
WIDE, SPAN, CHUNK = 272, 264, 88
AHEAD = 9
REACH = 8
C0 = math.sqrt(2.0 / math.pi)
C1 = C0 * 0.044715
SIDE = 16
TOTAL = 256
SEM = pltpu.SemaphoreType.DMA


def iota(shape, dim):
    return lax.broadcasted_iota(jnp.int32, shape, dim)


def lane_block(rows):
    return lax.shift_right_logical(iota((rows, 128), 1), 5)


def gelu(x, with_slope):
    cubic = C1 * (x * x)
    s = 0.5 * jnp.tanh(x * (cubic + C0)) + 0.5
    value = x * s
    slope = s + value * (1.0 - s) * (6.0 * cubic + 2.0 * C0) if with_slope else None
    return value.astype(BF16).astype(F32), slope


def split(x):
    high = x.astype(BF16)
    return high, (x - high.astype(F32)).astype(BF16)


def fold(x):
    total = x[0:8]
    for i in range(1, x.shape[0] // 8):
        total = total + x[8 * i : 8 * i + 8]
    return total


def dot(a, b):
    return jnp.dot(a, b, preferred_element_type=F32)


def dot_t(a, b):
    return lax.dot_general(a, b, (((0,), (0,)), ((), ())), preferred_element_type=F32)


def dot_nt(a, b):
    return lax.dot_general(a, b, (((1,), (1,)), ((), ())), preferred_element_type=F32)


def repeater(lanes):
    return (jnp.bitwise_and(iota((PAIR, lanes), 1), 31) == iota((PAIR, lanes), 0)).astype(F32).astype(BF16)


def spread(block):
    turned = [block] + [pltpu.roll(block, 32 * s, 1) for s in (1, 2, 3)]
    where_block = lane_block(8)
    outs = []
    for b in range(4):
        value = turned[(3 - b) % 4]
        for other in range(3):
            value = jnp.where(where_block == other, turned[(other - b) % 4], value)
        outs.append(value)
    return outs


def step_kernel(
    n, feat_in, row_in, col_in, target_in, k1_in, k2_in, ro, red,
    feat, row_t, col_t, target, k1, k2,
    proj, sbuf, rbuf, tlow, thigh, roww, w1, wa, w2, rol, colr, mk, ts, act0, d0, act1, f1, d1, mis, g1,
    lhs, lhs2, k2t, res, qbuf, wq, xall, gall, fg, tacc, colacc, tiles, colp, rowg, cbuf, vbuf, arbuf, rsbuf, bbuf, mine, gbuf,
    loads, sems,
):
    me = lax.axis_index("diag")
    start = me * ROWS
    side = n // SIDE
    part = TOTAL // side
    pos = lax.rem(me, SIDE)
    plane = lax.div(me, SIDE)

    def dev(step):
        return lax.rem(me + step + n, n)

    def in_line(s):
        return me - pos + lax.rem(pos + s, SIDE)

    def across(s):
        return lax.rem(plane + s, side) * SIDE + pos

    fetches = [
        pltpu.make_async_copy(source, place, loads.at[i])
        for i, (source, place) in enumerate(
            ((feat_in, feat), (row_in, row_t), (col_in, col_t), (k1_in, k1), (k2_in, k2), (target_in, target))
        )
    ]
    for fetch in fetches:
        fetch.start()

    barrier = pltpu.get_barrier_semaphore()
    for step in range(1, AHEAD + 1):
        for target_device in (dev(step), dev(-step)):
            pl.semaphore_signal(barrier, inc=1, device_id=(target_device,), device_id_type=MESH)

    def greet(sign, s, carry):
        pl.semaphore_signal(barrier, inc=1, device_id=(me + sign * s,), device_id_type=MESH)
        return carry

    lax.fori_loop(AHEAD + 1, SIDE - pos, functools.partial(greet, 1), 0)
    lax.fori_loop(AHEAD + 1, pos + 1, functools.partial(greet, -1), 0)

    def greet_across(s, carry):
        pl.semaphore_signal(barrier, inc=1, device_id=(across(s),), device_id_type=MESH)
        return carry

    lax.fori_loop(1, side, greet_across, 0)

    for fetch in fetches[0:3]:
        fetch.wait()
    proj[...] = dot_nt(feat[...], jnp.concatenate([row_t[...]] * 4, axis=0))
    cc = dot_nt(feat[...], jnp.concatenate([col_t[...]] * 4, axis=0))
    where_block = lane_block(8)
    row_c = jnp.zeros((8, 128), F32)
    col_c = jnp.zeros((8, 128), F32)
    for b in range(4):
        row_c = jnp.where(where_block == b, proj[pl.ds(b, 8, stride=4), :], row_c)
        col_c = jnp.where(where_block == b, cc[8 * b : 8 * b + 8], col_c)
    sbuf[0:8] = col_c
    sbuf[8:16] = row_c
    greeted = jnp.maximum(SIDE - AHEAD - 1 - pos, 0) + jnp.maximum(pos - AHEAD, 0)
    pl.semaphore_wait(barrier, 2 * AHEAD + greeted + side - 1)
    gathers = []
    for m in range(AHEAD + 1, 2, -1):
        gathers.append(
            pltpu.make_async_remote_copy(
                sbuf.at[pl.ds(0, 8)], rbuf.at[m, pl.ds(0, 8)], sems.at[0], sems.at[1], device_id=(dev(1 - m),), device_id_type=MESH
            )
        )
    for slot, step in ((0, 1), (2, -1)):
        gathers.append(
            pltpu.make_async_remote_copy(sbuf, rbuf.at[slot], sems.at[0], sems.at[1], device_id=(dev(step),), device_id_type=MESH)
        )
    gathers.append(
        pltpu.make_async_remote_copy(
            target_in.at[pl.ds(24, 8)], tlow, sems.at[0], sems.at[1], device_id=(dev(1),), device_id_type=MESH
        )
    )
    gathers.append(
        pltpu.make_async_remote_copy(
            target_in.at[pl.ds(0, 8)], thigh, sems.at[0], sems.at[1], device_id=(dev(-1),), device_id_type=MESH
        )
    )
    for copy in gathers:
        copy.start()

    for fetch in fetches[3:6]:
        fetch.wait()
    rep8 = repeater(256)
    where_out = lax.shift_right_logical(iota((PAIR, 256), 1), 5)

    def build(weights, sign):
        for q in range(3):
            for place, ri in enumerate((8, 9, -2, -1, 0, 1, 2, 3, 4, 5, 6, 7)):
                value = jnp.zeros((PAIR, 256), F32)
                for p in range(3):
                    tap = 3 * p + q
                    ro_here = ri - sign * 2 * (p - 1)
                    if 0 <= ro_here < 8:
                        value = jnp.where(where_out == ro_here, tiles[32 * tap : 32 * tap + 32], value)
                row = (q * 12 + place) * 32
                weights[row : row + 32] = value.astype(BF16)

    tiles[...] = dot(k1[...], rep8)
    build(w1, 1)
    tiles[...] = dot_t(jnp.concatenate([k1[32 * tap : 32 * tap + 32] for tap in range(9)], axis=1), rep8)
    build(wa, -1)
    ro8 = jnp.broadcast_to(ro[...].astype(F32), (8, PAIR)).astype(BF16)
    rol[...] = dot(ro8, repeater(128))
    for tap in range(9):
        for b in range(4):
            row = 128 * tap + 32 * b
            k2t[row : row + 32] = k2[32 * tap : 32 * tap + 32]
        w2[8 * tap : 8 * tap + 8] = dot_nt(ro8, k2t[128 * tap : 128 * tap + 128])
    gbuf[320:328] = rol[...]

    same = lax.shift_right_logical(iota((256, 256), 0), 5) == lax.shift_right_logical(iota((256, 256), 1), 5)
    ones = same.astype(F32).astype(BF16)
    wq[0:256] = ones
    wq[256:512] = ones
    act0[0] = jnp.zeros((LENGTH, 128), F32)
    act0[GROUPS + 1] = jnp.zeros((LENGTH, 128), F32)
    colacc[...] = jnp.zeros((LENGTH, 128), F32)
    tacc[...] = jnp.zeros((80, 128), F32)
    ts[...] = jnp.zeros((LENGTH, 128), F32)
    arbuf[224:256] = jnp.zeros((32, 128), F32)
    column = iota((LENGTH, 128), 0) - PAD
    mk[...] = jnp.where(column + (start - HALO) < n * ROWS, column - lane_block(LENGTH), 1 << 20)

    def all_of(place, sem):
        pltpu.make_async_copy(place, place, sem).wait()

    all_of(arbuf.at[pl.ds(0, 128)], sems.at[1])
    for m in range(AHEAD + 2):
        for b, value in enumerate(spread(col_c if m == 1 else rbuf[m, 0:8])):
            row = 32 * (m - 1) + 8 * b + HALO + PAD
            if row >= 0 and row + 8 <= LENGTH:
                colr[row : row + 8] = value
    roww[0:8] = rbuf[0, 8:16]
    roww[8:16] = row_c
    roww[16:24] = rbuf[2, 8:16]
    def first_column(u):
        return pl.multiple_of(8 * lax.shift_right_logical(u, 1), 8)

    def mask_at(u, row, count):
        shift = 4 * u - jnp.where(start + 4 * u - HALO >= 0, 0, 1 << 20)
        return jnp.bitwise_and(mk[pl.ds(row, count), :] - shift, -BAND) == 0

    def clear_sides(buffer, index, base):
        buffer[index, pl.ds(base, 16), :] = jnp.zeros((16, 128), F32)
        buffer[index, pl.ds(base + PAD + SPAN, 24), :] = jnp.zeros((24, 128), F32)

    left = lane_block(WIDE) < 2

    def pieces(buffer, index, row):
        ends = jnp.where(left, buffer[index + 3, pl.ds(row, WIDE), :], buffer[index, pl.ds(row, WIDE), :])
        return ends, buffer[index + 1, pl.ds(row, WIDE), :], buffer[index + 2, pl.ds(row, WIDE), :]

    def make_field(with_slope, v):
        base = pl.multiple_of(8 * v, 8)
        for h in range(2):
            u = 2 * v + h
            clear_sides(act0, u + 1, base)
            row_here = roww[pl.ds(u + 5, 1), :]
            for ch in range(3):
                row = base + PAD + CHUNK * ch
                mask = mask_at(u, row, CHUNK)
                x = jnp.where(mask, row_here + colr[pl.ds(row, CHUNK), :], 0.0)
                act, slope = gelu(x, with_slope)
                act0[u + 1, pl.ds(row, CHUNK), :] = act
                if with_slope:
                    d0[u, pl.ds(row, CHUNK), :] = jnp.where(mask, slope, 0.0)

    def conv_operand(v):
        base = pl.multiple_of(8 * v, 8)
        for q in range(3):
            for d, piece in enumerate(pieces(act0, 2 * v, base + PAD + 2 * (q - 1))):
                lhs[:, 128 * (3 * q + d) : 128 * (3 * q + d + 1)] = piece.astype(BF16)

    def conv():
        res[0:WIDE] = dot(lhs[...], w1[...])

    def conv_result(with_slope, v):
        base = pl.multiple_of(8 * v, 8)
        for h in range(2):
            u = 2 * v + h
            clear_sides(act1, u, base)
            clear_sides(f1, u, base)
            row_here = roww[pl.ds(u + 5, 1), :]
            for ch in range(3):
                row = base + PAD + CHUNK * ch
                added = res[CHUNK * ch : CHUNK * ch + CHUNK, 128 * h : 128 * h + 128]
                mask = mask_at(u, row, CHUNK)
                x = jnp.where(mask, (row_here + colr[pl.ds(row, CHUNK), :]) + added, 0.0)
                act, slope = gelu(x, with_slope)
                act1[u, pl.ds(row, CHUNK), :] = act
                f1[u, pl.ds(row, CHUNK), :] = x
                if with_slope:
                    d1[u, pl.ds(row, CHUNK), :] = jnp.where(mask, slope, 0.0)

    make_field(False, 0)
    make_field(True, 1)
    conv_operand(0)
    wide = jnp.concatenate([tlow[...], target[...], thigh[...]], axis=0)
    wide = jnp.concatenate([wide, jnp.zeros((48, 128), F32)], axis=1)
    wide = jnp.concatenate([wide, jnp.zeros((80, 384), F32)], axis=0)
    sheared = pltpu.roll(wide, 0, 1, stride=1, stride_axis=0)
    ts[4 + PAD : 4 + PAD + 312] = sheared.T[0:312]
    make_field(True, 2)
    conv()

    def first_conv(with_field, v, carry):
        conv_operand(v)
        conv_result(True, v - 1)
        if with_field:
            make_field(True, v + 2)
        conv()
        return carry

    lax.fori_loop(1, 5, functools.partial(first_conv, True), 0)
    lax.fori_loop(5, 7, functools.partial(first_conv, False), 0)
    conv_result(False, 6)

    def make_misfit(w, carry):
        base = pl.multiple_of(8 * w, 8)
        for at, count in ((0, 48), (48, 48), (96, 48), (144, 48), (192, 48), (240, 32)):
            row = base + PAD + at
            values = [rol[0:1] * f1[2 * w + 1 + h, pl.ds(row, count), :] for h in range(2)]
            for g in range(4):
                for q in range(3):
                    act = act1[2 * w + g, pl.ds(row + 4 * (q - 1), count), :]
                    for h in range(2):
                        p = g - h
                        if 0 <= p < 3:
                            tap = 3 * p + q
                            values[h] = values[h] + w2[8 * tap : 8 * tap + 1] * act
            for h in range(2):
                high, low = split(values[h])
                qbuf[at : at + count, 128 * h : 128 * h + 128] = high
                qbuf[at : at + count, 256 + 128 * h : 384 + 128 * h] = low
            high, low = split(ts[pl.ds(row, count), :])
            qbuf[at : at + count, 512:640] = high
            qbuf[at : at + count, 640:768] = low
        pick = jnp.where(iota((128, 256), 0) == 8 * w + lax.shift_right_logical(iota((128, 256), 1), 5), -1.0, 0.0).astype(BF16)
        wq[512:640] = pick
        wq[640:768] = pick
        value = dot(qbuf[...], wq[...]) * (1.0 / BAND)
        for h in range(2):
            u = 2 * w + 1 + h
            clear_sides(mis, u, base)
            for at, count in ((0, 96), (96, 96), (192, 80)):
                row = base + PAD + at
                mis[u, pl.ds(row, count), :] = jnp.where(
                    mask_at(u, row, count), value[at : at + count, 128 * h : 128 * h + 128], 0.0
                )
        return carry

    lax.fori_loop(0, 6, make_misfit, 0)

    def make_cotangent(v, carry):
        base = pl.multiple_of(8 * v, 8)
        sums = [[None] * 10 for h in range(2)]
        for h in range(2):
            clear_sides(g1, 2 * v + h, base)
        for ch in range(SPAN // 24):
            row = base + PAD + 24 * ch
            acts = [act1[2 * v + h, pl.ds(row, 24), :] for h in range(2)]
            backs = [None, None]
            centers = [None, None]
            for g in range(4):
                for q in range(3):
                    m = mis[2 * v - 1 + g, pl.ds(row - 4 * (q - 1), 24), :]
                    for h in range(2):
                        p = h + 2 - g
                        if 0 <= p < 3:
                            tap = 3 * p + q
                            term = w2[8 * tap : 8 * tap + 1] * m
                            backs[h] = term if backs[h] is None else backs[h] + term
                            part_sum = fold(acts[h] * m)
                            sums[h][tap] = part_sum if sums[h][tap] is None else sums[h][tap] + part_sum
                            if tap == 4:
                                centers[h] = m
            for h in range(2):
                u = 2 * v + h
                part_sum = fold(centers[h] * f1[u, pl.ds(row, 24), :])
                sums[h][9] = part_sum if sums[h][9] is None else sums[h][9] + part_sum
                g1[u, pl.ds(row, 24), :] = rol[0:1] * centers[h] + d1[u, pl.ds(row, 24), :] * backs[h]
        for tap in range(10):
            for h in range(2):
                source = 2 * v + h - (tap // 3 - 1) if tap < 9 else 2 * v + h
                own = jnp.logical_and(source >= FIRST_OWN, source <= LAST_OWN)
                tacc[8 * tap : 8 * tap + 8] += jnp.where(own, sums[h][tap], 0.0)
        return carry

    lax.fori_loop(1, 6, make_cotangent, 0)

    def adjoint_operand(w):
        base = pl.multiple_of(8 * w + 8, 8)
        for q in range(3):
            for d, piece in enumerate(pieces(g1, 2 * w + 2, base + PAD - 2 * (q - 1))):
                high, low = split(piece)
                lanes = slice(128 * (3 * q + d), 128 * (3 * q + d + 1))
                lhs2[0:WIDE, lanes] = high
                lhs2[WIDE : 2 * WIDE, lanes] = low

    def adjoint():
        res[...] = dot(lhs2[...], wa[...])

    def adjoint_result(w):
        base = pl.multiple_of(8 * w + 8, 8)
        for h in range(2):
            u = 2 * w + 3 + h
            total_row = None
            for ch in range(3):
                at = CHUNK * ch + 8 * h
                row = base + PAD + at
                lanes = slice(128 * h, 128 * h + 128)
                back = res[at : at + CHUNK, lanes] + res[WIDE + at : WIDE + at + CHUNK, lanes]
                value = g1[u, pl.ds(row, CHUNK), :] + d0[u, pl.ds(row, CHUNK), :] * back
                colacc[pl.ds(row, CHUNK), :] += value
                part = fold(value)
                total_row = part if total_row is None else total_row + part
            rowg[pl.ds(u - 3, 1), :] = jnp.sum(total_row, axis=0, keepdims=True)

    def collect(w):
        for h in range(2):
            u = 2 * w + 3 + h
            base = pl.multiple_of(8 * w + 8 + 8 * h, 8)
            at = pl.multiple_of(WIDE * (2 * w + h), 16)
            high, low = split(g1[u, pl.ds(base + PAD, WIDE), :])
            gall[pl.ds(at, WIDE), 0:128] = high
            gall[pl.ds(at, WIDE), 128:256] = low
            for q in range(3):
                row = base + PAD + 2 * (q - 1)
                ends = jnp.where(left, act0[u + 2, pl.ds(row, WIDE), :], act0[u, pl.ds(row, WIDE), :])
                xall[pl.ds(at, WIDE), 256 * q : 256 * q + 128] = ends.astype(BF16)
                xall[pl.ds(at, WIDE), 256 * q + 128 : 256 * q + 256] = act0[u + 1, pl.ds(row, WIDE), :].astype(BF16)

    adjoint_operand(0)
    collect(0)
    adjoint()

    def first_adjoint(w, carry):
        adjoint_operand(w)
        adjoint_result(w - 1)
        collect(w)
        adjoint()
        return carry

    lax.fori_loop(1, 4, first_adjoint, 0)
    adjoint_result(3)

    where_block = lane_block(8)
    for m in range(REACH + 1):
        packed = jnp.zeros((8, 128), F32)
        for b in range(4):
            row = 32 * m + 8 * b + HALO + PAD
            value = colacc[row : row + 8]
            value = value + pltpu.roll(value, 64, 1)
            value = value + pltpu.roll(value, 32, 1)
            packed = jnp.where(where_block == b, value, packed)
        colp[8 * m : 8 * m + 8] = packed
    columns = []
    for m in range(1, REACH + 1):
        columns.append(
            pltpu.make_async_remote_copy(
                colp.at[pl.ds(8 * m, 8)], cbuf.at[m - 1], sems.at[2], sems.at[3], device_id=(dev(m),), device_id_type=MESH
            )
        )
    for copy in columns:
        copy.start()

    fg[...] = dot_t(gall[...], xall[...])

    where_block = lane_block(32)
    for group in range(3):
        packed = jnp.zeros((32, 128), F32)
        for place in range(4):
            tap = 4 * group + place
            if tap > 8:
                continue
            p, q = tap // 3 - 1, tap % 3
            value = jnp.zeros((32, 128), F32)
            for b in range(4):
                source = b + 2 * p
                lanes = 256 * q + (128 if 0 <= source < 4 else 0)
                both = fg[32 * b : 32 * b + 32, lanes : lanes + 128] + fg[128 + 32 * b : 160 + 32 * b, lanes : lanes + 128]
                value = value + jnp.where(where_block == source % 4, both, 0.0)
            value = value + pltpu.roll(value, 64, 1)
            value = value + pltpu.roll(value, 32, 1)
            packed = jnp.where(where_block == place, value, packed)
        arbuf[128 + 32 * group : 160 + 32 * group] = packed
    for tap in range(10):
        arbuf[224 + tap : 225 + tap] = jnp.sum(tacc[8 * tap : 8 * tap + 8], axis=0, keepdims=True)
    sums = arbuf[224:240]
    sums = sums + pltpu.roll(sums, 64, 1)
    arbuf[224:240] = sums + pltpu.roll(sums, 32, 1)
    high, low = split(jnp.concatenate([tacc[8 * tap : 8 * tap + 8] for tap in range(9)], axis=1))
    by_read = jnp.sum(dot(high, k2t[...]) + dot(low, k2t[...]), axis=0, keepdims=True)
    arbuf[233:234, 0:32] = arbuf[233:234, 0:32] + by_read

    def chunk(q):
        return pl.ds(pl.multiple_of(q * part, part), part)

    def send(source, place, at, device):
        pltpu.make_async_remote_copy(
            source, place, sems.at[at], sems.at[at + 1], device_id=(device,), device_id_type=MESH
        ).start()

    def scatter(begin, end):
        for q in range(begin, end):
            s = lax.rem(q - plane + side, side)

            @pl.when(s > 0)
            def _():
                send(arbuf.at[pl.ds(q * part, part)], rsbuf.at[s - 1], 4, across(s))

    scatter(side // 2, side)

    where_block = lane_block(8)
    rows = rowg[...]
    for b in range(4):
        vbuf[1, pl.ds(b, 8, stride=4), :] = jnp.where(where_block == 1, pltpu.roll(rows, (32 - 32 * b) % 128, 1) if b != 1 else rows, 0.0)
    all_of(arbuf.at[pl.ds(0, 128)], sems.at[0])
    all_of(cbuf, sems.at[3])
    all_of(cbuf, sems.at[2])
    own = colp[0:8]
    for m in range(1, REACH + 1):
        own = own + cbuf[m - 1]
    for b in range(4):
        vbuf[0, 8 * b : 8 * b + 8] = jnp.where(where_block == 0, pltpu.roll(own, (128 - 32 * b) % 128, 1) if b else own, 0.0)
    both = vbuf[0] + vbuf[1]
    high, low = split(both)
    by_feature = dot_t(jnp.concatenate([high, low], axis=0), jnp.concatenate([feat[...]] * 2, axis=0))
    arbuf[0:64] = by_feature[0:64, 0:128]
    arbuf[64:128] = by_feature[0:64, 128:256]

    scatter(0, side // 2)
    weights = jnp.concatenate([col_t[...], row_t[...]], axis=0)
    by_bin = dot(high[:, 0:64], weights) + dot(low[:, 0:64], weights)
    gbuf[256:288] = by_bin[:, 0:128]
    gbuf[288:320] = by_bin[:, 128:256]
    keep = pltpu.make_async_copy(gbuf.at[pl.ds(256, 72)], red.at[pl.ds(256, 72)], loads.at[6])
    keep.start()
    all_of(rsbuf, sems.at[5])
    total = arbuf[chunk(plane), :]
    for s in range(1, side):
        total = total + rsbuf[s - 1]
    mine[...] = total
    bbuf[pos] = total
    for s in range(1, SIDE):
        send(mine, bbuf.at[pos], 6, in_line(s))
    all_of(rsbuf, sems.at[4])
    all_of(bbuf.at[pl.ds(0, SIDE - 1)], sems.at[7])
    total = bbuf[0]
    for q in range(1, SIDE):
        total = total + bbuf[q]
    gbuf[chunk(plane), :] = total
    for s in range(1, side):
        send(gbuf.at[chunk(plane)], red.at[chunk(plane)], 8, across(s))
    place = pltpu.make_async_copy(gbuf.at[chunk(plane)], red.at[chunk(plane)], loads.at[7])
    place.start()
    all_of(bbuf.at[pl.ds(0, SIDE - 1)], sems.at[6])
    all_of(rsbuf, sems.at[9])
    all_of(rsbuf, sems.at[8])
    keep.wait()
    place.wait()


def finish_kernel(red, gfeat, grow, gcol, gone, gtwo, gread):
    gfeat[:, 0:128] = red[256:288]
    gfeat[:, 128:256] = red[288:320]
    gcol[:, 0:128] = red[0:32]
    gcol[:, 128:256] = red[64:96]
    grow[:, 0:128] = red[32:64]
    grow[:, 128:256] = red[96:128]
    for group in range(3):
        block = red[128 + 32 * group : 160 + 32 * group].T
        count = 128 if group < 2 else 32
        gone[128 * group : 128 * group + count] = block[0:count]
    by_channel = red[224:240].T
    read = red[320:321, 0:32]
    for tap in range(9):
        gtwo[32 * tap : 32 * tap + 32] = by_channel[0:32, tap : tap + 1] * read
    gread[...] = red[233:234, 0:32]


def shards(n, features, row_proj, col_proj, first_filter, second_filter, readout, target):
    side = n // SIDE
    part = TOTAL // side
    vmem = pl.BlockSpec(memory_space=pltpu.VMEM)

    def shape(*dims):
        return jax.ShapeDtypeStruct(dims, F32)

    def real(*dims):
        return pltpu.VMEM(dims, F32)

    def half(*dims):
        return pltpu.VMEM(dims, BF16)

    k1 = first_filter.reshape(9 * PAIR, PAIR)
    k2 = second_filter.reshape(9 * PAIR, PAIR)
    ro = readout.reshape(1, PAIR)
    row_t, col_t = row_proj.T, col_proj.T
    hbm = pl.BlockSpec(memory_space=pltpu.HBM)
    scratch = dict(
        feat=half(ROWS, 256), row_t=half(PAIR, 256), col_t=half(PAIR, 256), target=real(ROWS, 256), k1=half(288, PAIR), k2=half(288, PAIR),
        proj=real(32, 128), sbuf=real(16, 128), rbuf=real(AHEAD + 2, 16, 128), tlow=real(8, 256), thigh=real(8, 256),
        roww=real(24, 128), w1=half(1152, 256), wa=half(1152, 256), w2=real(72, 128), rol=real(8, 128),
        colr=real(LENGTH, 128), mk=pltpu.VMEM((LENGTH, 128), jnp.int32), ts=real(LENGTH, 128),
        act0=real(GROUPS + 2, LENGTH, 128), d0=real(GROUPS, LENGTH, 128),
        act1=real(GROUPS, LENGTH, 128), f1=real(GROUPS, LENGTH, 128), d1=real(GROUPS, LENGTH, 128),
        mis=real(GROUPS, LENGTH, 128), g1=real(GROUPS, LENGTH, 128),
        lhs=half(WIDE, 1152), lhs2=half(2 * WIDE, 1152), k2t=half(1152, PAIR), res=real(2 * WIDE, 256), qbuf=half(WIDE, 768), wq=half(768, 256),
        xall=half(8 * WIDE, 768), gall=half(8 * WIDE, 256), fg=real(256, 768), tacc=real(80, 128),
        colacc=real(LENGTH, 128), tiles=real(288, 256), colp=real(72, 128), rowg=real(8, 128),
        cbuf=real(REACH, 8, 128), vbuf=real(2, 32, 128), arbuf=real(256, 128), rsbuf=real(side - 1, part, 128),
        bbuf=real(SIDE, part, 128), mine=real(part, 128), gbuf=real(328, 128), loads=SEM((8,)), sems=SEM((10,)),
    )
    red = pl.pallas_call(
        functools.partial(step_kernel, n),
        out_shape=shape(328, 128),
        in_specs=[hbm] * 6 + [vmem],
        out_specs=hbm,
        scratch_shapes=list(scratch.values()),
        compiler_params=pltpu.CompilerParams(
            collective_id=0, has_side_effects=True, vmem_limit_bytes=60 * 1024 * 1024
        ),
        name="step",
    )(features, row_t, col_t, target, k1, k2, ro)

    gfeat, grow, gcol, gone, gtwo, gread = pl.pallas_call(
        finish_kernel,
        out_shape=(shape(ROWS, 256), shape(32, 256), shape(32, 256), shape(288, 32), shape(288, 32), shape(1, 32)),
        in_specs=[vmem],
        out_specs=(vmem,) * 6,
        compiler_params=pltpu.CompilerParams(vmem_limit_bytes=4 * 1024 * 1024),
        name="finish",
    )(red)
    return gfeat, grow.T, gcol.T, gone.reshape(3, 3, PAIR, PAIR), gtwo.reshape(3, 3, PAIR, PAIR), gread.reshape(PAIR)


def solution(mesh):
    n = mesh.shape["diag"]
    in_specs = (P("diag", None), P(), P(), P(), P(), P(), P("diag", None))
    out_specs = (P("diag", None), P(), P(), P(), P(), P())
    return jax.shard_map(
        functools.partial(shards, n), mesh=mesh, in_specs=in_specs, out_specs=out_specs, check_vma=False
    )
```

```python
import functools
import math

import jax
import jax.numpy as jnp
from jax import lax
from jax.experimental import pallas as pl
from jax.experimental.pallas import tpu as pltpu
from jax.sharding import PartitionSpec as P

MESH = pl.DeviceIdType.MESH
F32, BF16 = jnp.float32, jnp.bfloat16

ROWS = 32
BAND = 256
PAIR = 32
HALO = 12
GROUPS = (ROWS + 2 * HALO) // 4
FIRST_OWN, LAST_OWN = 3, 10
PAD = 16
LENGTH = 352
WIDE, SPAN, CHUNK = 272, 264, 88
AHEAD = 9
REACH = 8
C0 = math.sqrt(2.0 / math.pi)
C1 = C0 * 0.044715
SIDE = 16
LINE = 8
TOTAL = 256
SEM = pltpu.SemaphoreType.DMA


def iota(shape, dim):
    return lax.broadcasted_iota(jnp.int32, shape, dim)


def lane_block(rows):
    return lax.shift_right_logical(iota((rows, 128), 1), 5)


def gelu(x, with_slope):
    cubic = C1 * (x * x)
    s = 0.5 * jnp.tanh(x * (cubic + C0)) + 0.5
    value = x * s
    slope = s + value * (1.0 - s) * (6.0 * cubic + 2.0 * C0) if with_slope else None
    return value.astype(BF16).astype(F32), slope


def split(x):
    high = x.astype(BF16)
    return high, (x - high.astype(F32)).astype(BF16)


def fold(x):
    total = x[0:8]
    for i in range(1, x.shape[0] // 8):
        total = total + x[8 * i : 8 * i + 8]
    return total


def dot(a, b):
    return jnp.dot(a, b, preferred_element_type=F32)


def dot_t(a, b):
    return lax.dot_general(a, b, (((0,), (0,)), ((), ())), preferred_element_type=F32)


def dot_nt(a, b):
    return lax.dot_general(a, b, (((1,), (1,)), ((), ())), preferred_element_type=F32)


def repeater(lanes):
    return (jnp.bitwise_and(iota((PAIR, lanes), 1), 31) == iota((PAIR, lanes), 0)).astype(F32).astype(BF16)


def spread(block):
    turned = [block] + [pltpu.roll(block, 32 * s, 1) for s in (1, 2, 3)]
    where_block = lane_block(8)
    outs = []
    for b in range(4):
        value = turned[(3 - b) % 4]
        for other in range(3):
            value = jnp.where(where_block == other, turned[(other - b) % 4], value)
        outs.append(value)
    return outs


def step_kernel(
    n, feat_in, row_in, col_in, target_in, k1_in, k2_in, ro, red,
    feat, row_t, col_t, target, k1, k2,
    proj, sbuf, rbuf, tlow, thigh, roww, w1, wa, w2, rol, colr, mk, ts, act0, d0, act1, f1, d1, mis, g1,
    lhs, lhs2, k2t, res, qbuf, wq, xall, gall, fg, tacc, colacc, tiles, colp, rowg, cbuf, vbuf, arbuf, rsbuf, bbuf, mine, other, chip, gbuf,
    loads, sems,
):
    me = lax.axis_index("diag")
    start = me * ROWS
    side = n // SIDE
    part = TOTAL // side
    pos = lax.rem(me, SIDE)
    plane = lax.div(me, SIDE)
    depth = lax.div(pos, 2)

    def dev(step):
        return lax.rem(me + step + n, n)

    def across(s):
        return lax.rem(plane + s, side) * SIDE + pos

    fetches = [
        pltpu.make_async_copy(source, place, loads.at[i])
        for i, (source, place) in enumerate(
            ((feat_in, feat), (row_in, row_t), (col_in, col_t), (k1_in, k1), (k2_in, k2), (target_in, target))
        )
    ]
    for fetch in fetches:
        fetch.start()

    barrier = pltpu.get_barrier_semaphore()
    for step in range(1, AHEAD + 1):
        for target_device in (dev(step), dev(-step)):
            pl.semaphore_signal(barrier, inc=1, device_id=(target_device,), device_id_type=MESH)

    def greet(sign, s, carry):
        pl.semaphore_signal(barrier, inc=1, device_id=(me + sign * s,), device_id_type=MESH)
        return carry

    lax.fori_loop(AHEAD + 1, SIDE - pos, functools.partial(greet, 1), 0)
    lax.fori_loop(AHEAD + 1, pos + 1, functools.partial(greet, -1), 0)

    def greet_across(s, carry):
        pl.semaphore_signal(barrier, inc=1, device_id=(across(s),), device_id_type=MESH)
        return carry

    lax.fori_loop(1, side, greet_across, 0)

    for fetch in fetches[0:3]:
        fetch.wait()
    proj[...] = dot_nt(feat[...], jnp.concatenate([row_t[...]] * 4, axis=0))
    cc = dot_nt(feat[...], jnp.concatenate([col_t[...]] * 4, axis=0))
    where_block = lane_block(8)
    row_c = jnp.zeros((8, 128), F32)
    col_c = jnp.zeros((8, 128), F32)
    for b in range(4):
        row_c = jnp.where(where_block == b, proj[pl.ds(b, 8, stride=4), :], row_c)
        col_c = jnp.where(where_block == b, cc[8 * b : 8 * b + 8], col_c)
    sbuf[0:8] = col_c
    sbuf[8:16] = row_c
    greeted = jnp.maximum(SIDE - AHEAD - 1 - pos, 0) + jnp.maximum(pos - AHEAD, 0)
    pl.semaphore_wait(barrier, 2 * AHEAD + greeted + side - 1)
    gathers = []
    for m in range(AHEAD + 1, 2, -1):
        gathers.append(
            pltpu.make_async_remote_copy(
                sbuf.at[pl.ds(0, 8)], rbuf.at[m, pl.ds(0, 8)], sems.at[0], sems.at[1], device_id=(dev(1 - m),), device_id_type=MESH
            )
        )
    for slot, step in ((0, 1), (2, -1)):
        gathers.append(
            pltpu.make_async_remote_copy(sbuf, rbuf.at[slot], sems.at[0], sems.at[1], device_id=(dev(step),), device_id_type=MESH)
        )
    gathers.append(
        pltpu.make_async_remote_copy(
            target_in.at[pl.ds(24, 8)], tlow, sems.at[0], sems.at[1], device_id=(dev(1),), device_id_type=MESH
        )
    )
    gathers.append(
        pltpu.make_async_remote_copy(
            target_in.at[pl.ds(0, 8)], thigh, sems.at[0], sems.at[1], device_id=(dev(-1),), device_id_type=MESH
        )
    )
    for copy in gathers:
        copy.start()

    for fetch in fetches[3:6]:
        fetch.wait()
    rep8 = repeater(256)
    where_out = lax.shift_right_logical(iota((PAIR, 256), 1), 5)

    def build(weights, sign):
        for q in range(3):
            for place, ri in enumerate((8, 9, -2, -1, 0, 1, 2, 3, 4, 5, 6, 7)):
                value = jnp.zeros((PAIR, 256), F32)
                for p in range(3):
                    tap = 3 * p + q
                    ro_here = ri - sign * 2 * (p - 1)
                    if 0 <= ro_here < 8:
                        value = jnp.where(where_out == ro_here, tiles[32 * tap : 32 * tap + 32], value)
                row = (q * 12 + place) * 32
                weights[row : row + 32] = value.astype(BF16)

    tiles[...] = dot(k1[...], rep8)
    build(w1, 1)
    tiles[...] = dot_t(jnp.concatenate([k1[32 * tap : 32 * tap + 32] for tap in range(9)], axis=1), rep8)
    build(wa, -1)
    ro8 = jnp.broadcast_to(ro[...].astype(F32), (8, PAIR)).astype(BF16)
    rol[...] = dot(ro8, repeater(128))
    for tap in range(9):
        for b in range(4):
            row = 128 * tap + 32 * b
            k2t[row : row + 32] = k2[32 * tap : 32 * tap + 32]
        w2[8 * tap : 8 * tap + 8] = dot_nt(ro8, k2t[128 * tap : 128 * tap + 128])
    gbuf[320:328] = rol[...]

    same = lax.shift_right_logical(iota((256, 256), 0), 5) == lax.shift_right_logical(iota((256, 256), 1), 5)
    ones = same.astype(F32).astype(BF16)
    wq[0:256] = ones
    wq[256:512] = ones
    act0[0] = jnp.zeros((LENGTH, 128), F32)
    act0[GROUPS + 1] = jnp.zeros((LENGTH, 128), F32)
    colacc[...] = jnp.zeros((LENGTH, 128), F32)
    tacc[...] = jnp.zeros((80, 128), F32)
    ts[...] = jnp.zeros((LENGTH, 128), F32)
    arbuf[224:256] = jnp.zeros((32, 128), F32)
    column = iota((LENGTH, 128), 0) - PAD
    mk[...] = jnp.where(column + (start - HALO) < n * ROWS, column - lane_block(LENGTH), 1 << 20)

    def all_of(place, sem):
        pltpu.make_async_copy(place, place, sem).wait()

    all_of(arbuf.at[pl.ds(0, 128)], sems.at[1])
    for m in range(AHEAD + 2):
        for b, value in enumerate(spread(col_c if m == 1 else rbuf[m, 0:8])):
            row = 32 * (m - 1) + 8 * b + HALO + PAD
            if row >= 0 and row + 8 <= LENGTH:
                colr[row : row + 8] = value
    roww[0:8] = rbuf[0, 8:16]
    roww[8:16] = row_c
    roww[16:24] = rbuf[2, 8:16]
    def first_column(u):
        return pl.multiple_of(8 * lax.shift_right_logical(u, 1), 8)

    def mask_at(u, row, count):
        shift = 4 * u - jnp.where(start + 4 * u - HALO >= 0, 0, 1 << 20)
        return jnp.bitwise_and(mk[pl.ds(row, count), :] - shift, -BAND) == 0

    def clear_sides(buffer, index, base):
        buffer[index, pl.ds(base, 16), :] = jnp.zeros((16, 128), F32)
        buffer[index, pl.ds(base + PAD + SPAN, 24), :] = jnp.zeros((24, 128), F32)

    left = lane_block(WIDE) < 2

    def pieces(buffer, index, row):
        ends = jnp.where(left, buffer[index + 3, pl.ds(row, WIDE), :], buffer[index, pl.ds(row, WIDE), :])
        return ends, buffer[index + 1, pl.ds(row, WIDE), :], buffer[index + 2, pl.ds(row, WIDE), :]

    def make_field(with_slope, v):
        base = pl.multiple_of(8 * v, 8)
        for h in range(2):
            u = 2 * v + h
            clear_sides(act0, u + 1, base)
            row_here = roww[pl.ds(u + 5, 1), :]
            for ch in range(3):
                row = base + PAD + CHUNK * ch
                mask = mask_at(u, row, CHUNK)
                x = jnp.where(mask, row_here + colr[pl.ds(row, CHUNK), :], 0.0)
                act, slope = gelu(x, with_slope)
                act0[u + 1, pl.ds(row, CHUNK), :] = act
                if with_slope:
                    d0[u, pl.ds(row, CHUNK), :] = jnp.where(mask, slope, 0.0)

    def conv_operand(v):
        base = pl.multiple_of(8 * v, 8)
        for q in range(3):
            for d, piece in enumerate(pieces(act0, 2 * v, base + PAD + 2 * (q - 1))):
                lhs[:, 128 * (3 * q + d) : 128 * (3 * q + d + 1)] = piece.astype(BF16)

    def conv():
        res[0:WIDE] = dot(lhs[...], w1[...])

    def conv_result(with_slope, v):
        base = pl.multiple_of(8 * v, 8)
        for h in range(2):
            u = 2 * v + h
            clear_sides(act1, u, base)
            clear_sides(f1, u, base)
            row_here = roww[pl.ds(u + 5, 1), :]
            for ch in range(3):
                row = base + PAD + CHUNK * ch
                added = res[CHUNK * ch : CHUNK * ch + CHUNK, 128 * h : 128 * h + 128]
                mask = mask_at(u, row, CHUNK)
                x = jnp.where(mask, (row_here + colr[pl.ds(row, CHUNK), :]) + added, 0.0)
                act, slope = gelu(x, with_slope)
                act1[u, pl.ds(row, CHUNK), :] = act
                f1[u, pl.ds(row, CHUNK), :] = x
                if with_slope:
                    d1[u, pl.ds(row, CHUNK), :] = jnp.where(mask, slope, 0.0)

    make_field(False, 0)
    make_field(True, 1)
    conv_operand(0)
    wide = jnp.concatenate([tlow[...], target[...], thigh[...]], axis=0)
    wide = jnp.concatenate([wide, jnp.zeros((48, 128), F32)], axis=1)
    wide = jnp.concatenate([wide, jnp.zeros((80, 384), F32)], axis=0)
    sheared = pltpu.roll(wide, 0, 1, stride=1, stride_axis=0)
    ts[4 + PAD : 4 + PAD + 312] = sheared.T[0:312]
    make_field(True, 2)
    conv()

    def first_conv(with_field, v, carry):
        conv_operand(v)
        conv_result(True, v - 1)
        if with_field:
            make_field(True, v + 2)
        conv()
        return carry

    lax.fori_loop(1, 5, functools.partial(first_conv, True), 0)
    lax.fori_loop(5, 7, functools.partial(first_conv, False), 0)
    conv_result(False, 6)

    def make_misfit(w, carry):
        base = pl.multiple_of(8 * w, 8)
        for at, count in ((0, 48), (48, 48), (96, 48), (144, 48), (192, 48), (240, 32)):
            row = base + PAD + at
            values = [rol[0:1] * f1[2 * w + 1 + h, pl.ds(row, count), :] for h in range(2)]
            for g in range(4):
                for q in range(3):
                    act = act1[2 * w + g, pl.ds(row + 4 * (q - 1), count), :]
                    for h in range(2):
                        p = g - h
                        if 0 <= p < 3:
                            tap = 3 * p + q
                            values[h] = values[h] + w2[8 * tap : 8 * tap + 1] * act
            for h in range(2):
                high, low = split(values[h])
                qbuf[at : at + count, 128 * h : 128 * h + 128] = high
                qbuf[at : at + count, 256 + 128 * h : 384 + 128 * h] = low
            high, low = split(ts[pl.ds(row, count), :])
            qbuf[at : at + count, 512:640] = high
            qbuf[at : at + count, 640:768] = low
        pick = jnp.where(iota((128, 256), 0) == 8 * w + lax.shift_right_logical(iota((128, 256), 1), 5), -1.0, 0.0).astype(BF16)
        wq[512:640] = pick
        wq[640:768] = pick
        value = dot(qbuf[...], wq[...]) * (1.0 / BAND)
        for h in range(2):
            u = 2 * w + 1 + h
            clear_sides(mis, u, base)
            for at, count in ((0, 96), (96, 96), (192, 80)):
                row = base + PAD + at
                mis[u, pl.ds(row, count), :] = jnp.where(
                    mask_at(u, row, count), value[at : at + count, 128 * h : 128 * h + 128], 0.0
                )
        return carry

    lax.fori_loop(0, 6, make_misfit, 0)

    def make_cotangent(v, carry):
        base = pl.multiple_of(8 * v, 8)
        sums = [[None] * 10 for h in range(2)]
        for h in range(2):
            clear_sides(g1, 2 * v + h, base)
        for ch in range(SPAN // 24):
            row = base + PAD + 24 * ch
            acts = [act1[2 * v + h, pl.ds(row, 24), :] for h in range(2)]
            backs = [None, None]
            centers = [None, None]
            for g in range(4):
                for q in range(3):
                    m = mis[2 * v - 1 + g, pl.ds(row - 4 * (q - 1), 24), :]
                    for h in range(2):
                        p = h + 2 - g
                        if 0 <= p < 3:
                            tap = 3 * p + q
                            term = w2[8 * tap : 8 * tap + 1] * m
                            backs[h] = term if backs[h] is None else backs[h] + term
                            part_sum = fold(acts[h] * m)
                            sums[h][tap] = part_sum if sums[h][tap] is None else sums[h][tap] + part_sum
                            if tap == 4:
                                centers[h] = m
            for h in range(2):
                u = 2 * v + h
                part_sum = fold(centers[h] * f1[u, pl.ds(row, 24), :])
                sums[h][9] = part_sum if sums[h][9] is None else sums[h][9] + part_sum
                g1[u, pl.ds(row, 24), :] = rol[0:1] * centers[h] + d1[u, pl.ds(row, 24), :] * backs[h]
        for tap in range(10):
            for h in range(2):
                source = 2 * v + h - (tap // 3 - 1) if tap < 9 else 2 * v + h
                own = jnp.logical_and(source >= FIRST_OWN, source <= LAST_OWN)
                tacc[8 * tap : 8 * tap + 8] += jnp.where(own, sums[h][tap], 0.0)
        return carry

    lax.fori_loop(1, 6, make_cotangent, 0)

    def adjoint_operand(w):
        base = pl.multiple_of(8 * w + 8, 8)
        for q in range(3):
            for d, piece in enumerate(pieces(g1, 2 * w + 2, base + PAD - 2 * (q - 1))):
                high, low = split(piece)
                lanes = slice(128 * (3 * q + d), 128 * (3 * q + d + 1))
                lhs2[0:WIDE, lanes] = high
                lhs2[WIDE : 2 * WIDE, lanes] = low

    def adjoint():
        res[...] = dot(lhs2[...], wa[...])

    def adjoint_result(w):
        base = pl.multiple_of(8 * w + 8, 8)
        for h in range(2):
            u = 2 * w + 3 + h
            total_row = None
            for ch in range(3):
                at = CHUNK * ch + 8 * h
                row = base + PAD + at
                lanes = slice(128 * h, 128 * h + 128)
                back = res[at : at + CHUNK, lanes] + res[WIDE + at : WIDE + at + CHUNK, lanes]
                value = g1[u, pl.ds(row, CHUNK), :] + d0[u, pl.ds(row, CHUNK), :] * back
                colacc[pl.ds(row, CHUNK), :] += value
                part = fold(value)
                total_row = part if total_row is None else total_row + part
            rowg[pl.ds(u - 3, 1), :] = jnp.sum(total_row, axis=0, keepdims=True)

    def collect(w):
        for h in range(2):
            u = 2 * w + 3 + h
            base = pl.multiple_of(8 * w + 8 + 8 * h, 8)
            at = pl.multiple_of(WIDE * (2 * w + h), 16)
            high, low = split(g1[u, pl.ds(base + PAD, WIDE), :])
            gall[pl.ds(at, WIDE), 0:128] = high
            gall[pl.ds(at, WIDE), 128:256] = low
            for q in range(3):
                row = base + PAD + 2 * (q - 1)
                ends = jnp.where(left, act0[u + 2, pl.ds(row, WIDE), :], act0[u, pl.ds(row, WIDE), :])
                xall[pl.ds(at, WIDE), 256 * q : 256 * q + 128] = ends.astype(BF16)
                xall[pl.ds(at, WIDE), 256 * q + 128 : 256 * q + 256] = act0[u + 1, pl.ds(row, WIDE), :].astype(BF16)

    adjoint_operand(0)
    collect(0)
    adjoint()

    def first_adjoint(w, carry):
        adjoint_operand(w)
        adjoint_result(w - 1)
        collect(w)
        adjoint()
        return carry

    lax.fori_loop(1, 4, first_adjoint, 0)
    adjoint_result(3)

    where_block = lane_block(8)
    for m in range(REACH + 1):
        packed = jnp.zeros((8, 128), F32)
        for b in range(4):
            row = 32 * m + 8 * b + HALO + PAD
            value = colacc[row : row + 8]
            value = value + pltpu.roll(value, 64, 1)
            value = value + pltpu.roll(value, 32, 1)
            packed = jnp.where(where_block == b, value, packed)
        colp[8 * m : 8 * m + 8] = packed
    columns = []
    for m in range(1, REACH + 1):
        columns.append(
            pltpu.make_async_remote_copy(
                colp.at[pl.ds(8 * m, 8)], cbuf.at[m - 1], sems.at[2], sems.at[3], device_id=(dev(m),), device_id_type=MESH
            )
        )
    for copy in columns:
        copy.start()

    fg[...] = dot_t(gall[...], xall[...])

    where_block = lane_block(32)
    for group in range(3):
        packed = jnp.zeros((32, 128), F32)
        for place in range(4):
            tap = 4 * group + place
            if tap > 8:
                continue
            p, q = tap // 3 - 1, tap % 3
            value = jnp.zeros((32, 128), F32)
            for b in range(4):
                source = b + 2 * p
                lanes = 256 * q + (128 if 0 <= source < 4 else 0)
                both = fg[32 * b : 32 * b + 32, lanes : lanes + 128] + fg[128 + 32 * b : 160 + 32 * b, lanes : lanes + 128]
                value = value + jnp.where(where_block == source % 4, both, 0.0)
            value = value + pltpu.roll(value, 64, 1)
            value = value + pltpu.roll(value, 32, 1)
            packed = jnp.where(where_block == place, value, packed)
        arbuf[128 + 32 * group : 160 + 32 * group] = packed
    for tap in range(10):
        arbuf[224 + tap : 225 + tap] = jnp.sum(tacc[8 * tap : 8 * tap + 8], axis=0, keepdims=True)
    sums = arbuf[224:240]
    sums = sums + pltpu.roll(sums, 64, 1)
    arbuf[224:240] = sums + pltpu.roll(sums, 32, 1)
    high, low = split(jnp.concatenate([tacc[8 * tap : 8 * tap + 8] for tap in range(9)], axis=1))
    by_read = jnp.sum(dot(high, k2t[...]) + dot(low, k2t[...]), axis=0, keepdims=True)
    arbuf[233:234, 0:32] = arbuf[233:234, 0:32] + by_read

    def chunk(q):
        return pl.ds(pl.multiple_of(q * part, part), part)

    def send(source, place, at, device):
        pltpu.make_async_remote_copy(
            source, place, sems.at[at], sems.at[at + 1], device_id=(device,), device_id_type=MESH
        ).start()

    def scatter(begin, end):
        for q in range(begin, end):
            s = lax.rem(q - plane + side, side)

            @pl.when(s > 0)
            def _():
                send(arbuf.at[pl.ds(q * part, part)], rsbuf.at[s - 1], 4, across(s))

    scatter(side // 2, side)

    where_block = lane_block(8)
    rows = rowg[...]
    for b in range(4):
        vbuf[1, pl.ds(b, 8, stride=4), :] = jnp.where(where_block == 1, pltpu.roll(rows, (32 - 32 * b) % 128, 1) if b != 1 else rows, 0.0)
    all_of(arbuf.at[pl.ds(0, 128)], sems.at[0])
    all_of(cbuf, sems.at[3])
    all_of(cbuf, sems.at[2])
    own = colp[0:8]
    for m in range(1, REACH + 1):
        own = own + cbuf[m - 1]
    for b in range(4):
        vbuf[0, 8 * b : 8 * b + 8] = jnp.where(where_block == 0, pltpu.roll(own, (128 - 32 * b) % 128, 1) if b else own, 0.0)
    both = vbuf[0] + vbuf[1]
    high, low = split(both)
    by_feature = dot_t(jnp.concatenate([high, low], axis=0), jnp.concatenate([feat[...]] * 2, axis=0))
    arbuf[0:64] = by_feature[0:64, 0:128]
    arbuf[64:128] = by_feature[0:64, 128:256]

    scatter(0, side // 2)
    weights = jnp.concatenate([col_t[...], row_t[...]], axis=0)
    by_bin = dot(high[:, 0:64], weights) + dot(low[:, 0:64], weights)
    gbuf[256:288] = by_bin[:, 0:128]
    gbuf[288:320] = by_bin[:, 128:256]
    keep = pltpu.make_async_copy(gbuf.at[pl.ds(256, 72)], red.at[pl.ds(256, 72)], loads.at[6])
    keep.start()
    all_of(rsbuf, sems.at[5])
    total = arbuf[chunk(plane), :]
    for s in range(1, side):
        total = total + rsbuf[s - 1]
    mine[...] = total
    send(mine, other, 10, me + 1 - 2 * lax.rem(me, 2))
    all_of(rsbuf, sems.at[4])
    all_of(other, sems.at[11])
    total = total + other[...]
    chip[...] = total
    bbuf[depth] = total
    for s in range(1, LINE):
        send(chip, bbuf.at[depth], 6, me + 2 * (lax.rem(depth + s, LINE) - depth))
    all_of(other, sems.at[10])
    all_of(bbuf.at[pl.ds(0, LINE - 1)], sems.at[7])
    total = bbuf[0]
    for q in range(1, LINE):
        total = total + bbuf[q]
    gbuf[chunk(plane), :] = total
    for s in range(1, side):
        send(gbuf.at[chunk(plane)], red.at[chunk(plane)], 8, across(s))
    place = pltpu.make_async_copy(gbuf.at[chunk(plane)], red.at[chunk(plane)], loads.at[7])
    place.start()
    all_of(bbuf.at[pl.ds(0, LINE - 1)], sems.at[6])
    all_of(rsbuf, sems.at[9])
    all_of(rsbuf, sems.at[8])
    keep.wait()
    place.wait()


def finish_kernel(red, gfeat, grow, gcol, gone, gtwo, gread):
    gfeat[:, 0:128] = red[256:288]
    gfeat[:, 128:256] = red[288:320]
    gcol[:, 0:128] = red[0:32]
    gcol[:, 128:256] = red[64:96]
    grow[:, 0:128] = red[32:64]
    grow[:, 128:256] = red[96:128]
    for group in range(3):
        block = red[128 + 32 * group : 160 + 32 * group].T
        count = 128 if group < 2 else 32
        gone[128 * group : 128 * group + count] = block[0:count]
    by_channel = red[224:240].T
    read = red[320:321, 0:32]
    for tap in range(9):
        gtwo[32 * tap : 32 * tap + 32] = by_channel[0:32, tap : tap + 1] * read
    gread[...] = red[233:234, 0:32]


def shards(n, features, row_proj, col_proj, first_filter, second_filter, readout, target):
    side = n // SIDE
    part = TOTAL // side
    vmem = pl.BlockSpec(memory_space=pltpu.VMEM)

    def shape(*dims):
        return jax.ShapeDtypeStruct(dims, F32)

    def real(*dims):
        return pltpu.VMEM(dims, F32)

    def half(*dims):
        return pltpu.VMEM(dims, BF16)

    k1 = first_filter.reshape(9 * PAIR, PAIR)
    k2 = second_filter.reshape(9 * PAIR, PAIR)
    ro = readout.reshape(1, PAIR)
    row_t, col_t = row_proj.T, col_proj.T
    hbm = pl.BlockSpec(memory_space=pltpu.HBM)
    scratch = dict(
        feat=half(ROWS, 256), row_t=half(PAIR, 256), col_t=half(PAIR, 256), target=real(ROWS, 256), k1=half(288, PAIR), k2=half(288, PAIR),
        proj=real(32, 128), sbuf=real(16, 128), rbuf=real(AHEAD + 2, 16, 128), tlow=real(8, 256), thigh=real(8, 256),
        roww=real(24, 128), w1=half(1152, 256), wa=half(1152, 256), w2=real(72, 128), rol=real(8, 128),
        colr=real(LENGTH, 128), mk=pltpu.VMEM((LENGTH, 128), jnp.int32), ts=real(LENGTH, 128),
        act0=real(GROUPS + 2, LENGTH, 128), d0=real(GROUPS, LENGTH, 128),
        act1=real(GROUPS, LENGTH, 128), f1=real(GROUPS, LENGTH, 128), d1=real(GROUPS, LENGTH, 128),
        mis=real(GROUPS, LENGTH, 128), g1=real(GROUPS, LENGTH, 128),
        lhs=half(WIDE, 1152), lhs2=half(2 * WIDE, 1152), k2t=half(1152, PAIR), res=real(2 * WIDE, 256), qbuf=half(WIDE, 768), wq=half(768, 256),
        xall=half(8 * WIDE, 768), gall=half(8 * WIDE, 256), fg=real(256, 768), tacc=real(80, 128),
        colacc=real(LENGTH, 128), tiles=real(288, 256), colp=real(72, 128), rowg=real(8, 128),
        cbuf=real(REACH, 8, 128), vbuf=real(2, 32, 128), arbuf=real(256, 128), rsbuf=real(side - 1, part, 128),
        bbuf=real(LINE, part, 128), mine=real(part, 128), other=real(part, 128), chip=real(part, 128), gbuf=real(328, 128), loads=SEM((8,)), sems=SEM((12,)),
    )
    red = pl.pallas_call(
        functools.partial(step_kernel, n),
        out_shape=shape(328, 128),
        in_specs=[hbm] * 6 + [vmem],
        out_specs=hbm,
        scratch_shapes=list(scratch.values()),
        compiler_params=pltpu.CompilerParams(
            collective_id=0, has_side_effects=True, vmem_limit_bytes=60 * 1024 * 1024
        ),
        name="step",
    )(features, row_t, col_t, target, k1, k2, ro)

    gfeat, grow, gcol, gone, gtwo, gread = pl.pallas_call(
        finish_kernel,
        out_shape=(shape(ROWS, 256), shape(32, 256), shape(32, 256), shape(288, 32), shape(288, 32), shape(1, 32)),
        in_specs=[vmem],
        out_specs=(vmem,) * 6,
        compiler_params=pltpu.CompilerParams(vmem_limit_bytes=4 * 1024 * 1024),
        name="finish",
    )(red)
    return gfeat, grow.T, gcol.T, gone.reshape(3, 3, PAIR, PAIR), gtwo.reshape(3, 3, PAIR, PAIR), gread.reshape(PAIR)


def solution(mesh):
    n = mesh.shape["diag"]
    in_specs = (P("diag", None), P(), P(), P(), P(), P(), P("diag", None))
    out_specs = (P("diag", None), P(), P(), P(), P(), P())
    return jax.shard_map(
        functools.partial(shards, n), mesh=mesh, in_specs=in_specs, out_specs=out_specs, check_vma=False
    )
```

```python
import functools
import math

import jax
import jax.numpy as jnp
from jax import lax
from jax.experimental import pallas as pl
from jax.experimental.pallas import tpu as pltpu
from jax.sharding import PartitionSpec as P

MESH = pl.DeviceIdType.MESH
F32, BF16 = jnp.float32, jnp.bfloat16

ROWS = 32
BAND = 256
PAIR = 32
HALO = 12
GROUPS = (ROWS + 2 * HALO) // 4
FIRST_OWN, LAST_OWN = 3, 10
PAD = 16
LENGTH = 352
WIDE, SPAN, CHUNK = 272, 264, 88
AHEAD = 9
REACH = 8
C0 = math.sqrt(2.0 / math.pi)
C1 = C0 * 0.044715
SIDE = 16
LINE = 8
TOTAL = 256
SEM = pltpu.SemaphoreType.DMA


def iota(shape, dim):
    return lax.broadcasted_iota(jnp.int32, shape, dim)


def lane_block(rows):
    return lax.shift_right_logical(iota((rows, 128), 1), 5)


def gelu(x, with_slope):
    cubic = C1 * (x * x)
    s = 0.5 * jnp.tanh(x * (cubic + C0)) + 0.5
    value = x * s
    slope = s + value * (1.0 - s) * (6.0 * cubic + 2.0 * C0) if with_slope else None
    return value.astype(BF16).astype(F32), slope


def split(x):
    high = x.astype(BF16)
    return high, (x - high.astype(F32)).astype(BF16)


def fold(x):
    total = x[0:8]
    for i in range(1, x.shape[0] // 8):
        total = total + x[8 * i : 8 * i + 8]
    return total


def dot(a, b):
    return jnp.dot(a, b, preferred_element_type=F32)


def dot_t(a, b):
    return lax.dot_general(a, b, (((0,), (0,)), ((), ())), preferred_element_type=F32)


def dot_nt(a, b):
    return lax.dot_general(a, b, (((1,), (1,)), ((), ())), preferred_element_type=F32)


def repeater(lanes):
    return (jnp.bitwise_and(iota((PAIR, lanes), 1), 31) == iota((PAIR, lanes), 0)).astype(F32).astype(BF16)


def spread(block):
    turned = [block] + [pltpu.roll(block, 32 * s, 1) for s in (1, 2, 3)]
    where_block = lane_block(8)
    outs = []
    for b in range(4):
        value = turned[(3 - b) % 4]
        for other in range(3):
            value = jnp.where(where_block == other, turned[(other - b) % 4], value)
        outs.append(value)
    return outs


def step_kernel(
    n, feat_in, row_in, col_in, target_in, k1_in, k2_in, ro_in, red,
    feat, row_t, col_t, target, k1, k2, ro,
    proj, sbuf, rbuf, tlow, thigh, roww, w1, wa, w2, rol, colr, mk, ts, act0, d0, act1, f1, d1, mis, g1,
    lhs, lhs2, k2t, res, qbuf, wq, xall, gall, fg, tacc, colacc, tiles, colp, rowg, cbuf, vbuf, arbuf, rsbuf, bbuf, mine, other, chip, gbuf,
    loads, sems,
):
    me = lax.axis_index("diag")
    start = me * ROWS
    side = n // SIDE
    part = TOTAL // side
    pos = lax.rem(me, SIDE)
    plane = lax.div(me, SIDE)
    depth = lax.div(pos, 2)

    def dev(step):
        return lax.rem(me + step + n, n)

    def across(s):
        return lax.rem(plane + s, side) * SIDE + pos

    fetches = [
        pltpu.make_async_copy(source, place, loads.at[i])
        for i, (source, place) in enumerate(
            ((feat_in, feat), (row_in, row_t), (col_in, col_t), (k1_in, k1), (k2_in, k2), (target_in, target), (ro_in, ro))
        )
    ]
    for fetch in fetches:
        fetch.start()

    barrier = pltpu.get_barrier_semaphore()
    for step in range(1, AHEAD + 1):
        for target_device in (dev(step), dev(-step)):
            pl.semaphore_signal(barrier, inc=1, device_id=(target_device,), device_id_type=MESH)

    def greet(sign, s, carry):
        pl.semaphore_signal(barrier, inc=1, device_id=(me + sign * s,), device_id_type=MESH)
        return carry

    lax.fori_loop(AHEAD + 1, SIDE - pos, functools.partial(greet, 1), 0)
    lax.fori_loop(AHEAD + 1, pos + 1, functools.partial(greet, -1), 0)

    def greet_across(s, carry):
        pl.semaphore_signal(barrier, inc=1, device_id=(across(s),), device_id_type=MESH)
        return carry

    lax.fori_loop(1, side, greet_across, 0)

    for fetch in fetches[0:3]:
        fetch.wait()
    proj[...] = dot_nt(feat[...], jnp.concatenate([row_t[...]] * 4, axis=0))
    cc = dot_nt(feat[...], jnp.concatenate([col_t[...]] * 4, axis=0))
    where_block = lane_block(8)
    row_c = jnp.zeros((8, 128), F32)
    col_c = jnp.zeros((8, 128), F32)
    for b in range(4):
        row_c = jnp.where(where_block == b, proj[pl.ds(b, 8, stride=4), :], row_c)
        col_c = jnp.where(where_block == b, cc[8 * b : 8 * b + 8], col_c)
    sbuf[0:8] = col_c
    sbuf[8:16] = row_c
    greeted = jnp.maximum(SIDE - AHEAD - 1 - pos, 0) + jnp.maximum(pos - AHEAD, 0)
    pl.semaphore_wait(barrier, 2 * AHEAD + greeted + side - 1)
    gathers = []
    for m in range(AHEAD + 1, 2, -1):
        gathers.append(
            pltpu.make_async_remote_copy(
                sbuf.at[pl.ds(0, 8)], rbuf.at[m, pl.ds(0, 8)], sems.at[0], sems.at[1], device_id=(dev(1 - m),), device_id_type=MESH
            )
        )
    for slot, step in ((0, 1), (2, -1)):
        gathers.append(
            pltpu.make_async_remote_copy(sbuf, rbuf.at[slot], sems.at[0], sems.at[1], device_id=(dev(step),), device_id_type=MESH)
        )
    gathers.append(
        pltpu.make_async_remote_copy(
            target_in.at[pl.ds(24, 8)], tlow, sems.at[0], sems.at[1], device_id=(dev(1),), device_id_type=MESH
        )
    )
    gathers.append(
        pltpu.make_async_remote_copy(
            target_in.at[pl.ds(0, 8)], thigh, sems.at[0], sems.at[1], device_id=(dev(-1),), device_id_type=MESH
        )
    )
    for copy in gathers:
        copy.start()

    for fetch in fetches[3:7]:
        fetch.wait()
    rep8 = repeater(256)
    where_out = lax.shift_right_logical(iota((PAIR, 256), 1), 5)

    def build(weights, sign):
        for q in range(3):
            for place, ri in enumerate((8, 9, -2, -1, 0, 1, 2, 3, 4, 5, 6, 7)):
                value = jnp.zeros((PAIR, 256), F32)
                for p in range(3):
                    tap = 3 * p + q
                    ro_here = ri - sign * 2 * (p - 1)
                    if 0 <= ro_here < 8:
                        value = jnp.where(where_out == ro_here, tiles[32 * tap : 32 * tap + 32], value)
                row = (q * 12 + place) * 32
                weights[row : row + 32] = value.astype(BF16)

    tiles[...] = dot(k1[...], rep8)
    build(w1, 1)
    tiles[...] = dot_t(jnp.concatenate([k1[32 * tap : 32 * tap + 32] for tap in range(9)], axis=1), rep8)
    build(wa, -1)
    ro8 = jnp.broadcast_to(ro[...].astype(F32), (8, PAIR)).astype(BF16)
    rol[...] = dot(ro8, repeater(128))
    for tap in range(9):
        for b in range(4):
            row = 128 * tap + 32 * b
            k2t[row : row + 32] = k2[32 * tap : 32 * tap + 32]
        w2[8 * tap : 8 * tap + 8] = dot_nt(ro8, k2t[128 * tap : 128 * tap + 128])
    gbuf[320:328] = rol[...]

    same = lax.shift_right_logical(iota((256, 256), 0), 5) == lax.shift_right_logical(iota((256, 256), 1), 5)
    ones = same.astype(F32).astype(BF16)
    wq[0:256] = ones
    wq[256:512] = ones
    act0[0] = jnp.zeros((LENGTH, 128), F32)
    act0[GROUPS + 1] = jnp.zeros((LENGTH, 128), F32)
    colacc[...] = jnp.zeros((LENGTH, 128), F32)
    tacc[...] = jnp.zeros((80, 128), F32)
    ts[...] = jnp.zeros((LENGTH, 128), F32)
    arbuf[224:256] = jnp.zeros((32, 128), F32)
    column = iota((LENGTH, 128), 0) - PAD
    mk[...] = jnp.where(column + (start - HALO) < n * ROWS, column - lane_block(LENGTH), 1 << 20)

    def all_of(place, sem):
        pltpu.make_async_copy(place, place, sem).wait()

    all_of(arbuf.at[pl.ds(0, 128)], sems.at[1])
    for m in range(AHEAD + 2):
        for b, value in enumerate(spread(col_c if m == 1 else rbuf[m, 0:8])):
            row = 32 * (m - 1) + 8 * b + HALO + PAD
            if row >= 0 and row + 8 <= LENGTH:
                colr[row : row + 8] = value
    roww[0:8] = rbuf[0, 8:16]
    roww[8:16] = row_c
    roww[16:24] = rbuf[2, 8:16]
    def first_column(u):
        return pl.multiple_of(8 * lax.shift_right_logical(u, 1), 8)

    def mask_at(u, row, count):
        shift = 4 * u - jnp.where(start + 4 * u - HALO >= 0, 0, 1 << 20)
        return jnp.bitwise_and(mk[pl.ds(row, count), :] - shift, -BAND) == 0

    def clear_sides(buffer, index, base):
        buffer[index, pl.ds(base, 16), :] = jnp.zeros((16, 128), F32)
        buffer[index, pl.ds(base + PAD + SPAN, 24), :] = jnp.zeros((24, 128), F32)

    left = lane_block(WIDE) < 2

    def pieces(buffer, index, row):
        ends = jnp.where(left, buffer[index + 3, pl.ds(row, WIDE), :], buffer[index, pl.ds(row, WIDE), :])
        return ends, buffer[index + 1, pl.ds(row, WIDE), :], buffer[index + 2, pl.ds(row, WIDE), :]

    def make_field(with_slope, v):
        base = pl.multiple_of(8 * v, 8)
        for h in range(2):
            u = 2 * v + h
            clear_sides(act0, u + 1, base)
            row_here = roww[pl.ds(u + 5, 1), :]
            for ch in range(3):
                row = base + PAD + CHUNK * ch
                mask = mask_at(u, row, CHUNK)
                x = jnp.where(mask, row_here + colr[pl.ds(row, CHUNK), :], 0.0)
                act, slope = gelu(x, with_slope)
                act0[u + 1, pl.ds(row, CHUNK), :] = act
                if with_slope:
                    d0[u, pl.ds(row, CHUNK), :] = jnp.where(mask, slope, 0.0)

    def conv_operand(v):
        base = pl.multiple_of(8 * v, 8)
        for q in range(3):
            for d, piece in enumerate(pieces(act0, 2 * v, base + PAD + 2 * (q - 1))):
                lhs[:, 128 * (3 * q + d) : 128 * (3 * q + d + 1)] = piece.astype(BF16)

    def conv():
        res[0:WIDE] = dot(lhs[...], w1[...])

    def conv_result(with_slope, v):
        base = pl.multiple_of(8 * v, 8)
        for h in range(2):
            u = 2 * v + h
            clear_sides(act1, u, base)
            clear_sides(f1, u, base)
            row_here = roww[pl.ds(u + 5, 1), :]
            for ch in range(3):
                row = base + PAD + CHUNK * ch
                added = res[CHUNK * ch : CHUNK * ch + CHUNK, 128 * h : 128 * h + 128]
                mask = mask_at(u, row, CHUNK)
                x = jnp.where(mask, (row_here + colr[pl.ds(row, CHUNK), :]) + added, 0.0)
                act, slope = gelu(x, with_slope)
                act1[u, pl.ds(row, CHUNK), :] = act
                f1[u, pl.ds(row, CHUNK), :] = x
                if with_slope:
                    d1[u, pl.ds(row, CHUNK), :] = jnp.where(mask, slope, 0.0)

    make_field(False, 0)
    make_field(True, 1)
    conv_operand(0)
    wide = jnp.concatenate([tlow[...], target[...], thigh[...]], axis=0)
    wide = jnp.concatenate([wide, jnp.zeros((48, 128), F32)], axis=1)
    wide = jnp.concatenate([wide, jnp.zeros((80, 384), F32)], axis=0)
    sheared = pltpu.roll(wide, 0, 1, stride=1, stride_axis=0)
    ts[4 + PAD : 4 + PAD + 312] = sheared.T[0:312]
    make_field(True, 2)
    conv()

    def first_conv(with_field, v, carry):
        conv_operand(v)
        conv_result(True, v - 1)
        if with_field:
            make_field(True, v + 2)
        conv()
        return carry

    lax.fori_loop(1, 5, functools.partial(first_conv, True), 0)
    lax.fori_loop(5, 7, functools.partial(first_conv, False), 0)
    conv_result(False, 6)

    def make_misfit(w, carry):
        base = pl.multiple_of(8 * w, 8)
        for at, count in ((0, 48), (48, 48), (96, 48), (144, 48), (192, 48), (240, 32)):
            row = base + PAD + at
            values = [rol[0:1] * f1[2 * w + 1 + h, pl.ds(row, count), :] for h in range(2)]
            for g in range(4):
                for q in range(3):
                    act = act1[2 * w + g, pl.ds(row + 4 * (q - 1), count), :]
                    for h in range(2):
                        p = g - h
                        if 0 <= p < 3:
                            tap = 3 * p + q
                            values[h] = values[h] + w2[8 * tap : 8 * tap + 1] * act
            for h in range(2):
                high, low = split(values[h])
                qbuf[at : at + count, 128 * h : 128 * h + 128] = high
                qbuf[at : at + count, 256 + 128 * h : 384 + 128 * h] = low
            high, low = split(ts[pl.ds(row, count), :])
            qbuf[at : at + count, 512:640] = high
            qbuf[at : at + count, 640:768] = low
        pick = jnp.where(iota((128, 256), 0) == 8 * w + lax.shift_right_logical(iota((128, 256), 1), 5), -1.0, 0.0).astype(BF16)
        wq[512:640] = pick
        wq[640:768] = pick
        value = dot(qbuf[...], wq[...]) * (1.0 / BAND)
        for h in range(2):
            u = 2 * w + 1 + h
            clear_sides(mis, u, base)
            for at, count in ((0, 96), (96, 96), (192, 80)):
                row = base + PAD + at
                mis[u, pl.ds(row, count), :] = jnp.where(
                    mask_at(u, row, count), value[at : at + count, 128 * h : 128 * h + 128], 0.0
                )
        return carry

    lax.fori_loop(0, 6, make_misfit, 0)

    def make_cotangent(v, carry):
        base = pl.multiple_of(8 * v, 8)
        sums = [[None] * 10 for h in range(2)]
        for h in range(2):
            clear_sides(g1, 2 * v + h, base)
        for ch in range(SPAN // 24):
            row = base + PAD + 24 * ch
            acts = [act1[2 * v + h, pl.ds(row, 24), :] for h in range(2)]
            backs = [None, None]
            centers = [None, None]
            for g in range(4):
                for q in range(3):
                    m = mis[2 * v - 1 + g, pl.ds(row - 4 * (q - 1), 24), :]
                    for h in range(2):
                        p = h + 2 - g
                        if 0 <= p < 3:
                            tap = 3 * p + q
                            term = w2[8 * tap : 8 * tap + 1] * m
                            backs[h] = term if backs[h] is None else backs[h] + term
                            part_sum = fold(acts[h] * m)
                            sums[h][tap] = part_sum if sums[h][tap] is None else sums[h][tap] + part_sum
                            if tap == 4:
                                centers[h] = m
            for h in range(2):
                u = 2 * v + h
                part_sum = fold(centers[h] * f1[u, pl.ds(row, 24), :])
                sums[h][9] = part_sum if sums[h][9] is None else sums[h][9] + part_sum
                g1[u, pl.ds(row, 24), :] = rol[0:1] * centers[h] + d1[u, pl.ds(row, 24), :] * backs[h]
        for tap in range(10):
            for h in range(2):
                source = 2 * v + h - (tap // 3 - 1) if tap < 9 else 2 * v + h
                own = jnp.logical_and(source >= FIRST_OWN, source <= LAST_OWN)
                tacc[8 * tap : 8 * tap + 8] += jnp.where(own, sums[h][tap], 0.0)
        return carry

    lax.fori_loop(1, 6, make_cotangent, 0)

    def adjoint_operand(w):
        base = pl.multiple_of(8 * w + 8, 8)
        for q in range(3):
            for d, piece in enumerate(pieces(g1, 2 * w + 2, base + PAD - 2 * (q - 1))):
                high, low = split(piece)
                lanes = slice(128 * (3 * q + d), 128 * (3 * q + d + 1))
                lhs2[0:WIDE, lanes] = high
                lhs2[WIDE : 2 * WIDE, lanes] = low

    def adjoint():
        res[...] = dot(lhs2[...], wa[...])

    def adjoint_result(w):
        base = pl.multiple_of(8 * w + 8, 8)
        for h in range(2):
            u = 2 * w + 3 + h
            total_row = None
            for ch in range(3):
                at = CHUNK * ch + 8 * h
                row = base + PAD + at
                lanes = slice(128 * h, 128 * h + 128)
                back = res[at : at + CHUNK, lanes] + res[WIDE + at : WIDE + at + CHUNK, lanes]
                value = g1[u, pl.ds(row, CHUNK), :] + d0[u, pl.ds(row, CHUNK), :] * back
                colacc[pl.ds(row, CHUNK), :] += value
                part = fold(value)
                total_row = part if total_row is None else total_row + part
            rowg[pl.ds(u - 3, 1), :] = jnp.sum(total_row, axis=0, keepdims=True)

    def collect(w):
        for h in range(2):
            u = 2 * w + 3 + h
            base = pl.multiple_of(8 * w + 8 + 8 * h, 8)
            at = pl.multiple_of(WIDE * (2 * w + h), 16)
            high, low = split(g1[u, pl.ds(base + PAD, WIDE), :])
            gall[pl.ds(at, WIDE), 0:128] = high
            gall[pl.ds(at, WIDE), 128:256] = low
            for q in range(3):
                row = base + PAD + 2 * (q - 1)
                ends = jnp.where(left, act0[u + 2, pl.ds(row, WIDE), :], act0[u, pl.ds(row, WIDE), :])
                xall[pl.ds(at, WIDE), 256 * q : 256 * q + 128] = ends.astype(BF16)
                xall[pl.ds(at, WIDE), 256 * q + 128 : 256 * q + 256] = act0[u + 1, pl.ds(row, WIDE), :].astype(BF16)

    adjoint_operand(0)
    collect(0)
    adjoint()

    def first_adjoint(w, carry):
        adjoint_operand(w)
        adjoint_result(w - 1)
        collect(w)
        adjoint()
        return carry

    lax.fori_loop(1, 4, first_adjoint, 0)
    adjoint_result(3)

    where_block = lane_block(8)
    for m in range(REACH + 1):
        packed = jnp.zeros((8, 128), F32)
        for b in range(4):
            row = 32 * m + 8 * b + HALO + PAD
            value = colacc[row : row + 8]
            value = value + pltpu.roll(value, 64, 1)
            value = value + pltpu.roll(value, 32, 1)
            packed = jnp.where(where_block == b, value, packed)
        colp[8 * m : 8 * m + 8] = packed
    columns = []
    for m in range(1, REACH + 1):
        columns.append(
            pltpu.make_async_remote_copy(
                colp.at[pl.ds(8 * m, 8)], cbuf.at[m - 1], sems.at[2], sems.at[3], device_id=(dev(m),), device_id_type=MESH
            )
        )
    for copy in columns:
        copy.start()

    fg[...] = dot_t(gall[...], xall[...])

    where_block = lane_block(32)
    for group in range(3):
        packed = jnp.zeros((32, 128), F32)
        for place in range(4):
            tap = 4 * group + place
            if tap > 8:
                continue
            p, q = tap // 3 - 1, tap % 3
            value = jnp.zeros((32, 128), F32)
            for b in range(4):
                source = b + 2 * p
                lanes = 256 * q + (128 if 0 <= source < 4 else 0)
                both = fg[32 * b : 32 * b + 32, lanes : lanes + 128] + fg[128 + 32 * b : 160 + 32 * b, lanes : lanes + 128]
                value = value + jnp.where(where_block == source % 4, both, 0.0)
            value = value + pltpu.roll(value, 64, 1)
            value = value + pltpu.roll(value, 32, 1)
            packed = jnp.where(where_block == place, value, packed)
        arbuf[128 + 32 * group : 160 + 32 * group] = packed
    for tap in range(10):
        arbuf[224 + tap : 225 + tap] = jnp.sum(tacc[8 * tap : 8 * tap + 8], axis=0, keepdims=True)
    sums = arbuf[224:240]
    sums = sums + pltpu.roll(sums, 64, 1)
    arbuf[224:240] = sums + pltpu.roll(sums, 32, 1)
    high, low = split(jnp.concatenate([tacc[8 * tap : 8 * tap + 8] for tap in range(9)], axis=1))
    by_read = jnp.sum(dot(high, k2t[...]) + dot(low, k2t[...]), axis=0, keepdims=True)
    arbuf[233:234, 0:32] = arbuf[233:234, 0:32] + by_read

    def chunk(q):
        return pl.ds(pl.multiple_of(q * part, part), part)

    def send(source, place, at, device):
        pltpu.make_async_remote_copy(
            source, place, sems.at[at], sems.at[at + 1], device_id=(device,), device_id_type=MESH
        ).start()

    def scatter(begin, end):
        for q in range(begin, end):
            s = lax.rem(q - plane + side, side)

            @pl.when(s > 0)
            def _():
                send(arbuf.at[pl.ds(q * part, part)], rsbuf.at[s - 1], 4, across(s))

    scatter(side // 2, side)

    where_block = lane_block(8)
    rows = rowg[...]
    for b in range(4):
        vbuf[1, pl.ds(b, 8, stride=4), :] = jnp.where(where_block == 1, pltpu.roll(rows, (32 - 32 * b) % 128, 1) if b != 1 else rows, 0.0)
    all_of(arbuf.at[pl.ds(0, 128)], sems.at[0])
    all_of(cbuf, sems.at[3])
    all_of(cbuf, sems.at[2])
    own = colp[0:8]
    for m in range(1, REACH + 1):
        own = own + cbuf[m - 1]
    for b in range(4):
        vbuf[0, 8 * b : 8 * b + 8] = jnp.where(where_block == 0, pltpu.roll(own, (128 - 32 * b) % 128, 1) if b else own, 0.0)
    both = vbuf[0] + vbuf[1]
    high, low = split(both)
    by_feature = dot_t(jnp.concatenate([high, low], axis=0), jnp.concatenate([feat[...]] * 2, axis=0))
    arbuf[0:64] = by_feature[0:64, 0:128]
    arbuf[64:128] = by_feature[0:64, 128:256]

    scatter(0, side // 2)
    weights = jnp.concatenate([col_t[...], row_t[...]], axis=0)
    by_bin = dot(high[:, 0:64], weights) + dot(low[:, 0:64], weights)
    gbuf[256:288] = by_bin[:, 0:128]
    gbuf[288:320] = by_bin[:, 128:256]
    keep = pltpu.make_async_copy(gbuf.at[pl.ds(256, 72)], red.at[pl.ds(256, 72)], loads.at[7])
    keep.start()
    all_of(rsbuf, sems.at[5])
    total = arbuf[chunk(plane), :]
    for s in range(1, side):
        total = total + rsbuf[s - 1]
    mine[...] = total
    send(mine, other, 10, me + 1 - 2 * lax.rem(me, 2))
    all_of(rsbuf, sems.at[4])
    all_of(other, sems.at[11])
    total = total + other[...]
    chip[...] = total
    bbuf[depth] = total
    for s in range(1, LINE):
        send(chip, bbuf.at[depth], 6, me + 2 * (lax.rem(depth + s, LINE) - depth))
    all_of(other, sems.at[10])
    all_of(bbuf.at[pl.ds(0, LINE - 1)], sems.at[7])
    total = bbuf[0]
    for q in range(1, LINE):
        total = total + bbuf[q]
    gbuf[chunk(plane), :] = total
    for s in range(1, side):
        send(gbuf.at[chunk(plane)], red.at[chunk(plane)], 8, across(s))
    place = pltpu.make_async_copy(gbuf.at[chunk(plane)], red.at[chunk(plane)], loads.at[8])
    place.start()
    all_of(bbuf.at[pl.ds(0, LINE - 1)], sems.at[6])
    all_of(rsbuf, sems.at[9])
    all_of(rsbuf, sems.at[8])
    keep.wait()
    place.wait()


def finish_kernel(red, gfeat, grow, gcol, gone, gtwo, gread):
    gfeat[:, 0:128] = red[256:288]
    gfeat[:, 128:256] = red[288:320]
    gcol[:, 0:128] = red[0:32]
    gcol[:, 128:256] = red[64:96]
    grow[:, 0:128] = red[32:64]
    grow[:, 128:256] = red[96:128]
    for group in range(3):
        block = red[128 + 32 * group : 160 + 32 * group].T
        count = 128 if group < 2 else 32
        gone[128 * group : 128 * group + count] = block[0:count]
    by_channel = red[224:240].T
    read = red[320:321, 0:32]
    for tap in range(9):
        gtwo[32 * tap : 32 * tap + 32] = by_channel[0:32, tap : tap + 1] * read
    gread[...] = red[233:234, 0:32]


def shards(n, features, row_proj, col_proj, first_filter, second_filter, readout, target):
    side = n // SIDE
    part = TOTAL // side
    vmem = pl.BlockSpec(memory_space=pltpu.VMEM)

    def shape(*dims):
        return jax.ShapeDtypeStruct(dims, F32)

    def real(*dims):
        return pltpu.VMEM(dims, F32)

    def half(*dims):
        return pltpu.VMEM(dims, BF16)

    k1 = first_filter.reshape(9 * PAIR, PAIR)
    k2 = second_filter.reshape(9 * PAIR, PAIR)
    ro = readout.reshape(1, PAIR)
    row_t, col_t = row_proj.T, col_proj.T
    hbm = pl.BlockSpec(memory_space=pltpu.HBM)
    scratch = dict(
        feat=half(ROWS, 256), row_t=half(PAIR, 256), col_t=half(PAIR, 256), target=real(ROWS, 256), k1=half(288, PAIR), k2=half(288, PAIR), ro=half(1, PAIR),
        proj=real(32, 128), sbuf=real(16, 128), rbuf=real(AHEAD + 2, 16, 128), tlow=real(8, 256), thigh=real(8, 256),
        roww=real(24, 128), w1=half(1152, 256), wa=half(1152, 256), w2=real(72, 128), rol=real(8, 128),
        colr=real(LENGTH, 128), mk=pltpu.VMEM((LENGTH, 128), jnp.int32), ts=real(LENGTH, 128),
        act0=real(GROUPS + 2, LENGTH, 128), d0=real(GROUPS, LENGTH, 128),
        act1=real(GROUPS, LENGTH, 128), f1=real(GROUPS, LENGTH, 128), d1=real(GROUPS, LENGTH, 128),
        mis=real(GROUPS, LENGTH, 128), g1=real(GROUPS, LENGTH, 128),
        lhs=half(WIDE, 1152), lhs2=half(2 * WIDE, 1152), k2t=half(1152, PAIR), res=real(2 * WIDE, 256), qbuf=half(WIDE, 768), wq=half(768, 256),
        xall=half(8 * WIDE, 768), gall=half(8 * WIDE, 256), fg=real(256, 768), tacc=real(80, 128),
        colacc=real(LENGTH, 128), tiles=real(288, 256), colp=real(72, 128), rowg=real(8, 128),
        cbuf=real(REACH, 8, 128), vbuf=real(2, 32, 128), arbuf=real(256, 128), rsbuf=real(side - 1, part, 128),
        bbuf=real(LINE, part, 128), mine=real(part, 128), other=real(part, 128), chip=real(part, 128), gbuf=real(328, 128), loads=SEM((9,)), sems=SEM((12,)),
    )
    red = pl.pallas_call(
        functools.partial(step_kernel, n),
        out_shape=shape(328, 128),
        in_specs=[hbm] * 7,
        out_specs=hbm,
        scratch_shapes=list(scratch.values()),
        compiler_params=pltpu.CompilerParams(
            collective_id=0, has_side_effects=True, vmem_limit_bytes=60 * 1024 * 1024
        ),
        name="step",
    )(features, row_t, col_t, target, k1, k2, ro)

    gfeat, grow, gcol, gone, gtwo, gread = pl.pallas_call(
        finish_kernel,
        out_shape=(shape(ROWS, 256), shape(32, 256), shape(32, 256), shape(288, 32), shape(288, 32), shape(1, 32)),
        in_specs=[vmem],
        out_specs=(vmem,) * 6,
        compiler_params=pltpu.CompilerParams(vmem_limit_bytes=4 * 1024 * 1024),
        name="finish",
    )(red)
    return gfeat, grow.T, gcol.T, gone.reshape(3, 3, PAIR, PAIR), gtwo.reshape(3, 3, PAIR, PAIR), gread.reshape(PAIR)


def solution(mesh):
    n = mesh.shape["diag"]
    in_specs = (P("diag", None), P(), P(), P(), P(), P(), P("diag", None))
    out_specs = (P("diag", None), P(), P(), P(), P(), P())
    return jax.shard_map(
        functools.partial(shards, n), mesh=mesh, in_specs=in_specs, out_specs=out_specs, check_vma=False
    )
```

```python
import functools
import math

import jax
import jax.numpy as jnp
from jax import lax
from jax.experimental import pallas as pl
from jax.experimental.pallas import tpu as pltpu
from jax.sharding import PartitionSpec as P

MESH = pl.DeviceIdType.MESH
F32, BF16 = jnp.float32, jnp.bfloat16

ROWS = 32
BAND = 256
PAIR = 32
HALO = 12
GROUPS = (ROWS + 2 * HALO) // 4
FIRST_OWN, LAST_OWN = 3, 10
PAD = 16
LENGTH = 352
WIDE, SPAN, CHUNK = 272, 264, 88
AHEAD = 9
REACH = 8
C0 = math.sqrt(2.0 / math.pi)
C1 = C0 * 0.044715
SIDE = 16
LINE = 8
TOTAL = 256
SEM = pltpu.SemaphoreType.DMA


def iota(shape, dim):
    return lax.broadcasted_iota(jnp.int32, shape, dim)


def lane_block(rows):
    return lax.shift_right_logical(iota((rows, 128), 1), 5)


def gelu(x, with_slope):
    cubic = C1 * (x * x)
    s = 0.5 * jnp.tanh(x * (cubic + C0)) + 0.5
    value = x * s
    slope = s + value * (1.0 - s) * (6.0 * cubic + 2.0 * C0) if with_slope else None
    return value.astype(BF16).astype(F32), slope


def split(x):
    high = x.astype(BF16)
    return high, (x - high.astype(F32)).astype(BF16)


def fold(x):
    total = x[0:8]
    for i in range(1, x.shape[0] // 8):
        total = total + x[8 * i : 8 * i + 8]
    return total


def dot(a, b):
    return jnp.dot(a, b, preferred_element_type=F32)


def dot_t(a, b):
    return lax.dot_general(a, b, (((0,), (0,)), ((), ())), preferred_element_type=F32)


def dot_nt(a, b):
    return lax.dot_general(a, b, (((1,), (1,)), ((), ())), preferred_element_type=F32)


def repeater(lanes):
    return (jnp.bitwise_and(iota((PAIR, lanes), 1), 31) == iota((PAIR, lanes), 0)).astype(F32).astype(BF16)


def spread(block):
    turned = [block] + [pltpu.roll(block, 32 * s, 1) for s in (1, 2, 3)]
    where_block = lane_block(8)
    outs = []
    for b in range(4):
        value = turned[(3 - b) % 4]
        for other in range(3):
            value = jnp.where(where_block == other, turned[(other - b) % 4], value)
        outs.append(value)
    return outs


def step_kernel(
    n, feat_in, row_in, col_in, target_in, k1_in, k2_in, ro_in, red,
    feat, row_t, col_t, target, k1, k2, ro,
    proj, sbuf, rbuf, tlow, thigh, roww, w1, wa, w2, rol, colr, mk, ts, act0, d0, act1, f1, d1, mis, g1,
    lhs, lhs2, k2t, res, qbuf, wq, xall, gall, fg, tacc, colacc, tiles, colp, rowg, cbuf, vbuf, arbuf, rsbuf, bbuf, mine, other, chip, gbuf,
    loads, sems,
):
    me = lax.axis_index("diag")
    start = me * ROWS
    side = n // SIDE
    part = TOTAL // side
    pos = lax.rem(me, SIDE)
    plane = lax.div(me, SIDE)
    depth = lax.div(pos, 2)

    def dev(step):
        return lax.rem(me + step + n, n)

    def across(s):
        return lax.rem(plane + s, side) * SIDE + pos

    fetches = [
        pltpu.make_async_copy(source, place, loads.at[i])
        for i, (source, place) in enumerate(
            ((feat_in, feat), (row_in, row_t), (col_in, col_t), (k1_in, k1), (k2_in, k2), (target_in, target), (ro_in, ro))
        )
    ]
    for fetch in fetches:
        fetch.start()

    barrier = pltpu.get_barrier_semaphore()
    for step in range(1, AHEAD + 1):
        for target_device in (dev(step), dev(-step)):
            pl.semaphore_signal(barrier, inc=1, device_id=(target_device,), device_id_type=MESH)

    def greet(sign, s, carry):
        pl.semaphore_signal(barrier, inc=1, device_id=(me + sign * 2 * s,), device_id_type=MESH)
        return carry

    lax.fori_loop(AHEAD // 2 + 1, LINE - depth, functools.partial(greet, 1), 0)
    lax.fori_loop(AHEAD // 2 + 1, depth + 1, functools.partial(greet, -1), 0)

    def greet_across(s, carry):
        pl.semaphore_signal(barrier, inc=1, device_id=(across(s),), device_id_type=MESH)
        return carry

    lax.fori_loop(1, side, greet_across, 0)

    for fetch in fetches[0:3]:
        fetch.wait()
    proj[...] = dot_nt(feat[...], jnp.concatenate([row_t[...]] * 4, axis=0))
    cc = dot_nt(feat[...], jnp.concatenate([col_t[...]] * 4, axis=0))
    where_block = lane_block(8)
    row_c = jnp.zeros((8, 128), F32)
    col_c = jnp.zeros((8, 128), F32)
    for b in range(4):
        row_c = jnp.where(where_block == b, proj[pl.ds(b, 8, stride=4), :], row_c)
        col_c = jnp.where(where_block == b, cc[8 * b : 8 * b + 8], col_c)
    sbuf[0:8] = col_c
    sbuf[8:16] = row_c
    greeted = jnp.maximum(LINE - AHEAD // 2 - 1 - depth, 0) + jnp.maximum(depth - AHEAD // 2, 0)
    pl.semaphore_wait(barrier, 2 * AHEAD + greeted + side - 1)
    gathers = []
    for m in range(AHEAD + 1, 2, -1):
        gathers.append(
            pltpu.make_async_remote_copy(
                sbuf.at[pl.ds(0, 8)], rbuf.at[m, pl.ds(0, 8)], sems.at[0], sems.at[1], device_id=(dev(1 - m),), device_id_type=MESH
            )
        )
    for slot, step in ((0, 1), (2, -1)):
        gathers.append(
            pltpu.make_async_remote_copy(sbuf, rbuf.at[slot], sems.at[0], sems.at[1], device_id=(dev(step),), device_id_type=MESH)
        )
    gathers.append(
        pltpu.make_async_remote_copy(
            target_in.at[pl.ds(24, 8)], tlow, sems.at[0], sems.at[1], device_id=(dev(1),), device_id_type=MESH
        )
    )
    gathers.append(
        pltpu.make_async_remote_copy(
            target_in.at[pl.ds(0, 8)], thigh, sems.at[0], sems.at[1], device_id=(dev(-1),), device_id_type=MESH
        )
    )
    for copy in gathers:
        copy.start()

    for fetch in fetches[3:7]:
        fetch.wait()
    rep8 = repeater(256)
    where_out = lax.shift_right_logical(iota((PAIR, 256), 1), 5)

    def build(weights, sign):
        for q in range(3):
            for place, ri in enumerate((8, 9, -2, -1, 0, 1, 2, 3, 4, 5, 6, 7)):
                value = jnp.zeros((PAIR, 256), F32)
                for p in range(3):
                    tap = 3 * p + q
                    ro_here = ri - sign * 2 * (p - 1)
                    if 0 <= ro_here < 8:
                        value = jnp.where(where_out == ro_here, tiles[32 * tap : 32 * tap + 32], value)
                row = (q * 12 + place) * 32
                weights[row : row + 32] = value.astype(BF16)

    tiles[...] = dot(k1[...], rep8)
    build(w1, 1)
    tiles[...] = dot_t(jnp.concatenate([k1[32 * tap : 32 * tap + 32] for tap in range(9)], axis=1), rep8)
    build(wa, -1)
    ro8 = jnp.broadcast_to(ro[...].astype(F32), (8, PAIR)).astype(BF16)
    rol[...] = dot(ro8, repeater(128))
    for tap in range(9):
        for b in range(4):
            row = 128 * tap + 32 * b
            k2t[row : row + 32] = k2[32 * tap : 32 * tap + 32]
        w2[8 * tap : 8 * tap + 8] = dot_nt(ro8, k2t[128 * tap : 128 * tap + 128])
    gbuf[320:328] = rol[...]

    same = lax.shift_right_logical(iota((256, 256), 0), 5) == lax.shift_right_logical(iota((256, 256), 1), 5)
    ones = same.astype(F32).astype(BF16)
    wq[0:256] = ones
    wq[256:512] = ones
    act0[0] = jnp.zeros((LENGTH, 128), F32)
    act0[GROUPS + 1] = jnp.zeros((LENGTH, 128), F32)
    colacc[...] = jnp.zeros((LENGTH, 128), F32)
    tacc[...] = jnp.zeros((80, 128), F32)
    ts[...] = jnp.zeros((LENGTH, 128), F32)
    arbuf[224:256] = jnp.zeros((32, 128), F32)
    column = iota((LENGTH, 128), 0) - PAD
    mk[...] = jnp.where(column + (start - HALO) < n * ROWS, column - lane_block(LENGTH), 1 << 20)

    def all_of(place, sem):
        pltpu.make_async_copy(place, place, sem).wait()

    all_of(arbuf.at[pl.ds(0, 128)], sems.at[1])
    for m in range(AHEAD + 2):
        for b, value in enumerate(spread(col_c if m == 1 else rbuf[m, 0:8])):
            row = 32 * (m - 1) + 8 * b + HALO + PAD
            if row >= 0 and row + 8 <= LENGTH:
                colr[row : row + 8] = value
    roww[0:8] = rbuf[0, 8:16]
    roww[8:16] = row_c
    roww[16:24] = rbuf[2, 8:16]
    def first_column(u):
        return pl.multiple_of(8 * lax.shift_right_logical(u, 1), 8)

    def mask_at(u, row, count):
        shift = 4 * u - jnp.where(start + 4 * u - HALO >= 0, 0, 1 << 20)
        return jnp.bitwise_and(mk[pl.ds(row, count), :] - shift, -BAND) == 0

    def clear_sides(buffer, index, base):
        buffer[index, pl.ds(base, 16), :] = jnp.zeros((16, 128), F32)
        buffer[index, pl.ds(base + PAD + SPAN, 24), :] = jnp.zeros((24, 128), F32)

    left = lane_block(WIDE) < 2

    def pieces(buffer, index, row):
        ends = jnp.where(left, buffer[index + 3, pl.ds(row, WIDE), :], buffer[index, pl.ds(row, WIDE), :])
        return ends, buffer[index + 1, pl.ds(row, WIDE), :], buffer[index + 2, pl.ds(row, WIDE), :]

    def make_field(with_slope, v):
        base = pl.multiple_of(8 * v, 8)
        for h in range(2):
            u = 2 * v + h
            clear_sides(act0, u + 1, base)
            row_here = roww[pl.ds(u + 5, 1), :]
            for ch in range(3):
                row = base + PAD + CHUNK * ch
                mask = mask_at(u, row, CHUNK)
                x = jnp.where(mask, row_here + colr[pl.ds(row, CHUNK), :], 0.0)
                act, slope = gelu(x, with_slope)
                act0[u + 1, pl.ds(row, CHUNK), :] = act
                if with_slope:
                    d0[u, pl.ds(row, CHUNK), :] = jnp.where(mask, slope, 0.0)

    def conv_operand(v):
        base = pl.multiple_of(8 * v, 8)
        for q in range(3):
            for d, piece in enumerate(pieces(act0, 2 * v, base + PAD + 2 * (q - 1))):
                lhs[:, 128 * (3 * q + d) : 128 * (3 * q + d + 1)] = piece.astype(BF16)

    def conv():
        res[0:WIDE] = dot(lhs[...], w1[...])

    def conv_result(with_slope, v):
        base = pl.multiple_of(8 * v, 8)
        for h in range(2):
            u = 2 * v + h
            clear_sides(act1, u, base)
            clear_sides(f1, u, base)
            row_here = roww[pl.ds(u + 5, 1), :]
            for ch in range(3):
                row = base + PAD + CHUNK * ch
                added = res[CHUNK * ch : CHUNK * ch + CHUNK, 128 * h : 128 * h + 128]
                mask = mask_at(u, row, CHUNK)
                x = jnp.where(mask, (row_here + colr[pl.ds(row, CHUNK), :]) + added, 0.0)
                act, slope = gelu(x, with_slope)
                act1[u, pl.ds(row, CHUNK), :] = act
                f1[u, pl.ds(row, CHUNK), :] = x
                if with_slope:
                    d1[u, pl.ds(row, CHUNK), :] = jnp.where(mask, slope, 0.0)

    make_field(False, 0)
    make_field(True, 1)
    conv_operand(0)
    wide = jnp.concatenate([tlow[...], target[...], thigh[...]], axis=0)
    wide = jnp.concatenate([wide, jnp.zeros((48, 128), F32)], axis=1)
    wide = jnp.concatenate([wide, jnp.zeros((80, 384), F32)], axis=0)
    sheared = pltpu.roll(wide, 0, 1, stride=1, stride_axis=0)
    ts[4 + PAD : 4 + PAD + 312] = sheared.T[0:312]
    make_field(True, 2)
    conv()

    def first_conv(with_field, v, carry):
        conv_operand(v)
        conv_result(True, v - 1)
        if with_field:
            make_field(True, v + 2)
        conv()
        return carry

    lax.fori_loop(1, 5, functools.partial(first_conv, True), 0)
    lax.fori_loop(5, 7, functools.partial(first_conv, False), 0)
    conv_result(False, 6)

    def make_misfit(w, carry):
        base = pl.multiple_of(8 * w, 8)
        for at, count in ((0, 48), (48, 48), (96, 48), (144, 48), (192, 48), (240, 32)):
            row = base + PAD + at
            values = [rol[0:1] * f1[2 * w + 1 + h, pl.ds(row, count), :] for h in range(2)]
            for g in range(4):
                for q in range(3):
                    act = act1[2 * w + g, pl.ds(row + 4 * (q - 1), count), :]
                    for h in range(2):
                        p = g - h
                        if 0 <= p < 3:
                            tap = 3 * p + q
                            values[h] = values[h] + w2[8 * tap : 8 * tap + 1] * act
            for h in range(2):
                high, low = split(values[h])
                qbuf[at : at + count, 128 * h : 128 * h + 128] = high
                qbuf[at : at + count, 256 + 128 * h : 384 + 128 * h] = low
            high, low = split(ts[pl.ds(row, count), :])
            qbuf[at : at + count, 512:640] = high
            qbuf[at : at + count, 640:768] = low
        pick = jnp.where(iota((128, 256), 0) == 8 * w + lax.shift_right_logical(iota((128, 256), 1), 5), -1.0, 0.0).astype(BF16)
        wq[512:640] = pick
        wq[640:768] = pick
        value = dot(qbuf[...], wq[...]) * (1.0 / BAND)
        for h in range(2):
            u = 2 * w + 1 + h
            clear_sides(mis, u, base)
            for at, count in ((0, 96), (96, 96), (192, 80)):
                row = base + PAD + at
                mis[u, pl.ds(row, count), :] = jnp.where(
                    mask_at(u, row, count), value[at : at + count, 128 * h : 128 * h + 128], 0.0
                )
        return carry

    lax.fori_loop(0, 6, make_misfit, 0)

    def make_cotangent(v, carry):
        base = pl.multiple_of(8 * v, 8)
        sums = [[None] * 10 for h in range(2)]
        for h in range(2):
            clear_sides(g1, 2 * v + h, base)
        for ch in range(SPAN // 24):
            row = base + PAD + 24 * ch
            acts = [act1[2 * v + h, pl.ds(row, 24), :] for h in range(2)]
            backs = [None, None]
            centers = [None, None]
            for g in range(4):
                for q in range(3):
                    m = mis[2 * v - 1 + g, pl.ds(row - 4 * (q - 1), 24), :]
                    for h in range(2):
                        p = h + 2 - g
                        if 0 <= p < 3:
                            tap = 3 * p + q
                            term = w2[8 * tap : 8 * tap + 1] * m
                            backs[h] = term if backs[h] is None else backs[h] + term
                            part_sum = fold(acts[h] * m)
                            sums[h][tap] = part_sum if sums[h][tap] is None else sums[h][tap] + part_sum
                            if tap == 4:
                                centers[h] = m
            for h in range(2):
                u = 2 * v + h
                part_sum = fold(centers[h] * f1[u, pl.ds(row, 24), :])
                sums[h][9] = part_sum if sums[h][9] is None else sums[h][9] + part_sum
                g1[u, pl.ds(row, 24), :] = rol[0:1] * centers[h] + d1[u, pl.ds(row, 24), :] * backs[h]
        for tap in range(10):
            for h in range(2):
                source = 2 * v + h - (tap // 3 - 1) if tap < 9 else 2 * v + h
                own = jnp.logical_and(source >= FIRST_OWN, source <= LAST_OWN)
                tacc[8 * tap : 8 * tap + 8] += jnp.where(own, sums[h][tap], 0.0)
        return carry

    lax.fori_loop(1, 6, make_cotangent, 0)

    def adjoint_operand(w):
        base = pl.multiple_of(8 * w + 8, 8)
        for q in range(3):
            for d, piece in enumerate(pieces(g1, 2 * w + 2, base + PAD - 2 * (q - 1))):
                high, low = split(piece)
                lanes = slice(128 * (3 * q + d), 128 * (3 * q + d + 1))
                lhs2[0:WIDE, lanes] = high
                lhs2[WIDE : 2 * WIDE, lanes] = low

    def adjoint():
        res[...] = dot(lhs2[...], wa[...])

    def adjoint_result(w):
        base = pl.multiple_of(8 * w + 8, 8)
        for h in range(2):
            u = 2 * w + 3 + h
            total_row = None
            for ch in range(3):
                at = CHUNK * ch + 8 * h
                row = base + PAD + at
                lanes = slice(128 * h, 128 * h + 128)
                back = res[at : at + CHUNK, lanes] + res[WIDE + at : WIDE + at + CHUNK, lanes]
                value = g1[u, pl.ds(row, CHUNK), :] + d0[u, pl.ds(row, CHUNK), :] * back
                colacc[pl.ds(row, CHUNK), :] += value
                part = fold(value)
                total_row = part if total_row is None else total_row + part
            rowg[pl.ds(u - 3, 1), :] = jnp.sum(total_row, axis=0, keepdims=True)

    def collect(w):
        for h in range(2):
            u = 2 * w + 3 + h
            base = pl.multiple_of(8 * w + 8 + 8 * h, 8)
            at = pl.multiple_of(WIDE * (2 * w + h), 16)
            high, low = split(g1[u, pl.ds(base + PAD, WIDE), :])
            gall[pl.ds(at, WIDE), 0:128] = high
            gall[pl.ds(at, WIDE), 128:256] = low
            for q in range(3):
                row = base + PAD + 2 * (q - 1)
                ends = jnp.where(left, act0[u + 2, pl.ds(row, WIDE), :], act0[u, pl.ds(row, WIDE), :])
                xall[pl.ds(at, WIDE), 256 * q : 256 * q + 128] = ends.astype(BF16)
                xall[pl.ds(at, WIDE), 256 * q + 128 : 256 * q + 256] = act0[u + 1, pl.ds(row, WIDE), :].astype(BF16)

    adjoint_operand(0)
    collect(0)
    adjoint()

    def first_adjoint(w, carry):
        adjoint_operand(w)
        adjoint_result(w - 1)
        collect(w)
        adjoint()
        return carry

    lax.fori_loop(1, 4, first_adjoint, 0)
    adjoint_result(3)

    where_block = lane_block(8)
    for m in range(REACH + 1):
        packed = jnp.zeros((8, 128), F32)
        for b in range(4):
            row = 32 * m + 8 * b + HALO + PAD
            value = colacc[row : row + 8]
            value = value + pltpu.roll(value, 64, 1)
            value = value + pltpu.roll(value, 32, 1)
            packed = jnp.where(where_block == b, value, packed)
        colp[8 * m : 8 * m + 8] = packed
    columns = []
    for m in range(1, REACH + 1):
        columns.append(
            pltpu.make_async_remote_copy(
                colp.at[pl.ds(8 * m, 8)], cbuf.at[m - 1], sems.at[2], sems.at[3], device_id=(dev(m),), device_id_type=MESH
            )
        )
    for copy in columns:
        copy.start()

    fg[...] = dot_t(gall[...], xall[...])

    where_block = lane_block(32)
    for group in range(3):
        packed = jnp.zeros((32, 128), F32)
        for place in range(4):
            tap = 4 * group + place
            if tap > 8:
                continue
            p, q = tap // 3 - 1, tap % 3
            value = jnp.zeros((32, 128), F32)
            for b in range(4):
                source = b + 2 * p
                lanes = 256 * q + (128 if 0 <= source < 4 else 0)
                both = fg[32 * b : 32 * b + 32, lanes : lanes + 128] + fg[128 + 32 * b : 160 + 32 * b, lanes : lanes + 128]
                value = value + jnp.where(where_block == source % 4, both, 0.0)
            value = value + pltpu.roll(value, 64, 1)
            value = value + pltpu.roll(value, 32, 1)
            packed = jnp.where(where_block == place, value, packed)
        arbuf[128 + 32 * group : 160 + 32 * group] = packed
    for tap in range(10):
        arbuf[224 + tap : 225 + tap] = jnp.sum(tacc[8 * tap : 8 * tap + 8], axis=0, keepdims=True)
    sums = arbuf[224:240]
    sums = sums + pltpu.roll(sums, 64, 1)
    arbuf[224:240] = sums + pltpu.roll(sums, 32, 1)
    high, low = split(jnp.concatenate([tacc[8 * tap : 8 * tap + 8] for tap in range(9)], axis=1))
    by_read = jnp.sum(dot(high, k2t[...]) + dot(low, k2t[...]), axis=0, keepdims=True)
    arbuf[233:234, 0:32] = arbuf[233:234, 0:32] + by_read

    def chunk(q):
        return pl.ds(pl.multiple_of(q * part, part), part)

    def send(source, place, at, device):
        pltpu.make_async_remote_copy(
            source, place, sems.at[at], sems.at[at + 1], device_id=(device,), device_id_type=MESH
        ).start()

    def scatter(begin, end):
        for q in range(begin, end):
            s = lax.rem(q - plane + side, side)

            @pl.when(s > 0)
            def _():
                send(arbuf.at[pl.ds(q * part, part)], rsbuf.at[s - 1], 4, across(s))

    scatter(side // 2, side)

    where_block = lane_block(8)
    rows = rowg[...]
    for b in range(4):
        vbuf[1, pl.ds(b, 8, stride=4), :] = jnp.where(where_block == 1, pltpu.roll(rows, (32 - 32 * b) % 128, 1) if b != 1 else rows, 0.0)
    all_of(arbuf.at[pl.ds(0, 128)], sems.at[0])
    all_of(cbuf, sems.at[3])
    all_of(cbuf, sems.at[2])
    own = colp[0:8]
    for m in range(1, REACH + 1):
        own = own + cbuf[m - 1]
    for b in range(4):
        vbuf[0, 8 * b : 8 * b + 8] = jnp.where(where_block == 0, pltpu.roll(own, (128 - 32 * b) % 128, 1) if b else own, 0.0)
    both = vbuf[0] + vbuf[1]
    high, low = split(both)
    by_feature = dot_t(jnp.concatenate([high, low], axis=0), jnp.concatenate([feat[...]] * 2, axis=0))
    arbuf[0:64] = by_feature[0:64, 0:128]
    arbuf[64:128] = by_feature[0:64, 128:256]

    scatter(0, side // 2)
    weights = jnp.concatenate([col_t[...], row_t[...]], axis=0)
    by_bin = dot(high[:, 0:64], weights) + dot(low[:, 0:64], weights)
    gbuf[256:288] = by_bin[:, 0:128]
    gbuf[288:320] = by_bin[:, 128:256]
    keep = pltpu.make_async_copy(gbuf.at[pl.ds(256, 72)], red.at[pl.ds(256, 72)], loads.at[7])
    keep.start()
    all_of(rsbuf, sems.at[5])
    total = arbuf[chunk(plane), :]
    for s in range(1, side):
        total = total + rsbuf[s - 1]
    mine[...] = total
    send(mine, other, 10, me + 1 - 2 * lax.rem(me, 2))
    all_of(other, sems.at[11])
    total = total + other[...]
    chip[...] = total
    bbuf[depth] = total
    for s in range(1, LINE):
        send(chip, bbuf.at[depth], 6, me + 2 * (lax.rem(depth + s, LINE) - depth))
    all_of(bbuf.at[pl.ds(0, LINE - 1)], sems.at[7])
    total = bbuf[0]
    for q in range(1, LINE):
        total = total + bbuf[q]
    gbuf[chunk(plane), :] = total
    for s in range(1, side):
        send(gbuf.at[chunk(plane)], red.at[chunk(plane)], 8, across(s))
    place = pltpu.make_async_copy(gbuf.at[chunk(plane)], red.at[chunk(plane)], loads.at[8])
    place.start()
    all_of(bbuf.at[pl.ds(0, LINE - 1)], sems.at[6])
    all_of(rsbuf, sems.at[9])
    all_of(rsbuf, sems.at[8])
    all_of(rsbuf, sems.at[4])
    all_of(other, sems.at[10])
    keep.wait()
    place.wait()


def finish_kernel(red, gfeat, grow, gcol, gone, gtwo, gread):
    gfeat[:, 0:128] = red[256:288]
    gfeat[:, 128:256] = red[288:320]
    gcol[:, 0:128] = red[0:32]
    gcol[:, 128:256] = red[64:96]
    grow[:, 0:128] = red[32:64]
    grow[:, 128:256] = red[96:128]
    for group in range(3):
        block = red[128 + 32 * group : 160 + 32 * group].T
        count = 128 if group < 2 else 32
        gone[128 * group : 128 * group + count] = block[0:count]
    by_channel = red[224:240].T
    read = red[320:321, 0:32]
    for tap in range(9):
        gtwo[32 * tap : 32 * tap + 32] = by_channel[0:32, tap : tap + 1] * read
    gread[...] = red[233:234, 0:32]


def shards(n, features, row_proj, col_proj, first_filter, second_filter, readout, target):
    side = n // SIDE
    part = TOTAL // side
    vmem = pl.BlockSpec(memory_space=pltpu.VMEM)

    def shape(*dims):
        return jax.ShapeDtypeStruct(dims, F32)

    def real(*dims):
        return pltpu.VMEM(dims, F32)

    def half(*dims):
        return pltpu.VMEM(dims, BF16)

    k1 = first_filter.reshape(9 * PAIR, PAIR)
    k2 = second_filter.reshape(9 * PAIR, PAIR)
    ro = readout.reshape(1, PAIR)
    row_t, col_t = row_proj.T, col_proj.T
    hbm = pl.BlockSpec(memory_space=pltpu.HBM)
    scratch = dict(
        feat=half(ROWS, 256), row_t=half(PAIR, 256), col_t=half(PAIR, 256), target=real(ROWS, 256), k1=half(288, PAIR), k2=half(288, PAIR), ro=half(1, PAIR),
        proj=real(32, 128), sbuf=real(16, 128), rbuf=real(AHEAD + 2, 16, 128), tlow=real(8, 256), thigh=real(8, 256),
        roww=real(24, 128), w1=half(1152, 256), wa=half(1152, 256), w2=real(72, 128), rol=real(8, 128),
        colr=real(LENGTH, 128), mk=pltpu.VMEM((LENGTH, 128), jnp.int32), ts=real(LENGTH, 128),
        act0=real(GROUPS + 2, LENGTH, 128), d0=real(GROUPS, LENGTH, 128),
        act1=real(GROUPS, LENGTH, 128), f1=real(GROUPS, LENGTH, 128), d1=real(GROUPS, LENGTH, 128),
        mis=real(GROUPS, LENGTH, 128), g1=real(GROUPS, LENGTH, 128),
        lhs=half(WIDE, 1152), lhs2=half(2 * WIDE, 1152), k2t=half(1152, PAIR), res=real(2 * WIDE, 256), qbuf=half(WIDE, 768), wq=half(768, 256),
        xall=half(8 * WIDE, 768), gall=half(8 * WIDE, 256), fg=real(256, 768), tacc=real(80, 128),
        colacc=real(LENGTH, 128), tiles=real(288, 256), colp=real(72, 128), rowg=real(8, 128),
        cbuf=real(REACH, 8, 128), vbuf=real(2, 32, 128), arbuf=real(256, 128), rsbuf=real(side - 1, part, 128),
        bbuf=real(LINE, part, 128), mine=real(part, 128), other=real(part, 128), chip=real(part, 128), gbuf=real(328, 128), loads=SEM((9,)), sems=SEM((12,)),
    )
    red = pl.pallas_call(
        functools.partial(step_kernel, n),
        out_shape=shape(328, 128),
        in_specs=[hbm] * 7,
        out_specs=hbm,
        scratch_shapes=list(scratch.values()),
        compiler_params=pltpu.CompilerParams(
            collective_id=0, has_side_effects=True, vmem_limit_bytes=60 * 1024 * 1024
        ),
        name="step",
    )(features, row_t, col_t, target, k1, k2, ro)

    gfeat, grow, gcol, gone, gtwo, gread = pl.pallas_call(
        finish_kernel,
        out_shape=(shape(ROWS, 256), shape(32, 256), shape(32, 256), shape(288, 32), shape(288, 32), shape(1, 32)),
        in_specs=[vmem],
        out_specs=(vmem,) * 6,
        compiler_params=pltpu.CompilerParams(vmem_limit_bytes=4 * 1024 * 1024),
        name="finish",
    )(red)
    return gfeat, grow.T, gcol.T, gone.reshape(3, 3, PAIR, PAIR), gtwo.reshape(3, 3, PAIR, PAIR), gread.reshape(PAIR)


def solution(mesh):
    n = mesh.shape["diag"]
    in_specs = (P("diag", None), P(), P(), P(), P(), P(), P("diag", None))
    out_specs = (P("diag", None), P(), P(), P(), P(), P())
    return jax.shard_map(
        functools.partial(shards, n), mesh=mesh, in_specs=in_specs, out_specs=out_specs, check_vma=False
    )
```
